32 devices in a mesh: rep: 4 (over y, x), seq: 8 (over z, core).
Axes of the slice: x: 2, y: 2, z: 4, core: 2. Of those that a mesh axis runs over, the one named last changes fastest.
Arguments:
- tokens: bfloat16 [8, 2048, 2048], P('rep', 'seq'), may hold values from -6 to 6
- lengths: int32 [8], P('rep'), may hold values from 512 to 2048, as said below
- pre_gain: float32 [2048], replicated, may hold values from 0.5 to 1.5
- in_weight: bfloat16 [2048, 8512], P('seq'), may hold values from -0.125 to 0.125
- conv_weight: float32 [4, 4352], replicated, may hold values from -3 to 3
- conv_bias: float32 [4352], replicated, may hold values from -3 to 3
- step_bias: float32 [64], replicated, may hold values from -2 to 1
- decay_log: float32 [64], replicated, may hold values from -13 to -3
- skip_gain: float32 [64], replicated, may hold values from 0.5 to 1.5
- norm_gain: float32 [4096], replicated, may hold values from 0.5 to 1.5
- out_weight: bfloat16 [4096, 2048], P('seq'), may hold values from -0.09375 to 0.09375
- cotangent: bfloat16 [8, 2048, 2048], P('rep', 'seq'), may hold values from -6 to 6
Outputs:
- output: bfloat16 [8, 2048, 2048], P('rep', 'seq')
- tokens_grad: float32 [8, 2048, 2048], P('rep', 'seq')
- pre_gain_grad: float32 [2048], replicated
- in_weight_grad: float32 [2048, 8512], P('seq')
- conv_weight_grad: float32 [4, 4352], replicated
- conv_bias_grad: float32 [4352], replicated
- step_bias_grad: float32 [64], replicated
- decay_log_grad: float32 [64], replicated
- skip_gain_grad: float32 [64], replicated
- norm_gain_grad: float32 [4096], replicated
- out_weight_grad: float32 [4096, 2048], P('seq')
The draws below stay inside these ranges and needn't reach their ends.
Inputs may be any that keep to these rules, and one draw needn't show every extreme that they name: `lengths`: each replica group's 2 slots hold one of length 2048; one slot of all has length 512; the others lie evenly between.
All inputs are finite; a program needn't handle non-finite values.
Results may differ from the reference program's by a relative error of at most 0.0091.
Values may be sent and summed in bfloat16 or wider, within the bound.
No kernel may reach another device: no remote copies, remote signals or barrier semaphores. Data moves between devices by JAX's collectives and lax.ppermute only.
A program may use at most 576 MiB of HBM per device.

```python
import jax
import jax.numpy as jnp
from jax import lax

MODEL_DIMENSION = 2048
HEADS = 64
HEAD_DIM = 64
STATE = 128
KCONV = 4
BLOCK = 256
MICRO_BATCHES = 2
INNER = 4096
CONV_CH = 4352
NPROJ = 8512
SLOT_POSITIONS = 2048
SLOT_TOTAL = 8


def draw_lengths(key, part):
    key = jax.random.fold_in(key, 7)
    key_base, key_full, key_short = jax.random.split(key, 3)
    replica_groups = SLOT_TOTAL // MICRO_BATCHES
    drawn = jax.random.randint(key_base, (replica_groups, MICRO_BATCHES), SLOT_POSITIONS // 4, SLOT_POSITIONS + 1)
    full_pick = jax.random.randint(key_full, (replica_groups,), 0, MICRO_BATCHES)
    columns = jnp.arange(MICRO_BATCHES, dtype=jnp.int32)[None, :]
    drawn = jnp.where(columns == full_pick[:, None], SLOT_POSITIONS, drawn)
    short_replica = jax.random.randint(key_short, (), 0, replica_groups)
    short_column = (full_pick + 1) % MICRO_BATCHES
    replica_ids = jnp.arange(replica_groups, dtype=jnp.int32)[:, None]
    drawn = jnp.where((replica_ids == short_replica) & (columns == short_column[:, None]), SLOT_POSITIONS // 4, drawn)
    return drawn.reshape(-1).astype(jnp.int32)


def levels(key, dims, shards, low, largest):
    def one(position, shards_of):
        steps = jax.random.uniform(jax.random.fold_in(jax.random.fold_in(key, 6), position), (shards_of,), jnp.float32, low / len(shards), largest / len(shards))
        return jnp.repeat(jnp.exp(steps), dims[position] // shards_of).reshape((-1,) + (1,) * (len(dims) - position - 1))

    level = one(*shards[0])
    for cut in shards[1:]:
        level = level * one(*cut)
    return level


def gaussian(key, extent, deviation, reach, shards=(), kind=jnp.bfloat16):
    loudness = levels(key, extent, shards, -0.22, 0.18) if shards else 1.0
    entries = jax.random.normal(key, extent, jnp.float32) * deviation * loudness
    return jnp.minimum(jnp.maximum(entries, -reach), reach).astype(kind)


def setup_inputs(seed: int = 0) -> dict:
    key_of = jax.random.split(jax.random.key(seed), 13)
    return {
        "tokens": gaussian(key_of[0], (SLOT_TOTAL, SLOT_POSITIONS, MODEL_DIMENSION), 1.0, 6.0, ((0, 4), (1, 8))),
        "lengths": draw_lengths(jax.random.fold_in(key_of[12], 71), 0),
        "pre_gain": jnp.clip(1.0 + 0.1 * jax.random.normal(key_of[2], (MODEL_DIMENSION,), jnp.float32), 0.5, 1.5),
        "in_weight": gaussian(key_of[3], (MODEL_DIMENSION, NPROJ), MODEL_DIMENSION ** -0.5, 0.125, ((0, 8),)),
        "conv_weight": gaussian(key_of[4], (KCONV, CONV_CH), KCONV ** -0.5, 3.0, (), jnp.float32),
        "conv_bias": gaussian(key_of[5], (CONV_CH,), 0.5, 3.0, (), jnp.float32),
        "step_bias": jnp.clip(jax.random.uniform(key_of[6], (HEADS,), jnp.float32, -2.0, 1.0), -2.0, 1.0),
        "decay_log": jnp.clip(jax.random.uniform(key_of[7], (HEADS,), jnp.float32, -13.0, -3.0), -13.0, -3.0),
        "skip_gain": jnp.clip(jax.random.uniform(key_of[8], (HEADS,), jnp.float32, 0.5, 1.5), 0.5, 1.5),
        "norm_gain": jnp.clip(1.0 + 0.1 * jax.random.normal(key_of[9], (INNER,), jnp.float32), 0.5, 1.5),
        "out_weight": gaussian(key_of[10], (INNER, MODEL_DIMENSION), INNER ** -0.5, 0.09375, ((0, 8),)),
        "cotangent": gaussian(key_of[11], (SLOT_TOTAL, SLOT_POSITIONS, MODEL_DIMENSION), 1.0, 6.0, ((0, 4), (1, 8))),
    }


@jax.custom_vjp
def low(v):
    return lax.optimization_barrier(v.astype(jnp.bfloat16)).astype(jnp.float32)

@jax.custom_vjp
def low_back(v):
    return v

def low_keep(v):
    return (low(v), None)

def low_pass(kept, grad):
    return (grad,)

def back_keep(v):
    return (v, None)

def back_low(kept, grad):
    return (low(grad),)
low.defvjp(low_keep, low_pass)
low_back.defvjp(back_keep, back_low)
EPSILON = 1e-05
HIGHEST_PRECISION = lax.Precision.HIGHEST

def rms_scale(values, gain):
    return values * lax.rsqrt(lax.optimization_barrier(jnp.mean(values * values, axis=-1, keepdims=True)) + EPSILON) * gain

def silu_apply(values):
    return values * jax.nn.sigmoid(values)

def state_terms(head_inputs, b_rows, step_size, decay_rate):
    log_decay = jnp.cumsum(-step_size * decay_rate, axis=1)
    last_log = log_decay[:, -1, :]
    to_end = jnp.exp(last_log[:, None, :] - log_decay) * step_size
    local_state = jnp.einsum('msh,mshp,msn->mhpn', to_end, head_inputs, b_rows, precision=HIGHEST_PRECISION)
    return (jnp.exp(last_log), local_state)

def out_terms(head_inputs, b_rows, c_rows, step_size, decay_rate, skip_gain, carried):
    log_decay = jnp.cumsum(-step_size * decay_rate, axis=1)
    length = head_inputs.shape[1]
    causal = jnp.arange(length, dtype=jnp.int32)[:, None] >= jnp.arange(length, dtype=jnp.int32)[None, :]
    by_head = jnp.swapaxes(log_decay, 1, 2)
    log_gap = jnp.where(causal, by_head[:, :, :, None] - by_head[:, :, None, :], 0.0)
    decay_map = jnp.where(causal, jnp.exp(log_gap), 0.0)
    scores = jnp.einsum('mtn,msn->mts', c_rows, b_rows, precision=HIGHEST_PRECISION)
    weights = scores[:, None] * decay_map * jnp.swapaxes(step_size, 1, 2)[:, :, None, :]
    inside_group = jnp.einsum('mhts,mshp->mthp', weights, head_inputs, precision=HIGHEST_PRECISION)
    carry_in = jnp.einsum('mtn,mhpn->mthp', c_rows, carried, precision=HIGHEST_PRECISION) * jnp.exp(log_decay)[..., None]
    return inside_group + carry_in + skip_gain[:, None] * head_inputs

def front_mixer(extended, step_raw, conv_weight, conv_bias, step_bias, decay_log):
    length = step_raw.shape[1]
    conv_sum = conv_bias + conv_weight[0] * extended[:, 0:length]
    for offset in range(1, KCONV):
        conv_sum = conv_sum + conv_weight[offset] * extended[:, offset:offset + length]
    activated = silu_apply(conv_sum)
    inner_w = activated.shape[-1] - 2 * STATE
    head_inputs = activated[..., :inner_w].reshape(activated.shape[0], length, HEADS, HEAD_DIM)
    b_rows = activated[..., inner_w:inner_w + STATE]
    c_rows = activated[..., inner_w + STATE:]
    step_size = jax.nn.softplus(step_raw + step_bias)
    return (head_inputs, b_rows, c_rows, step_size, jnp.exp(decay_log))

def forward_layer_pass(token_rows, pre_gain, in_weight, conv_weight, conv_bias, step_bias, decay_log, skip_gain, norm_gain, out_weight, valid_mask):
    slot_count, length, model_width = token_rows.shape
    inner_w = norm_gain.shape[0]
    channels = conv_bias.shape[0]
    normed = low(rms_scale(token_rows, pre_gain))
    projected = low_back(low(jnp.einsum('msd,de->mse', normed, in_weight, precision=HIGHEST_PRECISION)))
    gate_raw = projected[..., :inner_w]
    mixed = projected[..., inner_w:inner_w + channels]
    step_raw = projected[..., inner_w + channels:]
    extended = jnp.pad(mixed, ((0, 0), (KCONV - 1, 0), (0, 0)))
    head_inputs, b_rows, c_rows, step_size, decay_rate = front_mixer(extended, step_raw, conv_weight, conv_bias, step_bias, decay_log)
    blocks = length // BLOCK

    def to_blocks(values):
        return jnp.swapaxes(values.reshape((slot_count, blocks, BLOCK) + values.shape[2:]), 0, 1)

    def block_step(carried, pieces):
        inputs_b, b_piece, c_piece, step_piece = pieces
        mixed_out = out_terms(inputs_b, b_piece, c_piece, step_piece, decay_rate, skip_gain, carried)
        fade_all, local_state = state_terms(inputs_b, b_piece, step_piece, decay_rate)
        return (fade_all[:, :, None, None] * carried + local_state, mixed_out)
    empty_initial_state = jnp.zeros((slot_count, HEADS, HEAD_DIM, STATE), jnp.float32)
    last_state, block_outs = lax.scan(jax.checkpoint(block_step), empty_initial_state, (to_blocks(head_inputs), to_blocks(b_rows), to_blocks(c_rows), to_blocks(step_size)))
    mixer_out = jnp.swapaxes(block_outs, 0, 1).reshape(slot_count, length, inner_w)
    gated_out = low(rms_scale(mixer_out * silu_apply(gate_raw), norm_gain))
    branch = jnp.einsum('msi,id->msd', gated_out, out_weight, precision=HIGHEST_PRECISION)
    return valid_mask[..., None] * (token_rows + branch)

def reference(tokens, lengths, pre_gain, in_weight, conv_weight, conv_bias, step_bias, decay_log, skip_gain, norm_gain, out_weight, cotangent):
    length = tokens.shape[1]
    valid_mask = (jnp.arange(length, dtype=jnp.int32)[None, :] < lengths[:, None]).astype(jnp.float32)
    float_args = (tokens.astype(jnp.float32), pre_gain, in_weight.astype(jnp.float32), conv_weight, conv_bias, step_bias, decay_log, skip_gain, norm_gain, out_weight.astype(jnp.float32))

    def closed(*values):
        return forward_layer_pass(*values, valid_mask)
    result, pullback = jax.vjp(closed, *float_args)
    gradients = pullback(cotangent.astype(jnp.float32))
    return (result.astype(jnp.bfloat16), gradients[0], gradients[1], gradients[2], gradients[3], gradients[4], gradients[5], gradients[6], gradients[7], gradients[8], gradients[9])
```

```python
import functools

import jax
import jax.numpy as jnp
from jax import lax
from jax.experimental import pallas as pl
from jax.experimental.pallas import tpu as pltpu
from jax.sharding import PartitionSpec as P

HEADS = 64
HEAD_DIM = 64
STATE = 128
KCONV = 4
LANES = 128
PAD = 8
COST = 1.0
LOW = 1.0
MARK = 16
EPSILON = 1e-05
NEVER = -1e30
BF16 = jnp.bfloat16
F32 = jnp.float32


def swap(value, axis, bit):
    return lax.ppermute(value, axis, [(i, i ^ bit) for i in range(lax.axis_size(axis))])


def after(value, *others):
    return lax.optimization_barrier((value,) + others)[0]


def gather_near(own):
    return own, swap(own, "rep", 1), swap(own, "rep", 2)


def to_far(near):
    own, one, two = near
    half = own.shape[0] // 2
    return one[:half], two[half:]


def far_parts(near, sent):
    return list(near) + [swap(sent[0], "rep", 2), swap(sent[1], "rep", 1)]


def gather_direct(own):
    return [own] + [swap(own, "rep", j) for j in (1, 2, 3)]


def scatter_direct(parts):
    total = parts[0].astype(F32)
    for j in (1, 2, 3):
        total = total + swap(parts[j], "rep", j).astype(F32)
    return total


def in_order(blocks):
    stack = jnp.stack(blocks)
    place = lax.axis_index("rep")
    return [lax.dynamic_index_in_dim(stack, place ^ q, 0, False) for q in range(len(blocks))]


def sum_seq(value):
    bit = 1
    while bit < lax.axis_size("seq"):
        value = value + swap(value, "seq", bit)
        bit *= 2
    return value


class SmallSums:
    def __init__(self, value):
        self.value, self.bit = value, 1

    def hop(self):
        if self.bit < lax.axis_size("seq"):
            sent = self.value
            self.value = sent + swap(sent, "seq", self.bit)
            self.bit *= 2
        return sent

    def rest(self):
        while self.bit < lax.axis_size("seq"):
            self.hop()
        return self.value


def sum_aligned(blocks):
    total = blocks
    for bit in (1, 2, 3):
        other = swap(blocks, "rep", bit)
        total = total + jnp.stack([other[j ^ bit] for j in range(blocks.shape[0])])
    return total


class Chain:
    def __init__(self, fade, part, message, reverse):
        count = lax.axis_size("seq")
        self.chips = count // 2
        first, lead = (1, 0) if reverse else (0, 1)
        hop = -1 if reverse else 1
        chips = range(self.chips)
        self.fade, self.part = fade, part
        self.homeward = [(2 * c + lead, 2 * c + first) for c in chips]
        onward = [(2 * c + lead, 2 * (c + hop) + lead) for c in chips if 0 <= c + hop < self.chips]
        self.onward = onward[::hop]
        self.leads = lax.axis_index("seq") % 2 == lead
        self.got = lax.ppermute(message, "seq", [(2 * c + first, 2 * c + lead) for c in chips])
        self.total = None
        self.enters = 0.0

    def hop(self):
        if self.total is None:
            got = self.got
            self.mate = got[:, :STATE].astype(F32)
            self.mate_fade = got[:, STATE : STATE + 1].astype(F32) + got[:, STATE + 1 : STATE + 2].astype(F32)
            self.total = self.part + self.fade * self.mate
            self.total_fade = self.fade * self.mate_fade
            onto = self.total.astype(BF16)
        else:
            onto = (self.total + self.total_fade * self.enters.astype(F32)).astype(BF16)
        self.enters = self.enters + lax.ppermute(onto, "seq", [self.onward.pop(0)])
        return onto

    def rest(self):
        while self.onward:
            self.hop()

    def back(self):
        self.handed = lax.ppermute(self.enters, "seq", self.homeward)
        return self.enters

    def end(self):
        own = (self.mate + self.mate_fade * self.enters.astype(F32)).astype(BF16)
        return jnp.where(self.leads, own, self.handed)


def nt(a, b):
    return lax.dot_general(a, b, (((1,), (1,)), ((), ())), preferred_element_type=F32)


def tn(a, b):
    return lax.dot_general(a, b, (((0,), (0,)), ((), ())), preferred_element_type=F32)


def nn(a, b):
    return jnp.dot(a, b, preferred_element_type=F32)


def col(p):
    return slice(p * LANES, (p + 1) * LANES)


def two_parts(value):
    heads = LANES // 4
    high = value.astype(BF16)
    low = (value - high.astype(F32)).astype(BF16).astype(F32)
    lane = lax.broadcasted_iota(jnp.int32, value.shape, 1)
    both = jnp.where(
        lane < heads, high.astype(F32), jnp.where(lane < 2 * heads, pltpu.roll(low, heads, 1), 0.0)
    )
    return both.astype(BF16)


def running(value, reverse):
    rows = value.shape[0]
    place = lax.broadcasted_iota(jnp.int32, value.shape, 0)
    shift = 1
    while shift < rows:
        if reverse:
            moved = jnp.where(place < rows - shift, pltpu.roll(value, rows - shift, 0), 0.0)
        else:
            moved = jnp.where(place >= shift, pltpu.roll(value, shift, 0), 0.0)
        value = value + moved
        shift *= 2
    return value


def head_sums(product, fold):
    high = product.astype(BF16)
    low = (product - high.astype(F32)).astype(BF16)
    return nn(high, fold) + nn(low, fold)


def softplus(v):
    return jnp.maximum(v, 0.0) + jnp.log1p(jnp.exp(-jnp.abs(v)))


def sigmoid(v):
    return 1.0 / (1.0 + jnp.exp(-v))


def split(value):
    high = value.astype(BF16)
    return high, (value - high.astype(F32)).astype(BF16)


def nt_fine(a, b):
    half = a.shape[1] // 2
    return nt(
        jnp.concatenate([a, a[:, :half]], axis=1),
        jnp.concatenate([b[:, :half], b[:, :half], b[:, half:]], axis=1),
    )


def nn_fine(a_high, a_low, b):
    half = b.shape[1] // 2
    return nn(
        jnp.concatenate([a_high, a_low, a_high], axis=1),
        jnp.concatenate([b[:, :half], b[:, :half], b[:, half:]], axis=0),
    )


def twice(value):
    return jnp.concatenate([value, value], axis=0)


def tn_sum(a, b):
    both = tn(a, b)
    half = both.shape[0] // 2
    return both[:half] + both[half:]


def message_of(out, p, part, fade):
    out[0, 0:STATE, col(p)] = part.astype(BF16)
    high, low = split(fade)
    place = lax.broadcasted_iota(jnp.int32, (MARK, LANES), 0)
    rows = jnp.where(place == 0, high.astype(F32), jnp.where(place == 1, low.astype(F32), 0.0))
    out[0, STATE : STATE + MARK, col(p)] = rows.astype(BF16)


def front_kernel(
    proj, halo, cw, cb, sb, dl, spread, x_out, bc_out, sl_out, st_out, msg_out, fade_out, ext
):
    rows = proj.shape[0]
    pairs = x_out.shape[1] // LANES
    raw_step = proj[:, (pairs + 2) * LANES :].astype(F32) + sb[...]
    step = softplus(raw_step)
    log_decay = running(-step * jnp.exp(dl[...]), False)
    last = log_decay[rows - 1 : rows, :]
    sl_out[:, :LANES] = step
    sl_out[:, LANES:] = log_decay
    weight = two_parts(jnp.exp(last - log_decay) * step)
    ending = two_parts(jnp.broadcast_to(jnp.exp(last), (PAD, LANES)))
    ext_rows = pl.ds(PAD, rows)

    def activated(p):
        ext[0:PAD, :] = halo[0, :, col(p)]
        ext[ext_rows, :] = proj[:, col(p)].astype(F32)
        z = cb[:, col(p)] + cw[0:1, col(p)] * ext[pl.ds(PAD - 3, rows), :]
        for k in range(1, KCONV):
            z = z + cw[k : k + 1, col(p)] * ext[pl.ds(PAD - 3 + k, rows), :]
        return z * sigmoid(z)

    b_rows = jnp.concatenate(split(activated(pairs)), axis=1)
    bc_out[:, : 2 * STATE] = b_rows
    bc_out[:, 2 * STATE :] = jnp.concatenate(split(activated(pairs + 1)), axis=1)
    for p in range(pairs):
        x = activated(p)
        x_out[:, col(p)] = x
        scaled = (x * nn(weight, spread[:, col(p)])).astype(BF16)
        part = tn_sum(b_rows, scaled)
        fade = nn(ending, spread[:, col(p)])[0:1, :]
        st_out[0, :, col(p)] = part
        fade_out[0, :, col(p)] = fade
        message_of(msg_out, p, part, fade)


def inside_kernel(x, bc, sl, spread, y_out):
    rows = x.shape[0]
    pairs = x.shape[1] // LANES
    scores = nt_fine(bc[:, 2 * STATE :], bc[:, : 2 * STATE])
    log_decay = sl[:, LANES:]
    across = log_decay.T
    step = two_parts(sl[:, :LANES])
    t = lax.broadcasted_iota(jnp.int32, (rows, rows), 0)
    s = lax.broadcasted_iota(jnp.int32, (rows, rows), 1)
    causal = t >= s
    low_lanes = lax.broadcasted_iota(jnp.int32, (rows, LANES), 1) < HEAD_DIM
    for p in range(pairs):
        scaled = (x[:, col(p)] * nn(step, spread[:, col(p)])).astype(BF16)
        outs = []
        for h in (2 * p, 2 * p + 1):
            gap = log_decay[:, h : h + 1] - across[h : h + 1, :]
            weights = (scores * jnp.exp(jnp.where(causal, gap, NEVER))).astype(BF16)
            outs.append(nn(weights, scaled))
        y_out[:, col(p)] = jnp.where(low_lanes, outs[0], outs[1])


def gate_kernel(y, x, bc, sl, start, gate, grad, gain, skip, spread, y_out, sums_out):
    rows = x.shape[0]
    pairs = x.shape[1] // LANES
    c_rows = bc[:, 2 * STATE :]
    decay = two_parts(jnp.exp(sl[:, LANES:]))
    squares = jnp.zeros((rows, LANES), F32)
    cross = jnp.zeros((rows, LANES), F32)
    for p in range(pairs):
        plain = y[:, col(p)] + nn(decay, spread[:, col(p)]) * nn(c_rows, twice(start[0, :, col(p)]))
        y_out[:, col(p)] = plain
        g = gate[:, col(p)].astype(F32)
        v = (plain + skip[:, col(p)] * x[:, col(p)]) * (g * sigmoid(g))
        squares = squares + v * v
        cross = cross + grad[:, col(p)].astype(F32) * gain[:, col(p)] * v
    lane = lax.broadcasted_iota(jnp.int32, (rows, LANES), 1)
    both = jnp.where(
        lane == 0,
        jnp.sum(squares, axis=1, keepdims=True),
        jnp.where(lane == 1, jnp.sum(cross, axis=1, keepdims=True), 0.0),
    )
    sums_out[0] = both.T[0:PAD, :]


def norm_kernel(
    inner, y, x, bc, sl, gate, grad, gain, skip, fade, sums, spread,
    gated_out, dy_out, dgate_out, dstart_out, msg_out, gain_out, skip_out,
):
    rows = x.shape[0]
    pairs = x.shape[1] // LANES

    @pl.when(pl.program_id(0) == 0)
    def _():
        gain_out[...] = jnp.zeros_like(gain_out)
        skip_out[...] = jnp.zeros_like(skip_out)

    c_rows = bc[:, 2 * STATE :]
    decay = two_parts(jnp.exp(sl[:, LANES:]))
    padded = jnp.concatenate([sums[0], jnp.zeros((LANES - PAD, rows), F32)], axis=0).T
    scale = lax.rsqrt(padded[:, 0:1] / inner + EPSILON)
    back = scale * scale * (padded[:, 1:2] / inner)
    for p in range(pairs):
        g = gate[:, col(p)].astype(F32)
        sg = sigmoid(g)
        silu = g * sg
        xp = x[:, col(p)]
        yp = y[:, col(p)] + skip[:, col(p)] * xp
        v = yp * silu
        gp = grad[:, col(p)].astype(F32)
        normal = v * scale
        gated_out[:, col(p)] = (normal * gain[:, col(p)]).astype(BF16)
        gain_out[0:1, col(p)] += jnp.sum(gp * normal, axis=0, keepdims=True)
        dv = scale * (gp * gain[:, col(p)] - v * back)
        dy = (dv * silu).astype(BF16)
        dy_out[:, col(p)] = dy
        dyf = dy.astype(F32)
        dgate_out[:, col(p)] = (dv * yp * (sg * (1.0 + g * (1.0 - sg)))).astype(BF16)
        skip_out[0:1, col(p)] += jnp.sum(dyf * xp, axis=0, keepdims=True)
        faded = (dyf * nn(decay, spread[:, col(p)])).astype(BF16)
        dstart = tn_sum(c_rows, faded)
        dstart_out[0, :, col(p)] = dstart
        message_of(msg_out, p, dstart, fade[0, :, col(p)])


def inside_back_kernel(x, bc, sl, dy, start, spread, dxs_out, dbc_out):
    rows = x.shape[0]
    pairs = x.shape[1] // LANES
    b_rows = bc[:, : 2 * STATE]
    c_rows = bc[:, 2 * STATE :]
    scores = nt_fine(b_rows, c_rows)
    log_decay = sl[:, LANES:]
    across = log_decay.T
    step = two_parts(sl[:, :LANES])
    decay = two_parts(jnp.exp(log_decay))
    s = lax.broadcasted_iota(jnp.int32, (rows, rows), 0)
    t = lax.broadcasted_iota(jnp.int32, (rows, rows), 1)
    causal = t >= s
    low_lanes = lax.broadcasted_iota(jnp.int32, (rows, LANES), 1) < HEAD_DIM
    score_grad = jnp.zeros((rows, rows), F32)
    dc = jnp.zeros((rows, LANES), F32)
    for p in range(pairs):
        scaled = x[:, col(p)] * nn(step, spread[:, col(p)])
        dyp = dy[:, col(p)]
        faded = (dyp.astype(F32) * nn(decay, spread[:, col(p)])).astype(BF16)
        dc = dc + nt(faded, start[0, :, col(p)])
        outs = []
        for h in (2 * p, 2 * p + 1):
            gap = across[h : h + 1, :] - log_decay[:, h : h + 1]
            fall = jnp.exp(jnp.where(causal, gap, NEVER))
            weights = (scores * fall).astype(BF16)
            outs.append(nn(weights, dyp))
            mine = low_lanes if h % 2 == 0 else jnp.logical_not(low_lanes)
            score_grad = score_grad + fall * nt(jnp.where(mine, scaled, 0.0).astype(BF16), dyp)
        dxs_out[:, col(p)] = jnp.where(low_lanes, outs[0], outs[1])
    dbc_out[:, col(0)] = nn_fine(*split(score_grad), c_rows)
    dbc_out[:, col(1)] = dc + nn_fine(*split(score_grad.T), b_rows)


def back_kernel(
    proj, halo, cw, cb, sb, dl, skip, spread, fold, x, bc, sl, y, dy, dxs, dbc, start, part, fade, later,
    pg_out, halo_out, tail_out, cw_out, cb_out, sb_out, dl_out, ext, dext,
):
    rows = x.shape[0]
    pairs = x.shape[1] // LANES

    @pl.when(pl.program_id(0) == 0)
    def _():
        for out in (cw_out, cb_out, sb_out, dl_out):
            out[...] = jnp.zeros_like(out)

    rate = jnp.exp(dl[...])
    step_f = sl[:, :LANES]
    log_decay = sl[:, LANES:]
    last = log_decay[rows - 1 : rows, :]
    step = two_parts(step_f)
    to_end = two_parts(jnp.exp(last - log_decay))
    b_rows = bc[:, : 2 * STATE]
    dext[0:PAD, :] = jnp.zeros((PAD, LANES), F32)
    dext[pl.ds(PAD + rows, PAD), :] = jnp.zeros((PAD, LANES), F32)

    def through_conv(p, grad):
        ext[0:PAD, :] = halo[0, :, col(p)]
        ext[pl.ds(PAD, rows), :] = proj[:, col(p)].astype(F32)
        taps = [ext[pl.ds(PAD - 3 + k, rows), :] for k in range(KCONV)]
        z = cb[:, col(p)] + cw[0:1, col(p)] * taps[0]
        for k in range(1, KCONV):
            z = z + cw[k : k + 1, col(p)] * taps[k]
        sg = sigmoid(z)
        dz = grad * (sg * (1.0 + z * (1.0 - sg)))
        cb_out[0:1, col(p)] += jnp.sum(dz, axis=0, keepdims=True)
        for k in range(KCONV):
            cw_out[k : k + 1, col(p)] += jnp.sum(dz * taps[k], axis=0, keepdims=True)
        dext[pl.ds(PAD, rows), :] = dz
        whole = rows + PAD
        dm = cw[KCONV - 1 : KCONV, col(p)] * dext[pl.ds(0, whole), :]
        for k in range(KCONV - 1):
            dm = dm + cw[k : k + 1, col(p)] * dext[pl.ds(KCONV - 1 - k, whole), :]
        halo_out[0, :, col(p)] = dm[0:PAD, :]
        pg_out[:, col(p)] = dm[PAD:, :].astype(BF16)
        tail_out[0, :, col(p)] = dm[rows:, :]

    db = dbc[:, col(0)]
    dstep = jnp.zeros((rows, LANES), F32)
    dlog = jnp.zeros((rows, LANES), F32)
    dlast = jnp.zeros((PAD, LANES), F32)
    for p in range(pairs):
        xp = x[:, col(p)]
        step_p = nn(step, spread[:, col(p)])
        end_p = nn(to_end, spread[:, col(p)])
        later_p = later[0, :, col(p)]
        dyf = dy[:, col(p)].astype(F32)
        scaled = xp * step_p
        dxs_p = dxs[:, col(p)] + end_p * nn(b_rows, twice(later_p))
        db = db + nt((end_p * scaled).astype(BF16), later_p)
        dstep = dstep + head_sums(xp * dxs_p, fold[col(p), :])
        dlog = dlog + head_sums(dyf * y[:, col(p)] - scaled * dxs_p, fold[col(p), :])
        end_state = fade[0, :, col(p)] * start[0, :, col(p)].astype(F32) + part[0, :, col(p)]
        ends = jnp.sum(later_p.astype(F32) * end_state, axis=0, keepdims=True)
        dlast = dlast + head_sums(jnp.broadcast_to(ends, (PAD, LANES)), fold[col(p), :])
        through_conv(p, step_p * dxs_p + skip[:, col(p)] * dyf)
    through_conv(pairs, db)
    through_conv(pairs + 1, dbc[:, col(1)])
    place = lax.broadcasted_iota(jnp.int32, (rows, LANES), 0)
    dlog = dlog + jnp.where(place == rows - 1, dlast[0:1, :], 0.0)
    da = running(dlog, True)
    dstep = dstep - rate * da
    raw_step = proj[:, (pairs + 2) * LANES :].astype(F32) + sb[...]
    draw = dstep * sigmoid(raw_step)
    pg_out[:, (pairs + 2) * LANES :] = draw.astype(BF16)
    sb_out[0:1, :] += jnp.sum(draw, axis=0, keepdims=True)
    dl_out[0:1, :] += -rate * jnp.sum(step_f * da, axis=0, keepdims=True)


def rows_kernel(product, left, right, out):
    out[...] = product(left[...], right[...]).astype(BF16)


def gathered_kernel(product, own, one, two, low, high, right, out, left):
    half = low.shape[0]
    for j, block in enumerate((own, one, two)):

        @pl.when(pl.program_id(0) == j)
        def _():
            left[...] = block[...]

    @pl.when(pl.program_id(0) == 3)
    def _():
        left[:half, :] = low[...]
        left[half:, :] = high[...]

    out[...] = product(left[...], right[...]).astype(BF16)


def weight_kernel(*refs):
    count = len(refs) // 2
    total = tn(refs[0][...], refs[count][...])
    for m in range(1, count):
        total = total + tn(refs[m][...], refs[count + m][...])
    refs[-1][...] = total.astype(BF16)


def both_weights_kernel(count, *refs):
    normed, gates, gated, cots = (refs[i * count : (i + 1) * count] for i in range(4))
    out = refs[-1]
    gate = sum(tn(a[...], b[...]) for a, b in zip(normed, gates))
    back = sum(tn(a[...], b[...]) for a, b in zip(gated, cots))
    rows, width = gate.shape
    half = back.shape[0]
    out[0, :rows] = gate.astype(BF16)
    for part in range(back.shape[1] // width):
        out[0, rows + part * half : rows + (part + 1) * half] = back[:, part * width : (part + 1) * width].astype(BF16)


def branch_kernel(left, right, *outs):
    value = nn(left[...], right[...]).astype(BF16)
    for q, out in enumerate(outs):

        @pl.when(pl.program_id(0) == q)
        def _():
            out[...] = value


def grad_kernel(mix, gate, w_mix, w_gate, normed, o0, o1, o2, o3, pre):
    @pl.when(pl.program_id(0) == 0)
    def _():
        pre[...] = jnp.zeros_like(pre)

    grad = nt(mix[...], w_mix[...]) + nt(gate[...], w_gate[...])
    pre[0:1, :] += jnp.sum(grad * normed[...].astype(F32), axis=0, keepdims=True)
    grad = grad.astype(BF16)
    for q, out in enumerate((o0, o1, o2, o3)):

        @pl.when(pl.program_id(0) == q)
        def _():
            out[...] = grad


def ordered(place, blocks):
    odd = (place & 1) == 1
    high = (place & 2) == 2
    a, b, c, d = blocks
    a, b = jnp.where(odd, b, a), jnp.where(odd, a, b)
    c, d = jnp.where(odd, d, c), jnp.where(odd, c, d)
    return [jnp.where(high, c, a), jnp.where(high, d, b), jnp.where(high, a, c), jnp.where(high, b, d)]


def turned(place, blocks, out):
    unit = blocks[0].shape[1]
    for q, block in enumerate(ordered(place[0], [b[...].astype(F32) for b in blocks])):
        out[q * unit : (q + 1) * unit, :] = block.T


def gate_grad_kernel(place, g0, g1, g2, g3, out):
    turned(place, (g0, g1, g2, g3), out)


def mix_grad_kernel(groups, heads, before, place, *refs):
    mixes, lasts, (where_heads, out) = refs[:4], refs[4:8], refs[8:]
    step = pl.program_id(0)

    @pl.when(step < groups)
    def _():
        turned(place, mixes, out)

    @pl.when(step == groups)
    def _():
        both = ordered(place[0], [b[:, : 2 * STATE].astype(F32) for b in lasts])
        out[: 2 * STATE, :] = ((both[0] + both[1]) + (both[2] + both[3])).T
        steps = ordered(place[0], [b[:, 2 * STATE :] for b in lasts])
        placed = nn(steps[0], where_heads[0])
        for q in range(1, 4):
            placed = placed + nn(steps[q], where_heads[q])
        out[2 * STATE : 2 * STATE + 4 * heads, :] = placed.T[: 4 * heads, :]


def out_grad_kernel(rows, place, b0, b1, b2, b3, out):
    from_rep = place[0] ^ pl.program_id(0)
    count = out.shape[0]
    for j, block in enumerate((b0, b1, b2, b3)):

        @pl.when(from_rep == j)
        def _():
            width = block.shape[1]
            for part in range(out.shape[1] // width):
                first = rows + part * count
                out[:, part * width : (part + 1) * width] = block[first : first + count, :].astype(F32)


def each(*shape):
    return pl.BlockSpec((1,) + shape, lambda i: (i, 0, 0))


def whole(*shape):
    return pl.BlockSpec(shape, lambda i: (0,) * len(shape))


def call(kernel, slots, ins, outs, scratch, us, held=None, alias=None):
    arrays = [a for a, _ in ins]
    if held is not None:
        arrays[0] = held(arrays[0])
    out_shape = [o for o, _ in outs]
    return pl.pallas_call(
        kernel,
        grid=(slots,),
        in_specs=[s for _, s in ins],
        out_specs=[s for _, s in outs],
        out_shape=out_shape,
        scratch_shapes=scratch,
        input_output_aliases=alias or {},
        compiler_params=pltpu.CompilerParams(
            dimension_semantics=("arbitrary",), vmem_limit_bytes=56 * 1024 * 1024
        ),
        cost_estimate=pl.CostEstimate(
            flops=int(us * slots * 1.1e9 * COST), bytes_accessed=int(us * slots * 1e6 * COST), transcendentals=0
        ),
    )(*arrays)


def sds(shape, dtype):
    return jax.ShapeDtypeStruct(shape, dtype)


def rows_times(left, right, product, block, held):
    rows, depth = left.shape
    width = right.shape[1] if product is nn else right.shape[0]
    (out,) = call(
        functools.partial(rows_kernel, product),
        rows // block,
        [(left, pl.BlockSpec((block, depth), lambda i: (i, 0))), (right, whole(*right.shape))],
        [(sds((rows, width), BF16), pl.BlockSpec((block, width), lambda i: (i, 0)))],
        [],
        2.0,
        held,
    )
    return out


def gathered_times(parts, right, product, held):
    rows, depth = parts[0].shape
    width = right.shape[1] if product is nn else right.shape[0]
    block = lambda w: (sds((4 * rows, w), BF16), pl.BlockSpec((rows, w), lambda i: (i, 0)))
    return call(
        functools.partial(gathered_kernel, product),
        4,
        [(v, whole(*v.shape)) for v in parts] + [(right, whole(*right.shape))],
        [block(width), block(depth)],
        [],
        2.7,
        held,
    )


def weight_sum(lefts, rights, held, us=2.0):
    rows, width = lefts[0].shape
    depth = rights[0].shape[1]
    block = min(256, width)
    (out,) = call(
        weight_kernel,
        width // block,
        [(v, pl.BlockSpec((rows, block), lambda i: (0, i))) for v in lefts] + [(v, whole(*v.shape)) for v in rights],
        [(sds((width, depth), BF16), pl.BlockSpec((block, depth), lambda i: (i, 0)))],
        [],
        us,
        held,
    )
    return out


def per_device(
    tokens, lengths, pre_gain, in_weight, conv_weight, conv_bias, step_bias, decay_log, skip_gain,
    norm_gain, out_weight, cotangent,
):
    micro, length, model = tokens.shape
    reps = lax.axis_size("rep")
    pieces = lax.axis_size("seq")
    rep = lax.axis_index("rep")
    inner = norm_gain.shape[0]
    heads = HEADS // reps
    width = heads * HEAD_DIM
    rows = reps * length
    xbc = width + 2 * STATE
    cols = xbc + LANES
    groups = pieces if HEADS % (pieces * reps) == 0 else 1
    strided = groups == pieces

    def pick(v, unit):
        each_group = heads // groups * unit
        v = v.reshape(v.shape[:-1] + (groups, reps, each_group))
        v = lax.dynamic_index_in_dim(v, rep, v.ndim - 2, False)
        return v.reshape(v.shape[:-2] + (groups * each_group,))

    def unpick(parts, unit):
        each_group = heads // groups * unit
        lead = parts[0].shape[:-1]
        v = jnp.stack([q.reshape(lead + (groups, each_group)) for q in parts], axis=-2)
        return v.reshape(lead + (HEADS * unit,))

    def lanes_of(v):
        return jnp.pad(v, [(0, 0)] * (v.ndim - 1) + [(0, LANES - v.shape[-1])])

    def conv_share(v):
        return jnp.concatenate([pick(v[..., :inner], HEAD_DIM), v[..., inner:]], axis=-1)

    position = lax.axis_index("seq") * length + jnp.arange(length, dtype=jnp.int32)
    valid = (position[None, :] < lengths[:, None])[..., None]
    token_rows = tokens.astype(F32)
    inverse = lax.rsqrt(jnp.mean(token_rows * token_rows, axis=-1, keepdims=True) + EPSILON)
    normed = (token_rows * inverse * pre_gain).astype(BF16)
    masked = jnp.where(valid, cotangent, jnp.zeros_like(cotangent))

    w_mix = jnp.concatenate(
        [
            pick(in_weight[:, inner : 2 * inner], HEAD_DIM),
            in_weight[:, 2 * inner : 2 * inner + 2 * STATE],
            lanes_of(pick(in_weight[:, 2 * inner + 2 * STATE :], 1)),
        ],
        axis=1,
    )
    w_gate = pick(in_weight[:, :inner], HEAD_DIM)
    w_mix = lax.all_gather(w_mix, "seq", axis=0, tiled=True)
    w_gate = lax.all_gather(w_gate, "seq", axis=0, tiled=True)
    if strided:
        share = out_weight.shape[0] // reps
        w_out = lax.dynamic_slice_in_dim(out_weight, rep * share, share, 0)
        w_out = lax.all_gather(w_out, "seq", axis=0, tiled=True)
    else:
        w_out = lax.all_gather(out_weight, "seq", axis=0, tiled=True)
        w_out = lax.dynamic_slice_in_dim(w_out, rep * width, width, 0)

    spread_row = jnp.arange(LANES, dtype=jnp.int32)[:, None]
    spread = (
        (spread_row < LANES // 2)
        & (spread_row % (LANES // 4) == jnp.arange(width, dtype=jnp.int32)[None, :] // HEAD_DIM)
    ).astype(BF16)
    fold = (
        jnp.arange(width, dtype=jnp.int32)[:, None] // HEAD_DIM
        == jnp.arange(LANES, dtype=jnp.int32)[None, :]
    ).astype(BF16)

    cw = conv_share(conv_weight)
    cb = conv_share(conv_bias)[None, :]
    sb = lanes_of(pick(step_bias, 1))[None, :]
    dl = lanes_of(pick(decay_log, 1))[None, :]
    skip = jnp.repeat(pick(skip_gain, 1), HEAD_DIM)[None, :]
    gain = pick(norm_gain, HEAD_DIM)[None, :]

    line = []

    def held(*others):
        return lambda value: after(value, *line, *others)

    def later(values):
        return list(after(tuple(values), *line))

    def ran(out):
        line[:] = [out]
        return out

    row_spec = lambda w: pl.BlockSpec((length, w), lambda i: (i, 0))
    small = [
        (cw, whole(KCONV, xbc)),
        (cb, whole(1, xbc)),
        (sb, whole(1, LANES)),
        (dl, whole(1, LANES)),
    ]
    spread_in = (spread, whole(LANES, width))
    gain_in = (gain, whole(1, width))
    skip_in = (skip, whole(1, width))
    wide = lambda v: (v, row_spec(width))
    state = lambda v: (v, each(STATE, width))
    out_wide = lambda t: (sds((rows, width), t), row_spec(width))
    out_state = (sds((reps, STATE, width), F32), each(STATE, width))
    out_message = (sds((reps, STATE + MARK, width), BF16), each(STATE + MARK, width))
    out_gain = (sds((PAD, width), F32), whole(PAD, width))
    ext = pltpu.VMEM((length + PAD, LANES), F32)

    proj_in, halo_in, x_in, bc_in, sl_in, part_in, fade_in, start_in = ([None] * micro for _ in range(8))
    gate_in, grad_in, y_in, sums, inside = ([None] * micro for _ in range(5))
    forward_chain = [None] * micro

    def project(m, *others):
        proj, normed_all[m] = gathered_times(normed_parts[m], w_mix, nn, held(*others))
        ran(proj)
        tail = proj.reshape(reps, length, cols)[:, length - (KCONV - 1) :, :xbc]
        halo = lax.ppermute(tail, "seq", [(i, i + 1) for i in range(pieces - 1)])
        halo = jnp.pad(halo.astype(F32), ((0, 0), (PAD - (KCONV - 1), 0), (0, 0)))
        proj_in[m], halo_in[m] = (proj, row_spec(cols)), (halo, each(PAD, xbc))

    def front(m, *others):
        x, bc, sl, part, message, fade = call(
            front_kernel,
            reps,
            [proj_in[m], halo_in[m]] + small + [spread_in],
            [
                out_wide(F32),
                (sds((rows, 4 * STATE), BF16), row_spec(4 * STATE)),
                (sds((rows, 2 * LANES), F32), row_spec(2 * LANES)),
                out_state,
                out_message,
                (sds((reps, 1, width), F32), each(1, width)),
            ],
            [ext],
            2.3,
            held(*others),
        )
        ran(fade)
        x_in[m], bc_in[m], sl_in[m] = wide(x), (bc, row_spec(4 * STATE)), (sl, row_spec(2 * LANES))
        part_in[m], fade_in[m] = state(part), (fade, each(1, width))
        forward_chain[m] = Chain(fade, part, message, False)

    def within(m, *others):
        (inside[m],) = call(
            inside_kernel, reps, [x_in[m], bc_in[m], sl_in[m], spread_in], [out_wide(F32)], [], 2.2, held(*others)
        )
        ran(inside[m])

    def gate_of(m, *others):
        gate_in[m] = wide(ran(rows_times(normed_all[m], w_gate, nn, length, held(*others))))

    def grad_of(m, *others):
        grad, cot_all[m] = gathered_times(later(cot_parts[m]), w_out, nt, held(*others))
        grad_in[m] = wide(ran(grad))

    def gating(m, *others):
        start_in[m] = state(forward_chain[m].end())
        y, partial = call(
            gate_kernel,
            reps,
            [wide(inside[m]), x_in[m], bc_in[m], sl_in[m], start_in[m], gate_in[m], grad_in[m], gain_in, skip_in, spread_in],
            [out_wide(F32), (sds((reps, PAD, length), F32), each(PAD, length))],
            [],
            2.8,
            held(*others),
        )
        ran(partial)
        y_in[m] = wide(y)
        partial = sum_aligned(partial[:, :2])
        sums[m] = (jnp.pad(partial, ((0, 0), (0, PAD - 2), (0, 0))), each(PAD, length))

    near = [gather_near(normed[0])]
    far = [to_far(near[0])]
    normed_all, cot_all = [None] * micro, [None] * micro
    normed_parts = [far_parts(near[0], far[0])]
    near.append(gather_near(after(normed[1], *normed_parts[0][3:])))
    project(0, near[1][0])
    near[1] = later(near[1])
    far.append(to_far(near[1]))
    normed_parts.append(far_parts(near[1], far[1]))
    front(0, *far[1])
    cot_near = [gather_near(after(masked[0], *line))]
    project(1, cot_near[0][0])
    front(1, forward_chain[0].hop())
    gate_of(0)
    cot_near[0] = later(cot_near[0])
    cot_far = [to_far(cot_near[0])]
    cot_near.append(gather_near(after(masked[1], *line, *cot_far[0])))
    cot_parts = [far_parts(cot_near[0], cot_far[0])]
    within(0, forward_chain[0].hop(), forward_chain[1].hop(), cot_near[1][0])
    gate_of(1)
    within(1, forward_chain[0].hop(), forward_chain[1].hop())
    cot_near[1] = later(cot_near[1])
    cot_far.append(to_far(cot_near[1]))
    cot_parts.append(far_parts(cot_near[1], cot_far[1]))
    grad_of(0, *cot_far[1])
    forward_chain[0].rest()
    grad_of(1, forward_chain[0].back(), forward_chain[1].hop())
    forward_chain[1].rest()
    gating(0, forward_chain[1].back())
    gating(1)

    gated, dy_in, dgate, later_in, gains, skips = ([None] * micro for _ in range(6))
    backward_chain = [None] * micro

    def normalise(m, *others):
        gated[m], dy, dgate[m], dstart, message, gains[m], skips[m] = call(
            functools.partial(norm_kernel, float(inner)),
            reps,
            [y_in[m], x_in[m], bc_in[m], sl_in[m], gate_in[m], grad_in[m], gain_in, skip_in, fade_in[m], sums[m], spread_in],
            [out_wide(BF16), out_wide(BF16), out_wide(BF16), out_state, out_message, out_gain, out_gain],
            [],
            3.1,
            held(*others),
        )
        ran(gains[m])
        dy_in[m] = wide(dy)
        backward_chain[m] = Chain(fade_in[m][0], dstart, message, True)

    inner_back = [None] * micro

    def within_back(m, *others):
        inner_back[m] = call(
            inside_back_kernel,
            reps,
            [x_in[m], bc_in[m], sl_in[m], dy_in[m], start_in[m], spread_in],
            [out_wide(F32), (sds((rows, 2 * STATE), F32), row_spec(2 * STATE))],
            [],
            3.6 * LOW,
            held(*others),
        )
        ran(inner_back[m][1])

    pgs, smalls = [None] * micro, [None] * micro

    def back(m, *others):
        dxs, dbc = inner_back[m]
        later_in[m] = state(backward_chain[m].end())
        pg, halo_grad, tail_grad, *smalls[m] = call(
            back_kernel,
            reps,
            [proj_in[m], halo_in[m]] + small
            + [skip_in, spread_in, (fold, whole(width, LANES)), x_in[m], bc_in[m], sl_in[m], y_in[m], dy_in[m]]
            + [wide(dxs), (dbc, row_spec(2 * STATE)), start_in[m], part_in[m], fade_in[m], later_in[m]],
            [
                (sds((rows, cols), BF16), row_spec(cols)),
                (sds((reps, PAD, xbc), F32), each(PAD, xbc)),
                (sds((reps, PAD, xbc), F32), each(PAD, xbc)),
                (sds((PAD, xbc), F32), whole(PAD, xbc)),
                (sds((PAD, xbc), F32), whole(PAD, xbc)),
                (sds((PAD, LANES), F32), whole(PAD, LANES)),
                (sds((PAD, LANES), F32), whole(PAD, LANES)),
            ],
            [ext, pltpu.VMEM((length + 2 * PAD, LANES), F32)],
            5.1 * LOW,
            held(*others),
        )
        ran(smalls[m][0])
        from_next = lax.ppermute(
            halo_grad[:, PAD - (KCONV - 1) :].astype(BF16), "seq", [(i, i - 1) for i in range(1, pieces)]
        )
        pgs[m] = pg, tail_grad[:, PAD - (KCONV - 1) :], from_next

    def complete(m):
        pg, last_rows, from_next = pgs[m]
        last_rows = last_rows + later([from_next])[0].astype(F32)
        pgs[m] = lax.dynamic_update_slice(
            pg.reshape(reps, length, cols), last_rows.astype(BF16), (0, length - (KCONV - 1), 0)
        ).reshape(rows, cols)

    normed_grad, pre_parts = [None] * micro, [None] * micro

    def grad_through(m, *others):
        *blocks, pre = call(
            grad_kernel,
            reps,
            [(pgs[m], row_spec(cols)), wide(dgate[m]), (w_mix, whole(*w_mix.shape)), (w_gate, whole(*w_gate.shape))]
            + [(normed_all[m], row_spec(model))],
            [(sds((length, model), BF16), whole(length, model))] * reps + [(sds((PAD, model), F32), whole(PAD, model))],
            [],
            30.0 if m == micro - 1 else 10.0,
            held(*others),
        )
        pre_parts[m] = ran(pre)[0]
        normed_grad[m] = blocks[:1] + [swap(blocks[q], "rep", q) for q in (1, 2, 3)]

    def over_seq(parts):
        return lax.psum_scatter(parts, "seq", scatter_dimension=0, tiled=True)

    def project_out(m, *others):
        blocks = call(
            branch_kernel,
            reps,
            [wide(gated[m]), (w_out, whole(*w_out.shape))],
            [(sds((length, model), BF16), whole(length, model))] * reps,
            [],
            1.9,
            held(*others),
        )
        ran(blocks[0])
        return list(blocks[:1]) + [swap(blocks[q], "rep", q) for q in (1, 2, 3)]

    normalise(0)
    branch = [project_out(0)]
    normalise(1, backward_chain[0].hop())
    branch.append(project_out(1))
    within_back(0, backward_chain[0].hop(), backward_chain[1].hop())
    within_back(1, backward_chain[0].hop(), backward_chain[1].hop())
    backward_chain[0].rest()
    back(0, backward_chain[0].back(), backward_chain[1].hop())
    backward_chain[1].rest()
    if strided:
        k_rows, out_share = model // pieces, width // pieces
        both_rows = k_rows + out_share * model // width
        columns = lambda w: pl.BlockSpec((rows, w), lambda i: (0, i))
        (both_part,) = call(
            functools.partial(both_weights_kernel, micro),
            pieces,
            [(v, columns(k_rows)) for v in normed_all]
            + [(v, whole(*v.shape)) for v in dgate]
            + [(v, columns(out_share)) for v in gated]
            + [(v, whole(*v.shape)) for v in cot_all],
            [(sds((pieces, both_rows, width), BF16), each(both_rows, width))],
            [],
            3.2,
            held(backward_chain[1].back()),
        )
        ran(both_part)
        gate_sums = out_sums = over_seq(both_part)[0]
    else:
        gate_sums = over_seq(ran(weight_sum(normed_all, dgate, held(backward_chain[1].back()))))
        out_part = ran(weight_sum(gated, cot_all, held()))
        out_sums = over_seq(
            lax.dynamic_update_slice(jnp.zeros((inner, model), BF16), out_part, (rep * width, 0))
        )
    complete(0)
    back(1)
    grad_through(0, *branch[0])
    complete(1)
    gain_part, skip_part = sum(g[0] for g in gains), sum(v[0] for v in skips)
    cw_part, cb_part, sb_part, dl_part = (sum(v) for v in zip(*smalls))
    skip_heads = skip_part.reshape(heads, HEAD_DIM).sum(axis=1)
    packed = jnp.concatenate(
        [cw_part[:KCONV].reshape(-1), cb_part[0], gain_part, lanes_of(skip_heads), sb_part[0], dl_part[0]]
    )
    branch = [later(b) for b in branch]
    output = jnp.stack([sum(v.astype(F32) for v in b) for b in branch])
    output = jnp.where(valid, token_rows + output, 0.0).astype(BF16)
    mix_part = ran(weight_sum(normed_all, pgs, held(output), 5.0))
    mix_sums = over_seq(after(mix_part, gate_sums, out_sums))
    gate_rows = gather_direct(gate_sums)
    out_rows = gate_rows if strided else gather_direct(out_sums)
    grad_through(1, *normed_grad[0])
    pre_part = sum(pre_parts)
    small_sums = SmallSums(jnp.concatenate([packed, pre_part]).reshape(-1, LANES)).rest()
    normed_grad = [list(after(tuple(v), mix_sums)) for v in normed_grad]

    normed_grad = jnp.stack([sum(v.astype(F32) for v in n) for n in normed_grad])
    xhat = token_rows * inverse
    scaled = normed_grad * pre_gain
    rows_grad = inverse * (scaled - xhat * jnp.mean(scaled * xhat, axis=-1, keepdims=True))
    tokens_grad = jnp.where(valid, cotangent.astype(F32), 0.0) + rows_grad

    rep_scalar = rep.astype(jnp.int32).reshape(1)
    place_in = (rep_scalar, pl.BlockSpec(memory_space=pltpu.SMEM))
    local = jnp.arange(LANES, dtype=jnp.int32)
    a_group = heads // groups
    head_of = (local[None, :] // a_group * reps + jnp.arange(reps, dtype=jnp.int32)[:, None]) * a_group + local % a_group
    head_of = jnp.where(local < heads, head_of, -1)
    where_heads = (head_of[:, :, None] == local[None, None, :]).astype(BF16)
    unit = width // groups
    k_rows = in_weight.shape[0]
    lanes_spec = lambda index: pl.BlockSpec((k_rows, unit), lambda i: (0, index(i)))
    column = lambda first: (
        sds(in_weight.shape[::-1], F32),
        pl.BlockSpec((reps * unit, k_rows), lambda i: (i + first, 0)),
    )
    finished = []
    if strided:
        (out_weight_grad,) = call(
            functools.partial(out_grad_kernel, k_rows),
            reps,
            [place_in] + [(b, whole(*b.shape)) for b in out_rows],
            [(sds(out_weight.shape, F32), pl.BlockSpec((out_share, model), lambda i: (i, 0)))],
            [],
            0.9,
        )
        (gate_done,) = call(
            gate_grad_kernel,
            groups,
            [place_in] + [(b, lanes_spec(lambda i: i)) for b in gate_rows],
            [column(0)],
            [],
            0.8,
        )
        finished = [out_weight_grad, gate_done]
    mix_rows = gather_direct(after(mix_sums, *finished))
    packed = gather_direct(after(small_sums, mix_sums))
    if strided:
        (in_weight_grad,) = call(
            functools.partial(mix_grad_kernel, groups, heads),
            groups + 1,
            [(gate_done, pl.BlockSpec(memory_space=pl.ANY)), place_in]
            + [(b, lanes_spec(lambda i: jnp.minimum(i, groups - 1))) for b in mix_rows]
            + [(b[:, width:], whole(k_rows, cols - width)) for b in mix_rows]
            + [(where_heads, whole(reps, LANES, LANES))],
            [column(groups)],
            [],
            0.5,
            alias={0: 0},
        )
        in_weight_grad = in_weight_grad.T
    else:
        out_weight_grad = sum(v.astype(F32) for v in in_order(out_rows))
        gates, mixes = in_order(gate_rows), in_order(mix_rows)
        in_weight_grad = jnp.concatenate(
            [
                unpick(gates, HEAD_DIM).astype(F32),
                unpick([v[:, :width] for v in mixes], HEAD_DIM).astype(F32),
                sum(v[:, width:xbc].astype(F32) for v in mixes),
                unpick([v[:, xbc : xbc + heads] for v in mixes], 1).astype(F32),
            ],
            axis=1,
        )
    flat = [v.reshape(-1) for v in in_order(packed)]
    def conv_join(values):
        return jnp.concatenate(
            [unpick([v[..., :width] for v in values], HEAD_DIM), sum(v[..., width:] for v in values)], axis=-1
        )

    conv_weight_grad = conv_join([v[: KCONV * xbc].reshape(KCONV, xbc) for v in flat])
    at = KCONV * xbc
    conv_bias_grad = conv_join([v[at : at + xbc] for v in flat])
    at += xbc
    norm_gain_grad = unpick([v[at : at + width] for v in flat], HEAD_DIM)
    at += width
    by_head = [lax.optimization_barrier(v[at : at + 3 * LANES]).reshape(3, LANES)[:, :heads] for v in flat]
    skip_gain_grad, step_bias_grad, decay_log_grad = unpick(by_head, 1)

    at += 3 * LANES
    pre_gain_grad = sum(v[at : at + model] for v in flat) / pre_gain

    return (
        output, tokens_grad, pre_gain_grad, in_weight_grad, conv_weight_grad, conv_bias_grad,
        step_bias_grad, decay_log_grad, skip_gain_grad, norm_gain_grad, out_weight_grad,
    )


def solution(mesh):
    rows = P("rep", "seq", None)
    shard = P("seq", None)
    in_specs = (rows, P("rep"), P(), shard, P(), P(), P(), P(), P(), P(), shard, rows)
    out_specs = (rows, rows, P(), shard, P(), P(), P(), P(), P(), P(), shard)
    return jax.shard_map(per_device, mesh=mesh, in_specs=in_specs, out_specs=out_specs, check_vma=False)
```

```python
import functools

import jax
import jax.numpy as jnp
from jax import lax
from jax.experimental import pallas as pl
from jax.experimental.pallas import tpu as pltpu
from jax.sharding import PartitionSpec as P

HEADS = 64
HEAD_DIM = 64
STATE = 128
KCONV = 4
LANES = 128
PAD = 8
COST = 1.0
LOW = 1.0
MARK = 16
EPSILON = 1e-05
NEVER = -1e30
BF16 = jnp.bfloat16
F32 = jnp.float32


def swap(value, axis, bit):
    return lax.ppermute(value, axis, [(i, i ^ bit) for i in range(lax.axis_size(axis))])


def after(value, *others):
    return lax.optimization_barrier((value,) + others)[0]


def gather_near(own):
    return own, swap(own, "rep", 1), swap(own, "rep", 2)


def to_far(near):
    own, one, two = near
    half = own.shape[0] // 2
    return one[:half], two[half:]


def far_parts(near, sent):
    return list(near) + [swap(sent[0], "rep", 2), swap(sent[1], "rep", 1)]


def gather_halves(own):
    near = gather_near(own)
    return far_parts(near, to_far(near))


def scatter_far(far):
    half = far.shape[0] // 2
    return swap(far[:half], "rep", 1), swap(far[half:], "rep", 2)


def scatter_near(own, one, two, low, high):
    half = low.shape[0]
    two = jnp.concatenate([(two[:half].astype(F32) + low.astype(F32)).astype(BF16), two[half:]], axis=0)
    one = jnp.concatenate([one[:half], (one[half:].astype(F32) + high.astype(F32)).astype(BF16)], axis=0)
    return [own, swap(one, "rep", 1), swap(two, "rep", 2)]


def gather_direct(own):
    return [own] + [swap(own, "rep", j) for j in (1, 2, 3)]


def scatter_direct(parts):
    total = parts[0].astype(F32)
    for j in (1, 2, 3):
        total = total + swap(parts[j], "rep", j).astype(F32)
    return total


def in_order(blocks):
    stack = jnp.stack(blocks)
    place = lax.axis_index("rep")
    return [lax.dynamic_index_in_dim(stack, place ^ q, 0, False) for q in range(len(blocks))]


def sum_seq(value):
    bit = 1
    while bit < lax.axis_size("seq"):
        value = value + swap(value, "seq", bit)
        bit *= 2
    return value


class SmallSums:
    def __init__(self, value):
        self.value, self.bit = value, 1

    def hop(self):
        if self.bit < lax.axis_size("seq"):
            sent = self.value
            self.value = sent + swap(sent, "seq", self.bit)
            self.bit *= 2
        return sent

    def rest(self):
        while self.bit < lax.axis_size("seq"):
            self.hop()
        return self.value


def sum_aligned(blocks):
    total = blocks
    for bit in (1, 2, 3):
        other = swap(blocks, "rep", bit)
        total = total + jnp.stack([other[j ^ bit] for j in range(blocks.shape[0])])
    return total


class Chain:
    def __init__(self, fade, part, message, reverse):
        count = lax.axis_size("seq")
        self.chips = count // 2
        first, lead = (1, 0) if reverse else (0, 1)
        hop = -1 if reverse else 1
        chips = range(self.chips)
        self.fade, self.part = fade, part
        self.homeward = [(2 * c + lead, 2 * c + first) for c in chips]
        onward = [(2 * c + lead, 2 * (c + hop) + lead) for c in chips if 0 <= c + hop < self.chips]
        self.onward = onward[::hop]
        self.leads = lax.axis_index("seq") % 2 == lead
        self.got = lax.ppermute(message, "seq", [(2 * c + first, 2 * c + lead) for c in chips])
        self.total = None
        self.enters = 0.0

    def hop(self):
        if self.total is None:
            got = self.got
            self.mate = got[:, :STATE].astype(F32)
            self.mate_fade = got[:, STATE : STATE + 1].astype(F32) + got[:, STATE + 1 : STATE + 2].astype(F32)
            self.total = self.part + self.fade * self.mate
            self.total_fade = self.fade * self.mate_fade
            onto = self.total.astype(BF16)
        else:
            onto = (self.total + self.total_fade * self.enters.astype(F32)).astype(BF16)
        self.enters = self.enters + lax.ppermute(onto, "seq", [self.onward.pop(0)])
        return onto

    def rest(self):
        while self.onward:
            self.hop()

    def back(self):
        self.handed = lax.ppermute(self.enters, "seq", self.homeward)
        return self.enters

    def end(self):
        own = (self.mate + self.mate_fade * self.enters.astype(F32)).astype(BF16)
        return jnp.where(self.leads, own, self.handed)


def nt(a, b):
    return lax.dot_general(a, b, (((1,), (1,)), ((), ())), preferred_element_type=F32)


def tn(a, b):
    return lax.dot_general(a, b, (((0,), (0,)), ((), ())), preferred_element_type=F32)


def nn(a, b):
    return jnp.dot(a, b, preferred_element_type=F32)


def col(p):
    return slice(p * LANES, (p + 1) * LANES)


def two_parts(value):
    heads = LANES // 4
    high = value.astype(BF16)
    low = (value - high.astype(F32)).astype(BF16).astype(F32)
    lane = lax.broadcasted_iota(jnp.int32, value.shape, 1)
    both = jnp.where(
        lane < heads, high.astype(F32), jnp.where(lane < 2 * heads, pltpu.roll(low, heads, 1), 0.0)
    )
    return both.astype(BF16)


def running(value, reverse):
    rows = value.shape[0]
    place = lax.broadcasted_iota(jnp.int32, value.shape, 0)
    shift = 1
    while shift < rows:
        if reverse:
            moved = jnp.where(place < rows - shift, pltpu.roll(value, rows - shift, 0), 0.0)
        else:
            moved = jnp.where(place >= shift, pltpu.roll(value, shift, 0), 0.0)
        value = value + moved
        shift *= 2
    return value


def head_sums(product, fold):
    high = product.astype(BF16)
    low = (product - high.astype(F32)).astype(BF16)
    return nn(high, fold) + nn(low, fold)


def softplus(v):
    return jnp.maximum(v, 0.0) + jnp.log1p(jnp.exp(-jnp.abs(v)))


def sigmoid(v):
    return 1.0 / (1.0 + jnp.exp(-v))


def split(value):
    high = value.astype(BF16)
    return high, (value - high.astype(F32)).astype(BF16)


def nt_fine(a, b):
    half = a.shape[1] // 2
    return nt(
        jnp.concatenate([a, a[:, :half]], axis=1),
        jnp.concatenate([b[:, :half], b[:, :half], b[:, half:]], axis=1),
    )


def nn_fine(a_high, a_low, b):
    half = b.shape[1] // 2
    return nn(
        jnp.concatenate([a_high, a_low, a_high], axis=1),
        jnp.concatenate([b[:, :half], b[:, :half], b[:, half:]], axis=0),
    )


def twice(value):
    return jnp.concatenate([value, value], axis=0)


def tn_sum(a, b):
    both = tn(a, b)
    half = both.shape[0] // 2
    return both[:half] + both[half:]


def message_of(out, p, part, fade):
    out[0, 0:STATE, col(p)] = part.astype(BF16)
    high, low = split(fade)
    place = lax.broadcasted_iota(jnp.int32, (MARK, LANES), 0)
    rows = jnp.where(place == 0, high.astype(F32), jnp.where(place == 1, low.astype(F32), 0.0))
    out[0, STATE : STATE + MARK, col(p)] = rows.astype(BF16)


def front_kernel(
    proj, halo, cw, cb, sb, dl, spread, x_out, bc_out, sl_out, st_out, msg_out, fade_out, ext
):
    rows = proj.shape[0]
    pairs = x_out.shape[1] // LANES
    raw_step = proj[:, (pairs + 2) * LANES :].astype(F32) + sb[...]
    step = softplus(raw_step)
    log_decay = running(-step * jnp.exp(dl[...]), False)
    last = log_decay[rows - 1 : rows, :]
    sl_out[:, :LANES] = step
    sl_out[:, LANES:] = log_decay
    weight = two_parts(jnp.exp(last - log_decay) * step)
    ending = two_parts(jnp.broadcast_to(jnp.exp(last), (PAD, LANES)))
    ext_rows = pl.ds(PAD, rows)

    def activated(p):
        ext[0:PAD, :] = halo[0, :, col(p)]
        ext[ext_rows, :] = proj[:, col(p)].astype(F32)
        z = cb[:, col(p)] + cw[0:1, col(p)] * ext[pl.ds(PAD - 3, rows), :]
        for k in range(1, KCONV):
            z = z + cw[k : k + 1, col(p)] * ext[pl.ds(PAD - 3 + k, rows), :]
        return z * sigmoid(z)

    b_rows = jnp.concatenate(split(activated(pairs)), axis=1)
    bc_out[:, : 2 * STATE] = b_rows
    bc_out[:, 2 * STATE :] = jnp.concatenate(split(activated(pairs + 1)), axis=1)
    for p in range(pairs):
        x = activated(p)
        x_out[:, col(p)] = x
        scaled = (x * nn(weight, spread[:, col(p)])).astype(BF16)
        part = tn_sum(b_rows, scaled)
        fade = nn(ending, spread[:, col(p)])[0:1, :]
        st_out[0, :, col(p)] = part
        fade_out[0, :, col(p)] = fade
        message_of(msg_out, p, part, fade)


def inside_kernel(x, bc, sl, spread, y_out):
    rows = x.shape[0]
    pairs = x.shape[1] // LANES
    scores = nt_fine(bc[:, 2 * STATE :], bc[:, : 2 * STATE])
    log_decay = sl[:, LANES:]
    across = log_decay.T
    step = two_parts(sl[:, :LANES])
    t = lax.broadcasted_iota(jnp.int32, (rows, rows), 0)
    s = lax.broadcasted_iota(jnp.int32, (rows, rows), 1)
    causal = t >= s
    low_lanes = lax.broadcasted_iota(jnp.int32, (rows, LANES), 1) < HEAD_DIM
    for p in range(pairs):
        scaled = (x[:, col(p)] * nn(step, spread[:, col(p)])).astype(BF16)
        outs = []
        for h in (2 * p, 2 * p + 1):
            gap = log_decay[:, h : h + 1] - across[h : h + 1, :]
            weights = (scores * jnp.exp(jnp.where(causal, gap, NEVER))).astype(BF16)
            outs.append(nn(weights, scaled))
        y_out[:, col(p)] = jnp.where(low_lanes, outs[0], outs[1])


def gate_kernel(y, x, bc, sl, start, gate, grad, gain, skip, spread, y_out, sums_out):
    rows = x.shape[0]
    pairs = x.shape[1] // LANES
    c_rows = bc[:, 2 * STATE :]
    decay = two_parts(jnp.exp(sl[:, LANES:]))
    squares = jnp.zeros((rows, LANES), F32)
    cross = jnp.zeros((rows, LANES), F32)
    for p in range(pairs):
        plain = y[:, col(p)] + nn(decay, spread[:, col(p)]) * nn(c_rows, twice(start[0, :, col(p)]))
        y_out[:, col(p)] = plain
        g = gate[:, col(p)].astype(F32)
        v = (plain + skip[:, col(p)] * x[:, col(p)]) * (g * sigmoid(g))
        squares = squares + v * v
        cross = cross + grad[:, col(p)].astype(F32) * gain[:, col(p)] * v
    lane = lax.broadcasted_iota(jnp.int32, (rows, LANES), 1)
    both = jnp.where(
        lane == 0,
        jnp.sum(squares, axis=1, keepdims=True),
        jnp.where(lane == 1, jnp.sum(cross, axis=1, keepdims=True), 0.0),
    )
    sums_out[0] = both.T[0:PAD, :]


def norm_kernel(
    inner, y, x, bc, sl, gate, grad, gain, skip, fade, sums, spread,
    gated_out, dy_out, dgate_out, dstart_out, msg_out, gain_out, skip_out,
):
    rows = x.shape[0]
    pairs = x.shape[1] // LANES

    @pl.when(pl.program_id(0) == 0)
    def _():
        gain_out[...] = jnp.zeros_like(gain_out)
        skip_out[...] = jnp.zeros_like(skip_out)

    c_rows = bc[:, 2 * STATE :]
    decay = two_parts(jnp.exp(sl[:, LANES:]))
    padded = jnp.concatenate([sums[0], jnp.zeros((LANES - PAD, rows), F32)], axis=0).T
    scale = lax.rsqrt(padded[:, 0:1] / inner + EPSILON)
    back = scale * scale * (padded[:, 1:2] / inner)
    for p in range(pairs):
        g = gate[:, col(p)].astype(F32)
        sg = sigmoid(g)
        silu = g * sg
        xp = x[:, col(p)]
        yp = y[:, col(p)] + skip[:, col(p)] * xp
        v = yp * silu
        gp = grad[:, col(p)].astype(F32)
        normal = v * scale
        gated_out[:, col(p)] = (normal * gain[:, col(p)]).astype(BF16)
        gain_out[0:1, col(p)] += jnp.sum(gp * normal, axis=0, keepdims=True)
        dv = scale * (gp * gain[:, col(p)] - v * back)
        dy = (dv * silu).astype(BF16)
        dy_out[:, col(p)] = dy
        dyf = dy.astype(F32)
        dgate_out[:, col(p)] = (dv * yp * (sg * (1.0 + g * (1.0 - sg)))).astype(BF16)
        skip_out[0:1, col(p)] += jnp.sum(dyf * xp, axis=0, keepdims=True)
        faded = (dyf * nn(decay, spread[:, col(p)])).astype(BF16)
        dstart = tn_sum(c_rows, faded)
        dstart_out[0, :, col(p)] = dstart
        message_of(msg_out, p, dstart, fade[0, :, col(p)])


def inside_back_kernel(x, bc, sl, dy, start, spread, dxs_out, dbc_out):
    rows = x.shape[0]
    pairs = x.shape[1] // LANES
    b_rows = bc[:, : 2 * STATE]
    c_rows = bc[:, 2 * STATE :]
    scores = nt_fine(b_rows, c_rows)
    log_decay = sl[:, LANES:]
    across = log_decay.T
    step = two_parts(sl[:, :LANES])
    decay = two_parts(jnp.exp(log_decay))
    s = lax.broadcasted_iota(jnp.int32, (rows, rows), 0)
    t = lax.broadcasted_iota(jnp.int32, (rows, rows), 1)
    causal = t >= s
    low_lanes = lax.broadcasted_iota(jnp.int32, (rows, LANES), 1) < HEAD_DIM
    score_grad = jnp.zeros((rows, rows), F32)
    dc = jnp.zeros((rows, LANES), F32)
    for p in range(pairs):
        scaled = x[:, col(p)] * nn(step, spread[:, col(p)])
        dyp = dy[:, col(p)]
        faded = (dyp.astype(F32) * nn(decay, spread[:, col(p)])).astype(BF16)
        dc = dc + nt(faded, start[0, :, col(p)])
        outs = []
        for h in (2 * p, 2 * p + 1):
            gap = across[h : h + 1, :] - log_decay[:, h : h + 1]
            fall = jnp.exp(jnp.where(causal, gap, NEVER))
            weights = (scores * fall).astype(BF16)
            outs.append(nn(weights, dyp))
            mine = low_lanes if h % 2 == 0 else jnp.logical_not(low_lanes)
            score_grad = score_grad + fall * nt(jnp.where(mine, scaled, 0.0).astype(BF16), dyp)
        dxs_out[:, col(p)] = jnp.where(low_lanes, outs[0], outs[1])
    dbc_out[:, col(0)] = nn_fine(*split(score_grad), c_rows)
    dbc_out[:, col(1)] = dc + nn_fine(*split(score_grad.T), b_rows)


def back_kernel(
    proj, halo, cw, cb, sb, dl, skip, spread, fold, x, bc, sl, y, dy, dxs, dbc, start, part, fade, later,
    pg_out, halo_out, tail_out, cw_out, cb_out, sb_out, dl_out, ext, dext,
):
    rows = x.shape[0]
    pairs = x.shape[1] // LANES

    @pl.when(pl.program_id(0) == 0)
    def _():
        for out in (cw_out, cb_out, sb_out, dl_out):
            out[...] = jnp.zeros_like(out)

    rate = jnp.exp(dl[...])
    step_f = sl[:, :LANES]
    log_decay = sl[:, LANES:]
    last = log_decay[rows - 1 : rows, :]
    step = two_parts(step_f)
    to_end = two_parts(jnp.exp(last - log_decay))
    b_rows = bc[:, : 2 * STATE]
    dext[0:PAD, :] = jnp.zeros((PAD, LANES), F32)
    dext[pl.ds(PAD + rows, PAD), :] = jnp.zeros((PAD, LANES), F32)

    def through_conv(p, grad):
        ext[0:PAD, :] = halo[0, :, col(p)]
        ext[pl.ds(PAD, rows), :] = proj[:, col(p)].astype(F32)
        taps = [ext[pl.ds(PAD - 3 + k, rows), :] for k in range(KCONV)]
        z = cb[:, col(p)] + cw[0:1, col(p)] * taps[0]
        for k in range(1, KCONV):
            z = z + cw[k : k + 1, col(p)] * taps[k]
        sg = sigmoid(z)
        dz = grad * (sg * (1.0 + z * (1.0 - sg)))
        cb_out[0:1, col(p)] += jnp.sum(dz, axis=0, keepdims=True)
        for k in range(KCONV):
            cw_out[k : k + 1, col(p)] += jnp.sum(dz * taps[k], axis=0, keepdims=True)
        dext[pl.ds(PAD, rows), :] = dz
        whole = rows + PAD
        dm = cw[KCONV - 1 : KCONV, col(p)] * dext[pl.ds(0, whole), :]
        for k in range(KCONV - 1):
            dm = dm + cw[k : k + 1, col(p)] * dext[pl.ds(KCONV - 1 - k, whole), :]
        halo_out[0, :, col(p)] = dm[0:PAD, :]
        pg_out[:, col(p)] = dm[PAD:, :].astype(BF16)
        tail_out[0, :, col(p)] = dm[rows:, :]

    db = dbc[:, col(0)]
    dstep = jnp.zeros((rows, LANES), F32)
    dlog = jnp.zeros((rows, LANES), F32)
    dlast = jnp.zeros((PAD, LANES), F32)
    for p in range(pairs):
        xp = x[:, col(p)]
        step_p = nn(step, spread[:, col(p)])
        end_p = nn(to_end, spread[:, col(p)])
        later_p = later[0, :, col(p)]
        dyf = dy[:, col(p)].astype(F32)
        scaled = xp * step_p
        dxs_p = dxs[:, col(p)] + end_p * nn(b_rows, twice(later_p))
        db = db + nt((end_p * scaled).astype(BF16), later_p)
        dstep = dstep + head_sums(xp * dxs_p, fold[col(p), :])
        dlog = dlog + head_sums(dyf * y[:, col(p)] - scaled * dxs_p, fold[col(p), :])
        end_state = fade[0, :, col(p)] * start[0, :, col(p)].astype(F32) + part[0, :, col(p)]
        ends = jnp.sum(later_p.astype(F32) * end_state, axis=0, keepdims=True)
        dlast = dlast + head_sums(jnp.broadcast_to(ends, (PAD, LANES)), fold[col(p), :])
        through_conv(p, step_p * dxs_p + skip[:, col(p)] * dyf)
    through_conv(pairs, db)
    through_conv(pairs + 1, dbc[:, col(1)])
    place = lax.broadcasted_iota(jnp.int32, (rows, LANES), 0)
    dlog = dlog + jnp.where(place == rows - 1, dlast[0:1, :], 0.0)
    da = running(dlog, True)
    dstep = dstep - rate * da
    raw_step = proj[:, (pairs + 2) * LANES :].astype(F32) + sb[...]
    draw = dstep * sigmoid(raw_step)
    pg_out[:, (pairs + 2) * LANES :] = draw.astype(BF16)
    sb_out[0:1, :] += jnp.sum(draw, axis=0, keepdims=True)
    dl_out[0:1, :] += -rate * jnp.sum(step_f * da, axis=0, keepdims=True)


def rows_kernel(product, left, right, out):
    out[...] = product(left[...], right[...]).astype(BF16)


def gathered_kernel(product, own, one, two, low, high, right, out, left):
    half = low.shape[0]
    for j, block in enumerate((own, one, two)):

        @pl.when(pl.program_id(0) == j)
        def _():
            left[...] = block[...]

    @pl.when(pl.program_id(0) == 3)
    def _():
        left[:half, :] = low[...]
        left[half:, :] = high[...]

    out[...] = product(left[...], right[...]).astype(BF16)


def weight_kernel(*refs):
    count = len(refs) // 2
    total = tn(refs[0][...], refs[count][...])
    for m in range(1, count):
        total = total + tn(refs[m][...], refs[count + m][...])
    refs[-1][...] = total.astype(BF16)


def both_weights_kernel(count, *refs):
    normed, gates, gated, cots = (refs[i * count : (i + 1) * count] for i in range(4))
    out = refs[-1]
    gate = sum(tn(a[...], b[...]) for a, b in zip(normed, gates))
    back = sum(tn(a[...], b[...]) for a, b in zip(gated, cots))
    rows, width = gate.shape
    half = back.shape[0]
    out[0, :rows] = gate.astype(BF16)
    for part in range(back.shape[1] // width):
        out[0, rows + part * half : rows + (part + 1) * half] = back[:, part * width : (part + 1) * width].astype(BF16)


def branch_kernel(left, right, *outs):
    value = nn(left[...], right[...]).astype(BF16)
    for q, out in enumerate(outs):

        @pl.when(pl.program_id(0) == q)
        def _():
            out[...] = value


def grad_kernel(mix, gate, w_mix, w_gate, normed, o0, o1, o2, o3, pre):
    @pl.when(pl.program_id(0) == 0)
    def _():
        pre[...] = jnp.zeros_like(pre)

    grad = nt(mix[...], w_mix[...]) + nt(gate[...], w_gate[...])
    pre[0:1, :] += jnp.sum(grad * normed[...].astype(F32), axis=0, keepdims=True)
    grad = grad.astype(BF16)
    for q, out in enumerate((o0, o1, o2, o3)):

        @pl.when(pl.program_id(0) == q)
        def _():
            out[...] = grad


def ordered(place, blocks):
    odd = (place & 1) == 1
    high = (place & 2) == 2
    a, b, c, d = blocks
    a, b = jnp.where(odd, b, a), jnp.where(odd, a, b)
    c, d = jnp.where(odd, d, c), jnp.where(odd, c, d)
    return [jnp.where(high, c, a), jnp.where(high, d, b), jnp.where(high, a, c), jnp.where(high, b, d)]


def turned(place, blocks, out):
    unit = blocks[0].shape[1]
    for q, block in enumerate(ordered(place[0], [b.astype(F32) for b in blocks])):
        out[q * unit : (q + 1) * unit, :] = block.T


def gate_grad_kernel(place, g0, g1, g2, g3, out):
    turned(place, [g[...] for g in (g0, g1, g2, g3)], out)


def mix_grad_kernel(groups, heads, before, place, m0, m1, m2, low, high, where_heads, out):
    step = pl.program_id(0)
    width = heads * HEAD_DIM
    unit = width // groups

    def columns(at, count):
        whole_blocks = [m[:, pl.ds(at, count)] for m in (m0, m1, m2)]
        return whole_blocks + [jnp.concatenate([low[:, pl.ds(at, count)], high[:, pl.ds(at, count)]], axis=0)]

    @pl.when(step < groups)
    def _():
        turned(place, columns(pl.multiple_of(step * unit, LANES), unit), out)

    @pl.when(step == groups)
    def _():
        both = ordered(place[0], [b.astype(F32) for b in columns(width, 2 * STATE)])
        out[: 2 * STATE, :] = ((both[0] + both[1]) + (both[2] + both[3])).T
        steps = ordered(place[0], columns(width + 2 * STATE, LANES))
        placed = nn(steps[0], where_heads[0])
        for q in range(1, 4):
            placed = placed + nn(steps[q], where_heads[q])
        out[2 * STATE : 2 * STATE + 4 * heads, :] = placed.T[: 4 * heads, :]


def small_kernel(groups, heads, blocks, place, gain, where_heads, *refs):
    ins, (cw_out, cb_out, norm_out, head_out, pre_out) = refs[:4], refs[4:]
    parts = ordered(place[0], [b[...] for b in ins])
    total = (parts[0] + parts[1]) + (parts[2] + parts[3])
    width = groups * blocks

    def spread(out, row, first):
        for g in range(groups):
            for q in range(4):
                for k in range(blocks):
                    at = ((g * 4 + q) * blocks + k) * LANES
                    out[row : row + 1, at : at + LANES] = parts[q][first + g * blocks + k :][:1, :]

    first = 0
    for k in range(KCONV + 1):
        out, row = (cw_out, k) if k < KCONV else (cb_out, 0)
        spread(out, row, first)
        for c in (0, 1):
            at = (4 * width + c) * LANES
            out[row : row + 1, at : at + LANES] = total[first + width + c :][:1, :]
        first += width + 2
    spread(norm_out, 0, first)
    first += width
    placed = 0.0
    for q in range(4):
        rows = jnp.concatenate([parts[q][first : first + 3, :], jnp.zeros((PAD - 3, LANES), F32)], axis=0)
        placed = placed + jnp.dot(
            rows, where_heads[q].astype(F32), preferred_element_type=F32, precision=lax.Precision.HIGHEST
        )
    head_out[...] = placed
    first += 3
    for k in range(pre_out.shape[1] // LANES):
        pre_out[:, col(k)] = total[first + k :][:1, :] / gain[:, col(k)]


def out_grad_kernel(rows, place, b0, b1, b2, b3, out):
    from_rep = place[0] ^ pl.program_id(0)
    count = out.shape[0]
    for j, (block, skip) in enumerate(((b0, rows), (b1, rows), (b2, rows), (b3, 0))):

        @pl.when(from_rep == j)
        def _():
            width = block.shape[1]
            for part in range(out.shape[1] // width):
                first = skip + part * count
                out[:, part * width : (part + 1) * width] = block[first : first + count, :].astype(F32)


def each(*shape):
    return pl.BlockSpec((1,) + shape, lambda i: (i, 0, 0))


def whole(*shape):
    return pl.BlockSpec(shape, lambda i: (0,) * len(shape))


def call(kernel, slots, ins, outs, scratch, us, held=None, alias=None):
    arrays = [a for a, _ in ins]
    if held is not None:
        arrays[0] = held(arrays[0])
    out_shape = [o for o, _ in outs]
    return pl.pallas_call(
        kernel,
        grid=(slots,),
        in_specs=[s for _, s in ins],
        out_specs=[s for _, s in outs],
        out_shape=out_shape,
        scratch_shapes=scratch,
        input_output_aliases=alias or {},
        compiler_params=pltpu.CompilerParams(
            dimension_semantics=("arbitrary",), vmem_limit_bytes=56 * 1024 * 1024
        ),
        cost_estimate=pl.CostEstimate(
            flops=int(us * slots * 1.1e9 * COST), bytes_accessed=int(us * slots * 1e6 * COST), transcendentals=0
        ),
    )(*arrays)


def sds(shape, dtype):
    return jax.ShapeDtypeStruct(shape, dtype)


def rows_times(left, right, product, block, held):
    rows, depth = left.shape
    width = right.shape[1] if product is nn else right.shape[0]
    (out,) = call(
        functools.partial(rows_kernel, product),
        rows // block,
        [(left, pl.BlockSpec((block, depth), lambda i: (i, 0))), (right, whole(*right.shape))],
        [(sds((rows, width), BF16), pl.BlockSpec((block, width), lambda i: (i, 0)))],
        [],
        2.0,
        held,
    )
    return out


def gathered_times(parts, right, product, held):
    rows, depth = parts[0].shape
    width = right.shape[1] if product is nn else right.shape[0]
    block = lambda w: (sds((4 * rows, w), BF16), pl.BlockSpec((rows, w), lambda i: (i, 0)))
    return call(
        functools.partial(gathered_kernel, product),
        4,
        [(v, whole(*v.shape)) for v in parts] + [(right, whole(*right.shape))],
        [block(width), block(depth)],
        [],
        2.7,
        held,
    )


def weight_sum(lefts, rights, held, us=2.0):
    rows, width = lefts[0].shape
    depth = rights[0].shape[1]
    block = min(256, width)
    (out,) = call(
        weight_kernel,
        width // block,
        [(v, pl.BlockSpec((rows, block), lambda i: (0, i))) for v in lefts] + [(v, whole(*v.shape)) for v in rights],
        [(sds((width, depth), BF16), pl.BlockSpec((block, depth), lambda i: (i, 0)))],
        [],
        us,
        held,
    )
    return out


def per_device(
    tokens, lengths, pre_gain, in_weight, conv_weight, conv_bias, step_bias, decay_log, skip_gain,
    norm_gain, out_weight, cotangent,
):
    micro, length, model = tokens.shape
    reps = lax.axis_size("rep")
    pieces = lax.axis_size("seq")
    rep = lax.axis_index("rep")
    inner = norm_gain.shape[0]
    heads = HEADS // reps
    width = heads * HEAD_DIM
    rows = reps * length
    xbc = width + 2 * STATE
    cols = xbc + LANES
    groups = pieces if HEADS % (pieces * reps) == 0 else 1
    strided = groups == pieces

    def pick(v, unit):
        each_group = heads // groups * unit
        v = v.reshape(v.shape[:-1] + (groups, reps, each_group))
        v = lax.dynamic_index_in_dim(v, rep, v.ndim - 2, False)
        return v.reshape(v.shape[:-2] + (groups * each_group,))

    def unpick(parts, unit):
        each_group = heads // groups * unit
        lead = parts[0].shape[:-1]
        v = jnp.stack([q.reshape(lead + (groups, each_group)) for q in parts], axis=-2)
        return v.reshape(lead + (HEADS * unit,))

    def lanes_of(v):
        return jnp.pad(v, [(0, 0)] * (v.ndim - 1) + [(0, LANES - v.shape[-1])])

    def conv_share(v):
        return jnp.concatenate([pick(v[..., :inner], HEAD_DIM), v[..., inner:]], axis=-1)

    position = lax.axis_index("seq") * length + jnp.arange(length, dtype=jnp.int32)
    valid = (position[None, :] < lengths[:, None])[..., None]
    token_rows = tokens.astype(F32)
    inverse = lax.rsqrt(jnp.mean(token_rows * token_rows, axis=-1, keepdims=True) + EPSILON)
    normed = (token_rows * inverse * pre_gain).astype(BF16)
    masked = jnp.where(valid, cotangent, jnp.zeros_like(cotangent))

    w_mix = jnp.concatenate(
        [
            pick(in_weight[:, inner : 2 * inner], HEAD_DIM),
            in_weight[:, 2 * inner : 2 * inner + 2 * STATE],
            lanes_of(pick(in_weight[:, 2 * inner + 2 * STATE :], 1)),
        ],
        axis=1,
    )
    w_gate = pick(in_weight[:, :inner], HEAD_DIM)
    w_mix = lax.all_gather(w_mix, "seq", axis=0, tiled=True)
    w_gate = lax.all_gather(w_gate, "seq", axis=0, tiled=True)
    if strided:
        share = out_weight.shape[0] // reps
        w_out = lax.dynamic_slice_in_dim(out_weight, rep * share, share, 0)
        w_out = lax.all_gather(w_out, "seq", axis=0, tiled=True)
    else:
        w_out = lax.all_gather(out_weight, "seq", axis=0, tiled=True)
        w_out = lax.dynamic_slice_in_dim(w_out, rep * width, width, 0)

    spread_row = jnp.arange(LANES, dtype=jnp.int32)[:, None]
    spread = (
        (spread_row < LANES // 2)
        & (spread_row % (LANES // 4) == jnp.arange(width, dtype=jnp.int32)[None, :] // HEAD_DIM)
    ).astype(BF16)
    fold = (
        jnp.arange(width, dtype=jnp.int32)[:, None] // HEAD_DIM
        == jnp.arange(LANES, dtype=jnp.int32)[None, :]
    ).astype(BF16)

    cw = conv_share(conv_weight)
    cb = conv_share(conv_bias)[None, :]
    sb = lanes_of(pick(step_bias, 1))[None, :]
    dl = lanes_of(pick(decay_log, 1))[None, :]
    skip = jnp.repeat(pick(skip_gain, 1), HEAD_DIM)[None, :]
    gain = pick(norm_gain, HEAD_DIM)[None, :]

    line = []

    def held(*others):
        return lambda value: after(value, *line, *others)

    def later(values):
        return list(after(tuple(values), *line))

    def ran(out):
        line[:] = [out]
        return out

    row_spec = lambda w: pl.BlockSpec((length, w), lambda i: (i, 0))
    small = [
        (cw, whole(KCONV, xbc)),
        (cb, whole(1, xbc)),
        (sb, whole(1, LANES)),
        (dl, whole(1, LANES)),
    ]
    spread_in = (spread, whole(LANES, width))
    gain_in = (gain, whole(1, width))
    skip_in = (skip, whole(1, width))
    wide = lambda v: (v, row_spec(width))
    state = lambda v: (v, each(STATE, width))
    out_wide = lambda t: (sds((rows, width), t), row_spec(width))
    out_state = (sds((reps, STATE, width), F32), each(STATE, width))
    out_message = (sds((reps, STATE + MARK, width), BF16), each(STATE + MARK, width))
    out_gain = (sds((PAD, width), F32), whole(PAD, width))
    ext = pltpu.VMEM((length + PAD, LANES), F32)

    proj_in, halo_in, x_in, bc_in, sl_in, part_in, fade_in, start_in = ([None] * micro for _ in range(8))
    gate_in, grad_in, y_in, sums, inside = ([None] * micro for _ in range(5))
    forward_chain = [None] * micro

    def project(m, *others):
        proj, normed_all[m] = gathered_times(normed_parts[m], w_mix, nn, held(*others))
        ran(proj)
        tail = proj.reshape(reps, length, cols)[:, length - (KCONV - 1) :, :xbc]
        halo = lax.ppermute(tail, "seq", [(i, i + 1) for i in range(pieces - 1)])
        halo = jnp.pad(halo.astype(F32), ((0, 0), (PAD - (KCONV - 1), 0), (0, 0)))
        proj_in[m], halo_in[m] = (proj, row_spec(cols)), (halo, each(PAD, xbc))

    def front(m, *others):
        x, bc, sl, part, message, fade = call(
            front_kernel,
            reps,
            [proj_in[m], halo_in[m]] + small + [spread_in],
            [
                out_wide(F32),
                (sds((rows, 4 * STATE), BF16), row_spec(4 * STATE)),
                (sds((rows, 2 * LANES), F32), row_spec(2 * LANES)),
                out_state,
                out_message,
                (sds((reps, 1, width), F32), each(1, width)),
            ],
            [ext],
            2.3,
            held(*others),
        )
        ran(fade)
        x_in[m], bc_in[m], sl_in[m] = wide(x), (bc, row_spec(4 * STATE)), (sl, row_spec(2 * LANES))
        part_in[m], fade_in[m] = state(part), (fade, each(1, width))
        forward_chain[m] = Chain(fade, part, message, False)

    def within(m, *others):
        (inside[m],) = call(
            inside_kernel, reps, [x_in[m], bc_in[m], sl_in[m], spread_in], [out_wide(F32)], [], 2.2, held(*others)
        )
        ran(inside[m])

    def gate_of(m, *others):
        gate_in[m] = wide(ran(rows_times(normed_all[m], w_gate, nn, length, held(*others))))

    def grad_of(m, *others):
        grad, cot_all[m] = gathered_times(later(cot_parts[m]), w_out, nt, held(*others))
        grad_in[m] = wide(ran(grad))

    def gating(m, *others):
        start_in[m] = state(forward_chain[m].end())
        y, partial = call(
            gate_kernel,
            reps,
            [wide(inside[m]), x_in[m], bc_in[m], sl_in[m], start_in[m], gate_in[m], grad_in[m], gain_in, skip_in, spread_in],
            [out_wide(F32), (sds((reps, PAD, length), F32), each(PAD, length))],
            [],
            2.8,
            held(*others),
        )
        ran(partial)
        y_in[m] = wide(y)
        partial = sum_aligned(partial[:, :2])
        sums[m] = (jnp.pad(partial, ((0, 0), (0, PAD - 2), (0, 0))), each(PAD, length))

    near = [gather_near(normed[0])]
    far = [to_far(near[0])]
    normed_all, cot_all = [None] * micro, [None] * micro
    normed_parts = [far_parts(near[0], far[0])]
    near.append(gather_near(after(normed[1], *normed_parts[0][3:])))
    project(0, near[1][0])
    near[1] = later(near[1])
    far.append(to_far(near[1]))
    normed_parts.append(far_parts(near[1], far[1]))
    front(0, *far[1])
    cot_near = [gather_near(after(masked[0], *line))]
    project(1, cot_near[0][0])
    front(1, forward_chain[0].hop())
    gate_of(0)
    cot_near[0] = later(cot_near[0])
    cot_far = [to_far(cot_near[0])]
    cot_near.append(gather_near(after(masked[1], *line, *cot_far[0])))
    cot_parts = [far_parts(cot_near[0], cot_far[0])]
    within(0, forward_chain[0].hop(), forward_chain[1].hop(), cot_near[1][0])
    gate_of(1)
    within(1, forward_chain[0].hop(), forward_chain[1].hop())
    cot_near[1] = later(cot_near[1])
    cot_far.append(to_far(cot_near[1]))
    cot_parts.append(far_parts(cot_near[1], cot_far[1]))
    grad_of(0, *cot_far[1])
    forward_chain[0].rest()
    grad_of(1, forward_chain[0].back(), forward_chain[1].hop())
    forward_chain[1].rest()
    gating(0, forward_chain[1].back())
    gating(1)

    gated, dy_in, dgate, later_in, gains, skips = ([None] * micro for _ in range(6))
    backward_chain = [None] * micro

    def normalise(m, *others):
        gated[m], dy, dgate[m], dstart, message, gains[m], skips[m] = call(
            functools.partial(norm_kernel, float(inner)),
            reps,
            [y_in[m], x_in[m], bc_in[m], sl_in[m], gate_in[m], grad_in[m], gain_in, skip_in, fade_in[m], sums[m], spread_in],
            [out_wide(BF16), out_wide(BF16), out_wide(BF16), out_state, out_message, out_gain, out_gain],
            [],
            3.1,
            held(*others),
        )
        ran(gains[m])
        dy_in[m] = wide(dy)
        backward_chain[m] = Chain(fade_in[m][0], dstart, message, True)

    inner_back = [None] * micro

    def within_back(m, *others):
        inner_back[m] = call(
            inside_back_kernel,
            reps,
            [x_in[m], bc_in[m], sl_in[m], dy_in[m], start_in[m], spread_in],
            [out_wide(F32), (sds((rows, 2 * STATE), F32), row_spec(2 * STATE))],
            [],
            3.6 * LOW,
            held(*others),
        )
        ran(inner_back[m][1])

    pgs, smalls = [None] * micro, [None] * micro

    def back(m, *others):
        dxs, dbc = inner_back[m]
        later_in[m] = state(backward_chain[m].end())
        pg, halo_grad, tail_grad, *smalls[m] = call(
            back_kernel,
            reps,
            [proj_in[m], halo_in[m]] + small
            + [skip_in, spread_in, (fold, whole(width, LANES)), x_in[m], bc_in[m], sl_in[m], y_in[m], dy_in[m]]
            + [wide(dxs), (dbc, row_spec(2 * STATE)), start_in[m], part_in[m], fade_in[m], later_in[m]],
            [
                (sds((rows, cols), BF16), row_spec(cols)),
                (sds((reps, PAD, xbc), F32), each(PAD, xbc)),
                (sds((reps, PAD, xbc), F32), each(PAD, xbc)),
                (sds((PAD, xbc), F32), whole(PAD, xbc)),
                (sds((PAD, xbc), F32), whole(PAD, xbc)),
                (sds((PAD, LANES), F32), whole(PAD, LANES)),
                (sds((PAD, LANES), F32), whole(PAD, LANES)),
            ],
            [ext, pltpu.VMEM((length + 2 * PAD, LANES), F32)],
            5.1 * LOW,
            held(*others),
        )
        ran(smalls[m][0])
        from_next = lax.ppermute(
            halo_grad[:, PAD - (KCONV - 1) :].astype(BF16), "seq", [(i, i - 1) for i in range(1, pieces)]
        )
        pgs[m] = pg, tail_grad[:, PAD - (KCONV - 1) :], from_next

    def complete(m):
        pg, last_rows, from_next = pgs[m]
        last_rows = last_rows + later([from_next])[0].astype(F32)
        pgs[m] = lax.dynamic_update_slice(
            pg.reshape(reps, length, cols), last_rows.astype(BF16), (0, length - (KCONV - 1), 0)
        ).reshape(rows, cols)

    normed_grad, pre_parts = [None] * micro, [None] * micro

    def grad_through(m, *others):
        *blocks, pre = call(
            grad_kernel,
            reps,
            [(pgs[m], row_spec(cols)), wide(dgate[m]), (w_mix, whole(*w_mix.shape)), (w_gate, whole(*w_gate.shape))]
            + [(normed_all[m], row_spec(model))],
            [(sds((length, model), BF16), whole(length, model))] * reps + [(sds((PAD, model), F32), whole(PAD, model))],
            [],
            40.0,
            held(*others),
        )
        pre_parts[m] = ran(pre)[0]
        if m == 0:
            normed_grad[m] = list(blocks[:1]) + [swap(blocks[q], "rep", q) for q in (1, 2, 3)]
        else:
            normed_grad[m] = list(blocks[:3]) + list(scatter_far(blocks[3]))

    def over_seq(parts):
        return lax.psum_scatter(parts, "seq", scatter_dimension=0, tiled=True)

    def project_out(m, *others):
        blocks = call(
            branch_kernel,
            reps,
            [wide(gated[m]), (w_out, whole(*w_out.shape))],
            [(sds((length, model), BF16), whole(length, model))] * reps,
            [],
            1.9,
            held(*others),
        )
        ran(blocks[0])
        return list(blocks[:1]) + [swap(blocks[q], "rep", q) for q in (1, 2, 3)]

    normalise(0)
    branch = [project_out(0)]
    normalise(1, backward_chain[0].hop())
    branch.append(project_out(1))
    within_back(0, backward_chain[0].hop(), backward_chain[1].hop())
    within_back(1, backward_chain[0].hop(), backward_chain[1].hop(), *branch[0])
    backward_chain[0].rest()
    back(0, backward_chain[0].back(), backward_chain[1].hop())
    backward_chain[1].rest()
    if strided:
        k_rows, out_share = model // pieces, width // pieces
        both_rows = k_rows + out_share * model // width
        columns = lambda w: pl.BlockSpec((rows, w), lambda i: (0, i))
        (both_part,) = call(
            functools.partial(both_weights_kernel, micro),
            pieces,
            [(v, columns(k_rows)) for v in normed_all]
            + [(v, whole(*v.shape)) for v in dgate]
            + [(v, columns(out_share)) for v in gated]
            + [(v, whole(*v.shape)) for v in cot_all],
            [(sds((pieces, both_rows, width), BF16), each(both_rows, width))],
            [],
            3.2,
            held(backward_chain[1].back()),
        )
        ran(both_part)
        gate_sums = out_sums = over_seq(both_part)[0]
    else:
        gate_sums = over_seq(ran(weight_sum(normed_all, dgate, held(backward_chain[1].back()))))
        out_part = ran(weight_sum(gated, cot_all, held()))
        out_sums = over_seq(
            lax.dynamic_update_slice(jnp.zeros((inner, model), BF16), out_part, (rep * width, 0))
        )
    complete(0)
    back(1)
    grad_through(0)
    complete(1)
    grad_through(1)
    gain_part, skip_part = sum(g[0] for g in gains), sum(v[0] for v in skips)
    cw_part, cb_part, sb_part, dl_part = (sum(v) for v in zip(*smalls))
    skip_heads = skip_part.reshape(heads, HEAD_DIM).sum(axis=1)
    packed = jnp.concatenate(
        [cw_part[:KCONV].reshape(-1), cb_part[0], gain_part, lanes_of(skip_heads), sb_part[0], dl_part[0]]
    )
    branch = [later(b) for b in branch]
    output = jnp.stack([sum(v.astype(F32) for v in b) for b in branch])
    output = jnp.where(valid, token_rows + output, 0.0).astype(BF16)
    mix_part = ran(weight_sum(normed_all, pgs, held(output), 0.1))
    mix_sums = over_seq(after(mix_part, gate_sums, out_sums, *normed_grad[0], *normed_grad[1][3:]))
    normed_grad[0] = later(normed_grad[0])
    gate_near = gather_near(gate_sums)
    normed_grad[1] = scatter_near(*normed_grad[1][:3], *after(tuple(normed_grad[1][3:]), *line, *gate_near[1:]))
    gate_rows = far_parts(gate_near, to_far(gate_near)) if strided else gather_direct(gate_sums)
    out_rows = gate_rows if strided else gather_direct(out_sums)
    pre_part = sum(pre_parts)
    small_sums = SmallSums(jnp.concatenate([packed, pre_part]).reshape(-1, LANES)).rest()

    normed_grad = jnp.stack([sum(v.astype(F32) for v in n) for n in normed_grad])
    xhat = token_rows * inverse
    scaled = normed_grad * pre_gain
    rows_grad = inverse * (scaled - xhat * jnp.mean(scaled * xhat, axis=-1, keepdims=True))
    tokens_grad = jnp.where(valid, cotangent.astype(F32), 0.0) + rows_grad

    rep_scalar = rep.astype(jnp.int32).reshape(1)
    place_in = (rep_scalar, pl.BlockSpec(memory_space=pltpu.SMEM))
    local = jnp.arange(LANES, dtype=jnp.int32)
    a_group = heads // groups
    head_of = (local[None, :] // a_group * reps + jnp.arange(reps, dtype=jnp.int32)[:, None]) * a_group + local % a_group
    head_of = jnp.where(local < heads, head_of, -1)
    where_heads = (head_of[:, :, None] == local[None, None, :]).astype(BF16)
    unit = width // groups
    k_rows = in_weight.shape[0]
    lanes_spec = lambda index: pl.BlockSpec((k_rows, unit), lambda i: (0, index(i)))
    column = lambda first: (
        sds(in_weight.shape[::-1], F32),
        pl.BlockSpec((reps * unit, k_rows), lambda i: (i + first, 0)),
    )
    finished = []
    if strided:
        (out_weight_grad,) = call(
            functools.partial(out_grad_kernel, k_rows),
            reps,
            [place_in] + [(b, whole(*b.shape)) for b in gate_rows[:3] + gate_rows[4:]],
            [(sds(out_weight.shape, F32), pl.BlockSpec((out_share, model), lambda i: (i, 0)))],
            [],
            0.9,
        )
        (gate_done,) = call(
            gate_grad_kernel,
            groups,
            [place_in] + [(b, lanes_spec(lambda i: i)) for b in gate_rows[:4]],
            [column(0)],
            [],
            0.8,
        )
        finished = [out_weight_grad, gate_done]
    mix_rows = (gather_halves if strided else gather_direct)(after(mix_sums, tokens_grad, *finished))
    both_packed = jnp.stack([small_sums, swap(small_sums, "rep", 1)])
    far_packed = swap(both_packed, "rep", 2)
    packed = [both_packed[0], both_packed[1], far_packed[0], far_packed[1]]
    if strided:
        (in_weight_grad,) = call(
            functools.partial(mix_grad_kernel, groups, heads),
            groups + 1,
            [(gate_done, pl.BlockSpec(memory_space=pl.ANY)), place_in]
            + [(b, whole(*b.shape)) for b in mix_rows]
            + [(where_heads, whole(reps, LANES, LANES))],
            [column(groups)],
            [],
            0.5,
            alias={0: 0},
        )
        in_weight_grad = in_weight_grad.T
    else:
        out_weight_grad = sum(v.astype(F32) for v in in_order(out_rows))
        gates, mixes = in_order(gate_rows), in_order(mix_rows)
        in_weight_grad = jnp.concatenate(
            [
                unpick(gates, HEAD_DIM).astype(F32),
                unpick([v[:, :width] for v in mixes], HEAD_DIM).astype(F32),
                sum(v[:, width:xbc].astype(F32) for v in mixes),
                unpick([v[:, xbc : xbc + heads] for v in mixes], 1).astype(F32),
            ],
            axis=1,
        )
    channels = conv_bias.shape[0]
    conv_weight_grad, conv_bias_grad, norm_gain_grad, by_head, pre_gain_grad = call(
        functools.partial(small_kernel, groups, heads, width // groups // LANES),
        1,
        [place_in, (pre_gain[None, :], whole(1, model)), (where_heads, whole(reps, LANES, LANES))]
        + [(v, whole(*v.shape)) for v in packed],
        [
            (sds((KCONV, channels), F32), whole(KCONV, channels)),
            (sds((1, channels), F32), whole(1, channels)),
            (sds((1, inner), F32), whole(1, inner)),
            (sds((PAD, LANES), F32), whole(PAD, LANES)),
            (sds((1, model), F32), whole(1, model)),
        ],
        [],
        3.0,
    )
    conv_bias_grad, norm_gain_grad, pre_gain_grad = conv_bias_grad[0], norm_gain_grad[0], pre_gain_grad[0]
    skip_gain_grad, step_bias_grad, decay_log_grad = by_head[0, :HEADS], by_head[1, :HEADS], by_head[2, :HEADS]

    return (
        output, tokens_grad, pre_gain_grad, in_weight_grad, conv_weight_grad, conv_bias_grad,
        step_bias_grad, decay_log_grad, skip_gain_grad, norm_gain_grad, out_weight_grad,
    )


def solution(mesh):
    rows = P("rep", "seq", None)
    shard = P("seq", None)
    in_specs = (rows, P("rep"), P(), shard, P(), P(), P(), P(), P(), P(), shard, rows)
    out_specs = (rows, rows, P(), shard, P(), P(), P(), P(), P(), P(), shard)
    return jax.shard_map(per_device, mesh=mesh, in_specs=in_specs, out_specs=out_specs, check_vma=False)
```

```python
import functools

import jax
import jax.numpy as jnp
from jax import lax
from jax.experimental import pallas as pl
from jax.experimental.pallas import tpu as pltpu
from jax.sharding import PartitionSpec as P

HEADS = 64
HEAD_DIM = 64
STATE = 128
KCONV = 4
LANES = 128
PAD = 8
COST = 1.0
LOW = 1.0
MARK = 16
EPSILON = 1e-05
NEVER = -1e30
BF16 = jnp.bfloat16
F32 = jnp.float32


def swap(value, axis, bit):
    return lax.ppermute(value, axis, [(i, i ^ bit) for i in range(lax.axis_size(axis))])


def after(value, *others):
    return lax.optimization_barrier((value,) + others)[0]


def gather_near(own):
    return own, swap(own, "rep", 1), swap(own, "rep", 2)


def to_far(near):
    own, one, two = near
    half = own.shape[0] // 2
    return one[:half], two[half:]


def far_parts(near, sent):
    return list(near) + [swap(sent[0], "rep", 2), swap(sent[1], "rep", 1)]


def scatter_far(far):
    half = far.shape[0] // 2
    return swap(far[:half], "rep", 1), swap(far[half:], "rep", 2)


def scatter_near(own, one, two, low, high):
    half = low.shape[0]
    two = jnp.concatenate([(two[:half].astype(F32) + low.astype(F32)).astype(BF16), two[half:]], axis=0)
    one = jnp.concatenate([one[:half], (one[half:].astype(F32) + high.astype(F32)).astype(BF16)], axis=0)
    return [own, swap(one, "rep", 1), swap(two, "rep", 2)], (one, two)


def gather_direct(own):
    return [own] + [swap(own, "rep", j) for j in (1, 2, 3)]


def scatter_direct(parts):
    total = parts[0].astype(F32)
    for j in (1, 2, 3):
        total = total + swap(parts[j], "rep", j).astype(F32)
    return total


def in_order(blocks):
    stack = jnp.stack(blocks)
    place = lax.axis_index("rep")
    return [lax.dynamic_index_in_dim(stack, place ^ q, 0, False) for q in range(len(blocks))]


def sum_seq(value):
    bit = 1
    while bit < lax.axis_size("seq"):
        value = value + swap(value, "seq", bit)
        bit *= 2
    return value


class SmallSums:
    def __init__(self, value):
        self.value, self.bit = value, 1

    def hop(self):
        if self.bit < lax.axis_size("seq"):
            sent = self.value
            self.value = sent + swap(sent, "seq", self.bit)
            self.bit *= 2
        return sent

    def rest(self):
        while self.bit < lax.axis_size("seq"):
            self.hop()
        return self.value


def sum_aligned(blocks):
    total = blocks
    for bit in (1, 2, 3):
        other = swap(blocks, "rep", bit)
        total = total + jnp.stack([other[j ^ bit] for j in range(blocks.shape[0])])
    return total


class Chain:
    def __init__(self, fade, part, message, reverse):
        count = lax.axis_size("seq")
        self.chips = count // 2
        first, lead = (1, 0) if reverse else (0, 1)
        hop = -1 if reverse else 1
        chips = range(self.chips)
        self.fade, self.part = fade, part
        self.homeward = [(2 * c + lead, 2 * c + first) for c in chips]
        onward = [(2 * c + lead, 2 * (c + hop) + lead) for c in chips if 0 <= c + hop < self.chips]
        self.onward = onward[::hop]
        self.leads = lax.axis_index("seq") % 2 == lead
        self.got = lax.ppermute(message, "seq", [(2 * c + first, 2 * c + lead) for c in chips])
        self.total = None
        self.enters = 0.0

    def hop(self):
        if self.total is None:
            got = self.got
            self.mate = got[:, :STATE].astype(F32)
            self.mate_fade = got[:, STATE : STATE + 1].astype(F32) + got[:, STATE + 1 : STATE + 2].astype(F32)
            onto = self.total = (self.part + self.fade * self.mate).astype(BF16)
            self.total_fade = self.fade * self.mate_fade
        else:
            onto = (self.total.astype(F32) + self.total_fade * self.enters.astype(F32)).astype(BF16)
        self.enters = self.enters + lax.ppermute(onto, "seq", [self.onward.pop(0)])
        return onto

    def rest(self):
        while self.onward:
            self.hop()

    def back(self):
        self.handed = lax.ppermute(self.enters, "seq", self.homeward)
        return self.enters

    def end(self):
        own = (self.mate + self.mate_fade * self.enters.astype(F32)).astype(BF16)
        return jnp.where(self.leads, own, self.handed)


def nt(a, b):
    return lax.dot_general(a, b, (((1,), (1,)), ((), ())), preferred_element_type=F32)


def tn(a, b):
    return lax.dot_general(a, b, (((0,), (0,)), ((), ())), preferred_element_type=F32)


def nn(a, b):
    return jnp.dot(a, b, preferred_element_type=F32)


def col(p):
    return slice(p * LANES, (p + 1) * LANES)


def two_parts(value):
    heads = LANES // 4
    high = value.astype(BF16)
    low = (value - high.astype(F32)).astype(BF16).astype(F32)
    lane = lax.broadcasted_iota(jnp.int32, value.shape, 1)
    both = jnp.where(
        lane < heads, high.astype(F32), jnp.where(lane < 2 * heads, pltpu.roll(low, heads, 1), 0.0)
    )
    return both.astype(BF16)


def running(value, reverse):
    rows = value.shape[0]
    place = lax.broadcasted_iota(jnp.int32, value.shape, 0)
    shift = 1
    while shift < rows:
        if reverse:
            moved = jnp.where(place < rows - shift, pltpu.roll(value, rows - shift, 0), 0.0)
        else:
            moved = jnp.where(place >= shift, pltpu.roll(value, shift, 0), 0.0)
        value = value + moved
        shift *= 2
    return value


def head_sums(product, fold):
    high = product.astype(BF16)
    low = (product - high.astype(F32)).astype(BF16)
    return nn(high, fold) + nn(low, fold)


def softplus(v):
    return jnp.maximum(v, 0.0) + jnp.log1p(jnp.exp(-jnp.abs(v)))


def sigmoid(v):
    return 1.0 / (1.0 + jnp.exp(-v))


def split(value):
    high = value.astype(BF16)
    return high, (value - high.astype(F32)).astype(BF16)


def nt_fine(a, b):
    half = a.shape[1] // 2
    return nt(
        jnp.concatenate([a, a[:, :half]], axis=1),
        jnp.concatenate([b[:, :half], b[:, :half], b[:, half:]], axis=1),
    )


def nn_fine(a_high, a_low, b):
    half = b.shape[1] // 2
    return nn(
        jnp.concatenate([a_high, a_low, a_high], axis=1),
        jnp.concatenate([b[:, :half], b[:, :half], b[:, half:]], axis=0),
    )


def twice(value):
    return jnp.concatenate([value, value], axis=0)


def tn_sum(a, b):
    both = tn(a, b)
    half = both.shape[0] // 2
    return both[:half] + both[half:]


def message_of(out, p, part, fade):
    out[0, 0:STATE, col(p)] = part.astype(BF16)
    high, low = split(fade)
    place = lax.broadcasted_iota(jnp.int32, (MARK, LANES), 0)
    rows = jnp.where(place == 0, high.astype(F32), jnp.where(place == 1, low.astype(F32), 0.0))
    out[0, STATE : STATE + MARK, col(p)] = rows.astype(BF16)


def front_kernel(
    proj, halo, cw, cb, sb, dl, spread, x_out, bc_out, sl_out, st_out, msg_out, fade_out, ext
):
    rows = proj.shape[0]
    pairs = x_out.shape[1] // LANES
    raw_step = proj[:, (pairs + 2) * LANES :].astype(F32) + sb[...]
    step = softplus(raw_step)
    log_decay = running(-step * jnp.exp(dl[...]), False)
    last = log_decay[rows - 1 : rows, :]
    sl_out[:, :LANES] = step
    sl_out[:, LANES:] = log_decay
    weight = two_parts(jnp.exp(last - log_decay) * step)
    ending = two_parts(jnp.broadcast_to(jnp.exp(last), (PAD, LANES)))
    ext_rows = pl.ds(PAD, rows)

    def activated(p):
        ext[0:PAD, :] = halo[0, :, col(p)].astype(F32)[MARK - PAD :]
        ext[ext_rows, :] = proj[:, col(p)].astype(F32)
        z = cb[:, col(p)] + cw[0:1, col(p)] * ext[pl.ds(PAD - 3, rows), :]
        for k in range(1, KCONV):
            z = z + cw[k : k + 1, col(p)] * ext[pl.ds(PAD - 3 + k, rows), :]
        return z * sigmoid(z)

    b_rows = jnp.concatenate(split(activated(pairs)), axis=1)
    bc_out[:, : 2 * STATE] = b_rows
    bc_out[:, 2 * STATE :] = jnp.concatenate(split(activated(pairs + 1)), axis=1)
    for p in range(pairs):
        x = activated(p)
        x_out[:, col(p)] = x
        scaled = (x * nn(weight, spread[:, col(p)])).astype(BF16)
        part = tn_sum(b_rows, scaled)
        fade = nn(ending, spread[:, col(p)])[0:1, :]
        st_out[0, :, col(p)] = part
        fade_out[0, :, col(p)] = fade
        message_of(msg_out, p, part, fade)


def inside_kernel(x, bc, sl, spread, y_out):
    rows = x.shape[0]
    half = rows // 2
    pairs = x.shape[1] // LANES
    scores = nt_fine(bc[:, 2 * STATE :], bc[:, : 2 * STATE])
    log_decay = sl[:, LANES:]
    across = log_decay.T
    step = two_parts(sl[:, :LANES])
    t = lax.broadcasted_iota(jnp.int32, (half, half), 0)
    s = lax.broadcasted_iota(jnp.int32, (half, half), 1)
    causal = t >= s
    low_lanes = lax.broadcasted_iota(jnp.int32, (rows, LANES), 1) < HEAD_DIM

    def weights(h, later, earlier, masked):
        gap = log_decay[later, h : h + 1] - across[h : h + 1, earlier]
        gap = jnp.where(causal, gap, NEVER) if masked else gap
        return (scores[later, earlier] * jnp.exp(gap)).astype(BF16)

    first, second = slice(0, half), slice(half, rows)
    for p in range(pairs):
        scaled = (x[:, col(p)] * nn(step, spread[:, col(p)])).astype(BF16)
        outs = []
        for h in (2 * p, 2 * p + 1):
            above = nn(weights(h, first, first, True), scaled[:half])
            below = jnp.concatenate([weights(h, second, first, False), weights(h, second, second, True)], axis=1)
            outs.append(jnp.concatenate([above, nn(below, scaled)], axis=0))
        y_out[:, col(p)] = jnp.where(low_lanes, outs[0], outs[1])


def gate_kernel(y, x, bc, sl, start, gate, grad, gain, skip, spread, y_out, sums_out):
    rows = x.shape[0]
    pairs = x.shape[1] // LANES
    c_rows = bc[:, 2 * STATE :]
    decay = two_parts(jnp.exp(sl[:, LANES:]))
    squares = jnp.zeros((rows, LANES), F32)
    cross = jnp.zeros((rows, LANES), F32)
    for p in range(pairs):
        plain = y[:, col(p)] + nn(decay, spread[:, col(p)]) * nn(c_rows, twice(start[0, :, col(p)]))
        y_out[:, col(p)] = plain
        g = gate[:, col(p)].astype(F32)
        v = (plain + skip[:, col(p)] * x[:, col(p)]) * (g * sigmoid(g))
        squares = squares + v * v
        cross = cross + grad[:, col(p)].astype(F32) * gain[:, col(p)] * v
    lane = lax.broadcasted_iota(jnp.int32, (rows, LANES), 1)
    both = jnp.where(
        lane == 0,
        jnp.sum(squares, axis=1, keepdims=True),
        jnp.where(lane == 1, jnp.sum(cross, axis=1, keepdims=True), 0.0),
    )
    sums_out[0] = both.T[0:PAD, :]


def norm_kernel(
    inner, y, x, bc, sl, gate, grad, gain, skip, fade, sums, spread,
    gated_out, dy_out, dgate_out, dstart_out, msg_out, gain_out, skip_out,
):
    rows = x.shape[0]
    pairs = x.shape[1] // LANES

    @pl.when(pl.program_id(0) == 0)
    def _():
        gain_out[...] = jnp.zeros_like(gain_out)
        skip_out[...] = jnp.zeros_like(skip_out)

    c_rows = bc[:, 2 * STATE :]
    decay = two_parts(jnp.exp(sl[:, LANES:]))
    padded = jnp.concatenate([sums[0], jnp.zeros((LANES - PAD, rows), F32)], axis=0).T
    scale = lax.rsqrt(padded[:, 0:1] / inner + EPSILON)
    back = scale * scale * (padded[:, 1:2] / inner)
    for p in range(pairs):
        g = gate[:, col(p)].astype(F32)
        sg = sigmoid(g)
        silu = g * sg
        xp = x[:, col(p)]
        yp = y[:, col(p)] + skip[:, col(p)] * xp
        v = yp * silu
        gp = grad[:, col(p)].astype(F32)
        normal = v * scale
        gated_out[:, col(p)] = (normal * gain[:, col(p)]).astype(BF16)
        gain_out[0:1, col(p)] += jnp.sum(gp * normal, axis=0, keepdims=True)
        dv = scale * (gp * gain[:, col(p)] - v * back)
        dy = (dv * silu).astype(BF16)
        dy_out[:, col(p)] = dy
        dyf = dy.astype(F32)
        dgate_out[:, col(p)] = (dv * yp * (sg * (1.0 + g * (1.0 - sg)))).astype(BF16)
        skip_out[0:1, col(p)] += jnp.sum(dyf * xp, axis=0, keepdims=True)
        faded = (dyf * nn(decay, spread[:, col(p)])).astype(BF16)
        dstart = tn_sum(c_rows, faded)
        dstart_out[0, :, col(p)] = dstart
        message_of(msg_out, p, dstart, fade[0, :, col(p)])


def inside_back_kernel(x, bc, sl, dy, start, spread, dxs_out, dbc_out):
    rows = x.shape[0]
    half = rows // 2
    pairs = x.shape[1] // LANES
    b_rows = bc[:, : 2 * STATE]
    c_rows = bc[:, 2 * STATE :]
    scores = nt_fine(b_rows, c_rows)
    log_decay = sl[:, LANES:]
    across = log_decay.T
    step = two_parts(sl[:, :LANES])
    decay = two_parts(jnp.exp(log_decay))
    s = lax.broadcasted_iota(jnp.int32, (half, half), 0)
    t = lax.broadcasted_iota(jnp.int32, (half, half), 1)
    causal = t >= s
    low_lanes = lax.broadcasted_iota(jnp.int32, (rows, LANES), 1) < HEAD_DIM

    def falls(h, earlier, later, masked):
        gap = across[h : h + 1, later] - log_decay[earlier, h : h + 1]
        return jnp.exp(jnp.where(causal, gap, NEVER) if masked else gap)

    first, second = slice(0, half), slice(half, rows)
    above_grad = jnp.zeros((half, rows), F32)
    below_grad = jnp.zeros((half, half), F32)
    dc = jnp.zeros((rows, LANES), F32)
    for p in range(pairs):
        scaled = x[:, col(p)] * nn(step, spread[:, col(p)])
        dyp = dy[:, col(p)]
        faded = (dyp.astype(F32) * nn(decay, spread[:, col(p)])).astype(BF16)
        dc = dc + nt(faded, start[0, :, col(p)])
        outs = []
        for h in (2 * p, 2 * p + 1):
            above = jnp.concatenate([falls(h, first, first, True), falls(h, first, second, False)], axis=1)
            below = falls(h, second, second, True)
            outs.append(
                jnp.concatenate(
                    [
                        nn((scores[:half] * above).astype(BF16), dyp),
                        nn((scores[half:, half:] * below).astype(BF16), dyp[half:]),
                    ],
                    axis=0,
                )
            )
            mine = low_lanes if h % 2 == 0 else jnp.logical_not(low_lanes)
            own = jnp.where(mine, scaled, 0.0).astype(BF16)
            above_grad = above_grad + above * nt(own[:half], dyp)
            below_grad = below_grad + below * nt(own[half:], dyp[half:])
        dxs_out[:, col(p)] = jnp.where(low_lanes, outs[0], outs[1])
    below_grad = jnp.concatenate([jnp.zeros((half, half), F32), below_grad], axis=1)
    score_grad = jnp.concatenate([above_grad, below_grad], axis=0)
    dbc_out[:, col(0)] = nn_fine(*split(score_grad), c_rows)
    dbc_out[:, col(1)] = dc + nn_fine(*split(score_grad.T), b_rows)


def back_kernel(
    proj, halo, cw, cb, sb, dl, skip, spread, fold, x, bc, sl, y, dy, dxs, dbc, start, part, fade, later,
    pg_out, halo_out, tail_out, cw_out, cb_out, sb_out, dl_out, ext, dext,
):
    rows = x.shape[0]
    pairs = x.shape[1] // LANES

    @pl.when(pl.program_id(0) == 0)
    def _():
        for out in (cw_out, cb_out, sb_out, dl_out):
            out[...] = jnp.zeros_like(out)

    rate = jnp.exp(dl[...])
    step_f = sl[:, :LANES]
    log_decay = sl[:, LANES:]
    last = log_decay[rows - 1 : rows, :]
    step = two_parts(step_f)
    to_end = two_parts(jnp.exp(last - log_decay))
    b_rows = bc[:, : 2 * STATE]
    dext[0:PAD, :] = jnp.zeros((PAD, LANES), F32)
    dext[pl.ds(PAD + rows, PAD), :] = jnp.zeros((PAD, LANES), F32)

    def through_conv(p, grad):
        ext[0:PAD, :] = halo[0, :, col(p)].astype(F32)[MARK - PAD :]
        ext[pl.ds(PAD, rows), :] = proj[:, col(p)].astype(F32)
        taps = [ext[pl.ds(PAD - 3 + k, rows), :] for k in range(KCONV)]
        z = cb[:, col(p)] + cw[0:1, col(p)] * taps[0]
        for k in range(1, KCONV):
            z = z + cw[k : k + 1, col(p)] * taps[k]
        sg = sigmoid(z)
        dz = grad * (sg * (1.0 + z * (1.0 - sg)))
        cb_out[0:1, col(p)] += jnp.sum(dz, axis=0, keepdims=True)
        for k in range(KCONV):
            cw_out[k : k + 1, col(p)] += jnp.sum(dz * taps[k], axis=0, keepdims=True)
        dext[pl.ds(PAD, rows), :] = dz
        whole = rows + PAD
        dm = cw[KCONV - 1 : KCONV, col(p)] * dext[pl.ds(0, whole), :]
        for k in range(KCONV - 1):
            dm = dm + cw[k : k + 1, col(p)] * dext[pl.ds(KCONV - 1 - k, whole), :]
        halo_out[0, :, col(p)] = dm[0:PAD, :]
        pg_out[:, col(p)] = dm[PAD:, :].astype(BF16)
        tail_out[0, :, col(p)] = dm[rows:, :]

    db = dbc[:, col(0)]
    dstep = jnp.zeros((rows, LANES), F32)
    dlog = jnp.zeros((rows, LANES), F32)
    dlast = jnp.zeros((PAD, LANES), F32)
    for p in range(pairs):
        xp = x[:, col(p)]
        step_p = nn(step, spread[:, col(p)])
        end_p = nn(to_end, spread[:, col(p)])
        later_p = later[0, :, col(p)]
        dyf = dy[:, col(p)].astype(F32)
        scaled = xp * step_p
        dxs_p = dxs[:, col(p)] + end_p * nn(b_rows, twice(later_p))
        db = db + nt((end_p * scaled).astype(BF16), later_p)
        dstep = dstep + head_sums(xp * dxs_p, fold[col(p), :])
        dlog = dlog + head_sums(dyf * y[:, col(p)] - scaled * dxs_p, fold[col(p), :])
        end_state = fade[0, :, col(p)] * start[0, :, col(p)].astype(F32) + part[0, :, col(p)]
        ends = jnp.sum(later_p.astype(F32) * end_state, axis=0, keepdims=True)
        dlast = dlast + head_sums(jnp.broadcast_to(ends, (PAD, LANES)), fold[col(p), :])
        through_conv(p, step_p * dxs_p + skip[:, col(p)] * dyf)
    through_conv(pairs, db)
    through_conv(pairs + 1, dbc[:, col(1)])
    place = lax.broadcasted_iota(jnp.int32, (rows, LANES), 0)
    dlog = dlog + jnp.where(place == rows - 1, dlast[0:1, :], 0.0)
    da = running(dlog, True)
    dstep = dstep - rate * da
    raw_step = proj[:, (pairs + 2) * LANES :].astype(F32) + sb[...]
    draw = dstep * sigmoid(raw_step)
    pg_out[:, (pairs + 2) * LANES :] = draw.astype(BF16)
    sb_out[0:1, :] += jnp.sum(draw, axis=0, keepdims=True)
    dl_out[0:1, :] += -rate * jnp.sum(step_f * da, axis=0, keepdims=True)


def rows_kernel(product, left, right, out):
    out[...] = product(left[...], right[...]).astype(BF16)


def gathered_kernel(product, count, *refs):
    blocks, (right, out, left, *last) = refs[:count], refs[count:]
    for j in range(4):

        @pl.when(pl.program_id(0) == j)
        def _():
            first = 0
            for block in blocks[j : j + 1] if j < 3 else blocks[3:]:
                value = block[...].reshape(block.shape[-2:])
                left[first : first + value.shape[0], :] = value
                first += value.shape[0]

    out[...] = product(left[...], right[...]).astype(BF16)
    for tail in last:
        tail[0] = out[out.shape[0] - tail.shape[1] :, : tail.shape[2]]


def weight_kernel(*refs):
    count = len(refs) // 2
    total = tn(refs[0][...], refs[count][...])
    for m in range(1, count):
        total = total + tn(refs[m][...], refs[count + m][...])
    refs[-1][...] = total.astype(BF16)


def both_weights_kernel(count, *refs):
    normed, gates, gated, cots = (refs[i * count : (i + 1) * count] for i in range(4))
    out = refs[-1]
    gate = sum(tn(a[...], b[...]) for a, b in zip(normed, gates))
    back = sum(tn(a[...], b[...]) for a, b in zip(gated, cots))
    rows, width = gate.shape
    half = back.shape[0]
    out[0, :rows] = gate.astype(BF16)
    for part in range(back.shape[1] // width):
        out[0, rows + part * half : rows + (part + 1) * half] = back[:, part * width : (part + 1) * width].astype(BF16)


def branch_kernel(count, *refs):
    lefts, right, outs = refs[:count], refs[count], refs[count + 1 :]
    values = [nn(left[...], right[...]).astype(BF16) for left in lefts]
    for q, out in enumerate(outs):

        @pl.when(pl.program_id(0) == q)
        def _():
            for m, value in enumerate(values):
                out[m] = value


def grad_kernel(mix, gate, w_mix, w_gate, normed, o0, o1, o2, o3, pre):
    @pl.when(pl.program_id(0) == 0)
    def _():
        pre[...] = jnp.zeros_like(pre)

    grad = nt(mix[...], w_mix[...]) + nt(gate[...], w_gate[...])
    pre[0:1, :] += jnp.sum(grad * normed[...].astype(F32), axis=0, keepdims=True)
    grad = grad.astype(BF16)
    for q, out in enumerate((o0, o1, o2, o3)):

        @pl.when(pl.program_id(0) == q)
        def _():
            out[...] = grad


def ordered(place, blocks):
    odd = (place & 1) == 1
    high = (place & 2) == 2
    a, b, c, d = blocks
    a, b = jnp.where(odd, b, a), jnp.where(odd, a, b)
    c, d = jnp.where(odd, d, c), jnp.where(odd, c, d)
    return [jnp.where(high, c, a), jnp.where(high, d, b), jnp.where(high, a, c), jnp.where(high, b, d)]


def turned(place, blocks, out):
    unit = blocks[0].shape[1]
    for q, block in enumerate(ordered(place[0], [b.astype(F32) for b in blocks])):
        out[q * unit : (q + 1) * unit, :] = block.T


def gate_grad_kernel(place, g0, g1, g2, g3, out):
    turned(place, [g[...] for g in (g0, g1, g2, g3)], out)


def mix_grad_kernel(groups, heads, before, place, m0, m1, m2, low, high, where_heads, out):
    step = pl.program_id(0)
    width = heads * HEAD_DIM
    unit = width // groups

    def columns(at, count):
        whole_blocks = [m[:, pl.ds(at, count)] for m in (m0, m1, m2)]
        return whole_blocks + [jnp.concatenate([low[:, pl.ds(at, count)], high[:, pl.ds(at, count)]], axis=0)]

    @pl.when(step < groups)
    def _():
        turned(place, columns(pl.multiple_of(step * unit, LANES), unit), out)

    @pl.when(step == groups)
    def _():
        both = ordered(place[0], [b.astype(F32) for b in columns(width, 2 * STATE)])
        out[: 2 * STATE, :] = ((both[0] + both[1]) + (both[2] + both[3])).T
        steps = ordered(place[0], columns(width + 2 * STATE, LANES))
        placed = nn(steps[0], where_heads[0])
        for q in range(1, 4):
            placed = placed + nn(steps[q], where_heads[q])
        out[2 * STATE : 2 * STATE + 4 * heads, :] = placed.T[: 4 * heads, :]


def small_kernel(groups, heads, blocks, place, gain, where_heads, *refs):
    ins, (cw_out, cb_out, norm_out, head_out, pre_out) = refs[:4], refs[4:]
    parts = ordered(place[0], [b[...] for b in ins])
    total = (parts[0] + parts[1]) + (parts[2] + parts[3])
    width = groups * blocks

    def spread(out, row, first):
        for g in range(groups):
            for q in range(4):
                for k in range(blocks):
                    at = ((g * 4 + q) * blocks + k) * LANES
                    out[row : row + 1, at : at + LANES] = parts[q][first + g * blocks + k :][:1, :]

    first = 0
    for k in range(KCONV + 1):
        out, row = (cw_out, k) if k < KCONV else (cb_out, 0)
        spread(out, row, first)
        for c in (0, 1):
            at = (4 * width + c) * LANES
            out[row : row + 1, at : at + LANES] = total[first + width + c :][:1, :]
        first += width + 2
    spread(norm_out, 0, first)
    first += width
    placed = 0.0
    for q in range(4):
        rows = jnp.concatenate([parts[q][first : first + 3, :], jnp.zeros((PAD - 3, LANES), F32)], axis=0)
        placed = placed + jnp.dot(
            rows, where_heads[q].astype(F32), preferred_element_type=F32, precision=lax.Precision.HIGHEST
        )
    head_out[...] = placed
    first += 3
    for k in range(pre_out.shape[1] // LANES):
        pre_out[:, col(k)] = total[first + k :][:1, :] / gain[:, col(k)]


def out_grad_kernel(rows, place, b0, b1, b2, b3, out):
    from_rep = place[0] ^ pl.program_id(0)
    count = out.shape[0]
    for j, (block, skip) in enumerate(((b0, rows), (b1, rows), (b2, rows), (b3, 0))):

        @pl.when(from_rep == j)
        def _():
            width = block.shape[1]
            for part in range(out.shape[1] // width):
                first = skip + part * count
                out[:, part * width : (part + 1) * width] = block[first : first + count, :].astype(F32)


def each(*shape):
    return pl.BlockSpec((1,) + shape, lambda i: (i, 0, 0))


def whole(*shape):
    return pl.BlockSpec(shape, lambda i: (0,) * len(shape))


def call(kernel, slots, ins, outs, scratch, us, held=None, alias=None):
    arrays = [a for a, _ in ins]
    if held is not None:
        arrays[0] = held(arrays[0])
    out_shape = [o for o, _ in outs]
    return pl.pallas_call(
        kernel,
        grid=(slots,),
        in_specs=[s for _, s in ins],
        out_specs=[s for _, s in outs],
        out_shape=out_shape,
        scratch_shapes=scratch,
        input_output_aliases=alias or {},
        compiler_params=pltpu.CompilerParams(
            dimension_semantics=("arbitrary",), vmem_limit_bytes=48 * 1024 * 1024
        ),
        cost_estimate=pl.CostEstimate(
            flops=int(us * slots * 1.1e9 * COST), bytes_accessed=int(us * slots * 1e6 * COST), transcendentals=0
        ),
    )(*arrays)


def sds(shape, dtype):
    return jax.ShapeDtypeStruct(shape, dtype)


def rows_times(left, right, product, block, held):
    rows, depth = left.shape
    width = right.shape[1] if product is nn else right.shape[0]
    (out,) = call(
        functools.partial(rows_kernel, product),
        rows // block,
        [(left, pl.BlockSpec((block, depth), lambda i: (i, 0))), (right, whole(*right.shape))],
        [(sds((rows, width), BF16), pl.BlockSpec((block, width), lambda i: (i, 0)))],
        [],
        2.0,
        held,
    )
    return out


def gathered_times(parts, right, product, held, batch=None, last=()):
    rows, depth = parts[0].shape[-2:]
    if batch is None:
        ins = [(v, whole(*v.shape)) for v in parts]
    else:
        ins = [(v, pl.BlockSpec((1, rows, depth), lambda i: (batch, 0, 0))) for v in parts]
    width = right.shape[1] if product is nn else right.shape[0]
    block = lambda w: (sds((4 * rows, w), BF16), pl.BlockSpec((rows, w), lambda i: (i, 0)))
    return call(
        functools.partial(gathered_kernel, product, len(parts)),
        4,
        ins + [(right, whole(*right.shape))],
        [block(width), block(depth)] + [(sds((4, MARK, w), BF16), each(MARK, w)) for w in last],
        [],
        2.7,
        held,
    )


def weight_sum(lefts, rights, held, us=2.0):
    rows, width = lefts[0].shape
    depth = rights[0].shape[1]
    block = min(256, width)
    (out,) = call(
        weight_kernel,
        width // block,
        [(v, pl.BlockSpec((rows, block), lambda i: (0, i))) for v in lefts] + [(v, whole(*v.shape)) for v in rights],
        [(sds((width, depth), BF16), pl.BlockSpec((block, depth), lambda i: (i, 0)))],
        [],
        us,
        held,
    )
    return out


def per_device(
    tokens, lengths, pre_gain, in_weight, conv_weight, conv_bias, step_bias, decay_log, skip_gain,
    norm_gain, out_weight, cotangent,
):
    micro, length, model = tokens.shape
    reps = lax.axis_size("rep")
    pieces = lax.axis_size("seq")
    rep = lax.axis_index("rep")
    inner = norm_gain.shape[0]
    heads = HEADS // reps
    width = heads * HEAD_DIM
    rows = reps * length
    xbc = width + 2 * STATE
    cols = xbc + LANES
    groups = pieces if HEADS % (pieces * reps) == 0 else 1
    strided = groups == pieces

    def pick(v, unit):
        each_group = heads // groups * unit
        v = v.reshape(v.shape[:-1] + (groups, reps, each_group))
        v = lax.dynamic_index_in_dim(v, rep, v.ndim - 2, False)
        return v.reshape(v.shape[:-2] + (groups * each_group,))

    def unpick(parts, unit):
        each_group = heads // groups * unit
        lead = parts[0].shape[:-1]
        v = jnp.stack([q.reshape(lead + (groups, each_group)) for q in parts], axis=-2)
        return v.reshape(lead + (HEADS * unit,))

    def lanes_of(v):
        return jnp.pad(v, [(0, 0)] * (v.ndim - 1) + [(0, LANES - v.shape[-1])])

    def conv_share(v):
        return jnp.concatenate([pick(v[..., :inner], HEAD_DIM), v[..., inner:]], axis=-1)

    position = lax.axis_index("seq") * length + jnp.arange(length, dtype=jnp.int32)
    valid = (position[None, :] < lengths[:, None])[..., None]
    token_rows = tokens.astype(F32)
    inverse = lax.rsqrt(jnp.mean(token_rows * token_rows, axis=-1, keepdims=True) + EPSILON)
    normed = (token_rows * inverse * pre_gain).astype(BF16)
    masked = jnp.where(valid, cotangent, jnp.zeros_like(cotangent))

    w_mix = jnp.concatenate(
        [
            pick(in_weight[:, inner : 2 * inner], HEAD_DIM),
            in_weight[:, 2 * inner : 2 * inner + 2 * STATE],
            lanes_of(pick(in_weight[:, 2 * inner + 2 * STATE :], 1)),
        ],
        axis=1,
    )
    w_gate = pick(in_weight[:, :inner], HEAD_DIM)
    w_mix = lax.all_gather(w_mix, "seq", axis=0, tiled=True)
    w_gate = lax.all_gather(w_gate, "seq", axis=0, tiled=True)
    if strided:
        share = out_weight.shape[0] // reps
        w_out = lax.dynamic_slice_in_dim(out_weight, rep * share, share, 0)
        w_out = lax.all_gather(w_out, "seq", axis=0, tiled=True)
    else:
        w_out = lax.all_gather(out_weight, "seq", axis=0, tiled=True)
        w_out = lax.dynamic_slice_in_dim(w_out, rep * width, width, 0)

    spread_row = jnp.arange(LANES, dtype=jnp.int32)[:, None]
    spread = (
        (spread_row < LANES // 2)
        & (spread_row % (LANES // 4) == jnp.arange(width, dtype=jnp.int32)[None, :] // HEAD_DIM)
    ).astype(BF16)
    fold = (
        jnp.arange(width, dtype=jnp.int32)[:, None] // HEAD_DIM
        == jnp.arange(LANES, dtype=jnp.int32)[None, :]
    ).astype(BF16)

    cw = conv_share(conv_weight)
    cb = conv_share(conv_bias)[None, :]
    sb = lanes_of(pick(step_bias, 1))[None, :]
    dl = lanes_of(pick(decay_log, 1))[None, :]
    skip = jnp.repeat(pick(skip_gain, 1), HEAD_DIM)[None, :]
    gain = pick(norm_gain, HEAD_DIM)[None, :]

    line = []

    def held(*others):
        return lambda value: after(value, *line, *others)

    def later(values):
        return list(after(tuple(values), *line))

    def ran(out):
        line[:] = [out]
        return out

    row_spec = lambda w: pl.BlockSpec((length, w), lambda i: (i, 0))
    small = [
        (cw, whole(KCONV, xbc)),
        (cb, whole(1, xbc)),
        (sb, whole(1, LANES)),
        (dl, whole(1, LANES)),
    ]
    spread_in = (spread, whole(LANES, width))
    gain_in = (gain, whole(1, width))
    skip_in = (skip, whole(1, width))
    wide = lambda v: (v, row_spec(width))
    state = lambda v: (v, each(STATE, width))
    out_wide = lambda t: (sds((rows, width), t), row_spec(width))
    out_state = (sds((reps, STATE, width), F32), each(STATE, width))
    out_message = (sds((reps, STATE + MARK, width), BF16), each(STATE + MARK, width))
    out_gain = (sds((PAD, width), F32), whole(PAD, width))
    ext = pltpu.VMEM((length + PAD, LANES), F32)

    proj_in, halo_in, x_in, bc_in, sl_in, part_in, fade_in, start_in = ([None] * micro for _ in range(8))
    gate_in, grad_in, y_in, sums, inside = ([None] * micro for _ in range(5))
    forward_chain = [None] * micro

    def project(m, *others):
        proj, normed_all[m], tail = gathered_times(normed_parts[m], w_mix, nn, held(*others), last=(xbc,))
        ran(proj)
        halo = lax.ppermute(tail, "seq", [(i, i + 1) for i in range(pieces - 1)])
        proj_in[m], halo_in[m] = (proj, row_spec(cols)), (halo, each(MARK, xbc))

    def front(m, *others):
        x, bc, sl, part, message, fade = call(
            front_kernel,
            reps,
            [proj_in[m], halo_in[m]] + small + [spread_in],
            [
                out_wide(F32),
                (sds((rows, 4 * STATE), BF16), row_spec(4 * STATE)),
                (sds((rows, 2 * LANES), F32), row_spec(2 * LANES)),
                out_state,
                out_message,
                (sds((reps, 1, width), F32), each(1, width)),
            ],
            [ext],
            2.3,
            held(*others),
        )
        ran(fade)
        x_in[m], bc_in[m], sl_in[m] = wide(x), (bc, row_spec(4 * STATE)), (sl, row_spec(2 * LANES))
        part_in[m], fade_in[m] = state(part), (fade, each(1, width))
        forward_chain[m] = Chain(fade, part, message, False)

    def within(m, *others):
        (inside[m],) = call(
            inside_kernel, reps, [x_in[m], bc_in[m], sl_in[m], spread_in], [out_wide(F32)], [], 2.2, held(*others)
        )
        ran(inside[m])

    def gate_of(m, *others):
        gate_in[m] = wide(ran(rows_times(normed_all[m], w_gate, nn, length, held(*others))))

    def grad_of(m, *others):
        grad, cot_all[m] = gathered_times(cot_blocks, w_out, nt, held(*others), m)
        grad_in[m] = wide(ran(grad))

    def gating(m, *others):
        start_in[m] = state(forward_chain[m].end())
        y, partial = call(
            gate_kernel,
            reps,
            [wide(inside[m]), x_in[m], bc_in[m], sl_in[m], start_in[m], gate_in[m], grad_in[m], gain_in, skip_in, spread_in],
            [out_wide(F32), (sds((reps, PAD, length), F32), each(PAD, length))],
            [],
            2.8,
            held(*others),
        )
        ran(partial)
        y_in[m] = wide(y)
        partial = sum_aligned(partial[:, :2])
        sums[m] = (jnp.pad(partial, ((0, 0), (0, PAD - 2), (0, 0))), each(PAD, length))

    near = [gather_near(normed[0])]
    far = [to_far(near[0])]
    normed_all, cot_all = [None] * micro, [None] * micro
    normed_parts = [far_parts(near[0], far[0])]
    near.append(gather_near(after(normed[1], *normed_parts[0][3:])))
    project(0, near[1][0])
    near[1] = later(near[1])
    far.append(to_far(near[1]))
    normed_parts.append(far_parts(near[1], far[1]))
    front(0, *far[1])
    cot_blocks = gather_direct(after(masked, *line))
    project(1, cot_blocks[0])
    front(1, forward_chain[0].hop())
    gate_of(0)
    within(0, forward_chain[0].hop(), forward_chain[1].hop())
    gate_of(1)
    within(1, forward_chain[0].hop(), forward_chain[1].hop())
    cot_blocks = later(cot_blocks)
    grad_of(0)
    forward_chain[0].rest()
    grad_of(1, forward_chain[0].back(), forward_chain[1].hop())
    forward_chain[1].rest()
    gating(0, forward_chain[1].back())
    gating(1)

    gated, dy_in, dgate, later_in, gains, skips = ([None] * micro for _ in range(6))
    backward_chain = [None] * micro

    def normalise(m, *others):
        gated[m], dy, dgate[m], dstart, message, gains[m], skips[m] = call(
            functools.partial(norm_kernel, float(inner)),
            reps,
            [y_in[m], x_in[m], bc_in[m], sl_in[m], gate_in[m], grad_in[m], gain_in, skip_in, fade_in[m], sums[m], spread_in],
            [out_wide(BF16), out_wide(BF16), out_wide(BF16), out_state, out_message, out_gain, out_gain],
            [],
            3.1,
            held(*others),
        )
        ran(gains[m])
        dy_in[m] = wide(dy)
        backward_chain[m] = Chain(fade_in[m][0], dstart, message, True)

    inner_back = [None] * micro

    def within_back(m, *others):
        inner_back[m] = call(
            inside_back_kernel,
            reps,
            [x_in[m], bc_in[m], sl_in[m], dy_in[m], start_in[m], spread_in],
            [out_wide(F32), (sds((rows, 2 * STATE), F32), row_spec(2 * STATE))],
            [],
            3.6 * LOW,
            held(*others),
        )
        ran(inner_back[m][1])

    pgs, smalls = [None] * micro, [None] * micro

    def back(m, *others):
        dxs, dbc = inner_back[m]
        later_in[m] = state(backward_chain[m].end())
        pg, halo_grad, tail_grad, *smalls[m] = call(
            back_kernel,
            reps,
            [proj_in[m], halo_in[m]] + small
            + [skip_in, spread_in, (fold, whole(width, LANES)), x_in[m], bc_in[m], sl_in[m], y_in[m], dy_in[m]]
            + [wide(dxs), (dbc, row_spec(2 * STATE)), start_in[m], part_in[m], fade_in[m], later_in[m]],
            [
                (sds((rows, cols), BF16), row_spec(cols)),
                (sds((reps, PAD, xbc), F32), each(PAD, xbc)),
                (sds((reps, PAD, xbc), F32), each(PAD, xbc)),
                (sds((PAD, xbc), F32), whole(PAD, xbc)),
                (sds((PAD, xbc), F32), whole(PAD, xbc)),
                (sds((PAD, LANES), F32), whole(PAD, LANES)),
                (sds((PAD, LANES), F32), whole(PAD, LANES)),
            ],
            [ext, pltpu.VMEM((length + 2 * PAD, LANES), F32)],
            5.1 * LOW,
            held(*others),
        )
        ran(smalls[m][0])
        from_next = lax.ppermute(
            halo_grad[:, PAD - (KCONV - 1) :].astype(BF16), "seq", [(i, i - 1) for i in range(1, pieces)]
        )
        pgs[m] = pg, tail_grad[:, PAD - (KCONV - 1) :], from_next

    def complete(m):
        pg, last_rows, from_next = pgs[m]
        last_rows = last_rows + later([from_next])[0].astype(F32)
        pgs[m] = lax.dynamic_update_slice(
            pg.reshape(reps, length, cols), last_rows.astype(BF16), (0, length - (KCONV - 1), 0)
        ).reshape(rows, cols)

    normed_grad, pre_parts = [None] * micro, [None] * micro

    def grad_through(m, *others):
        *blocks, pre = call(
            grad_kernel,
            reps,
            [(pgs[m], row_spec(cols)), wide(dgate[m]), (w_mix, whole(*w_mix.shape)), (w_gate, whole(*w_gate.shape))]
            + [(normed_all[m], row_spec(model))],
            [(sds((length, model), BF16), whole(length, model))] * reps + [(sds((PAD, model), F32), whole(PAD, model))],
            [],
            80.0 if m == 0 else 0.1,
            held(*others),
        )
        pre_parts[m] = ran(pre)[0]
        if m == 0:
            normed_grad[m] = list(blocks[:1]) + [swap(blocks[q], "rep", q) for q in (1, 2, 3)]
        else:
            normed_grad[m] = list(blocks[:3]) + list(scatter_far(blocks[3]))

    def over_seq(parts):
        return lax.psum_scatter(parts, "seq", scatter_dimension=0, tiled=True)

    normalise(0)
    normalise(1)
    branch = call(
        functools.partial(branch_kernel, micro),
        reps,
        [wide(v) for v in gated] + [(w_out, whole(*w_out.shape))],
        [(sds((micro, length, model), BF16), whole(micro, length, model))] * reps,
        [],
        3.8,
        held(backward_chain[0].hop()),
    )
    ran(branch[0])
    branch = [branch[0]] + [swap(branch[q], "rep", q) for q in (1, 2, 3)]
    within_back(0, backward_chain[0].hop(), backward_chain[1].hop())
    within_back(1, backward_chain[0].hop(), backward_chain[1].hop())
    backward_chain[0].rest()
    back(0, backward_chain[0].back(), backward_chain[1].hop())
    backward_chain[1].rest()
    if strided:
        k_rows, out_share = model // pieces, width // pieces
        both_rows = k_rows + out_share * model // width
        columns = lambda w: pl.BlockSpec((rows, w), lambda i: (0, i))
        (both_part,) = call(
            functools.partial(both_weights_kernel, micro),
            pieces,
            [(v, columns(k_rows)) for v in normed_all]
            + [(v, whole(*v.shape)) for v in dgate]
            + [(v, columns(out_share)) for v in gated]
            + [(v, whole(*v.shape)) for v in cot_all],
            [(sds((pieces, both_rows, width), BF16), each(both_rows, width))],
            [],
            3.2,
            held(backward_chain[1].back()),
        )
        ran(both_part)
        gate_sums = out_sums = over_seq(both_part)[0]
    else:
        gate_sums = over_seq(ran(weight_sum(normed_all, dgate, held(backward_chain[1].back()))))
        out_part = ran(weight_sum(gated, cot_all, held()))
        out_sums = over_seq(
            lax.dynamic_update_slice(jnp.zeros((inner, model), BF16), out_part, (rep * width, 0))
        )
    complete(0)
    back(1, *branch[1:])
    grad_through(0)
    complete(1)
    mix_part = ran(weight_sum(normed_all, pgs, held(), 0.1))
    grad_through(1)
    gain_part, skip_part = sum(g[0] for g in gains), sum(v[0] for v in skips)
    cw_part, cb_part, sb_part, dl_part = (sum(v) for v in zip(*smalls))
    skip_heads = skip_part.reshape(heads, HEAD_DIM).sum(axis=1)
    packed = jnp.concatenate(
        [cw_part[:KCONV].reshape(-1), cb_part[0], gain_part, lanes_of(skip_heads), sb_part[0], dl_part[0]]
    )
    mix_sums = over_seq(after(mix_part, gate_sums, out_sums, *line, *normed_grad[0]))
    output = sum(v.astype(F32) for v in later(branch))
    output = jnp.where(valid, token_rows + output, 0.0).astype(BF16)
    normed_grad[0] = later(normed_grad[0])
    gate_near = gather_near(gate_sums)
    far_sums = after(tuple(normed_grad[1][3:]), *line)
    normed_grad[1], sent = scatter_near(*normed_grad[1][:3], *after(far_sums, *gate_near[1:], output))
    gate_rows = far_parts(gate_near, to_far(gate_near)) if strided else gather_direct(gate_sums)
    out_rows = gate_rows if strided else gather_direct(out_sums)
    pre_part = sum(pre_parts)
    small_sums = jnp.concatenate([packed, pre_part]).reshape(-1, LANES)
    small_sums = SmallSums(after(small_sums, *far_sums))
    small_sums.hop()
    small_sums.value = after(small_sums.value, *sent)
    small_sums = small_sums.rest()

    normed_grad = jnp.stack([sum(v.astype(F32) for v in n) for n in normed_grad])
    xhat = token_rows * inverse
    scaled = normed_grad * pre_gain
    rows_grad = inverse * (scaled - xhat * jnp.mean(scaled * xhat, axis=-1, keepdims=True))
    tokens_grad = jnp.where(valid, cotangent.astype(F32), 0.0) + rows_grad


    ready = tuple(gate_rows) + (small_sums, tokens_grad)
    if strided:
        mix_near = gather_near(after(mix_sums, *ready))
        mix_far = to_far(mix_near)
        mix_rows = far_parts(mix_near, mix_far)
    else:
        mix_rows = gather_direct(mix_sums)
        mix_far = mix_rows[1:]
    gate_rows = list(after(tuple(gate_rows), *mix_far))
    out_rows = gate_rows if strided else out_rows
    small_sums = after(small_sums, *mix_far)
    both_packed = jnp.stack([small_sums, swap(small_sums, "rep", 1)])
    far_packed = swap(both_packed, "rep", 2)
    packed = [both_packed[0], both_packed[1], far_packed[0], far_packed[1]]

    rep_scalar = rep.astype(jnp.int32).reshape(1)
    place_in = (rep_scalar, pl.BlockSpec(memory_space=pltpu.SMEM))
    local = jnp.arange(LANES, dtype=jnp.int32)
    a_group = heads // groups
    head_of = (local[None, :] // a_group * reps + jnp.arange(reps, dtype=jnp.int32)[:, None]) * a_group + local % a_group
    head_of = jnp.where(local < heads, head_of, -1)
    where_heads = (head_of[:, :, None] == local[None, None, :]).astype(BF16)
    unit = width // groups
    k_rows = in_weight.shape[0]
    lanes_spec = lambda index: pl.BlockSpec((k_rows, unit), lambda i: (0, index(i)))
    column = lambda first: (
        sds(in_weight.shape[::-1], F32),
        pl.BlockSpec((reps * unit, k_rows), lambda i: (i + first, 0)),
    )
    if strided:
        (out_weight_grad,) = call(
            functools.partial(out_grad_kernel, k_rows),
            reps,
            [place_in] + [(b, whole(*b.shape)) for b in gate_rows[:3] + gate_rows[4:]],
            [(sds(out_weight.shape, F32), pl.BlockSpec((out_share, model), lambda i: (i, 0)))],
            [],
            0.9,
        )
        (gate_done,) = call(
            gate_grad_kernel,
            groups,
            [place_in] + [(b, lanes_spec(lambda i: i)) for b in gate_rows[:4]],
            [column(0)],
            [],
            0.8,
        )
    if strided:
        (in_weight_grad,) = call(
            functools.partial(mix_grad_kernel, groups, heads),
            groups + 1,
            [(gate_done, pl.BlockSpec(memory_space=pl.ANY)), place_in]
            + [(b, whole(*b.shape)) for b in mix_rows]
            + [(where_heads, whole(reps, LANES, LANES))],
            [column(groups)],
            [],
            0.5,
            alias={0: 0},
        )
        in_weight_grad = in_weight_grad.T
    else:
        out_weight_grad = sum(v.astype(F32) for v in in_order(out_rows))
        gates, mixes = in_order(gate_rows), in_order(mix_rows)
        in_weight_grad = jnp.concatenate(
            [
                unpick(gates, HEAD_DIM).astype(F32),
                unpick([v[:, :width] for v in mixes], HEAD_DIM).astype(F32),
                sum(v[:, width:xbc].astype(F32) for v in mixes),
                unpick([v[:, xbc : xbc + heads] for v in mixes], 1).astype(F32),
            ],
            axis=1,
        )
    channels = conv_bias.shape[0]
    conv_weight_grad, conv_bias_grad, norm_gain_grad, by_head, pre_gain_grad = call(
        functools.partial(small_kernel, groups, heads, width // groups // LANES),
        1,
        [place_in, (pre_gain[None, :], whole(1, model)), (where_heads, whole(reps, LANES, LANES))]
        + [(v, whole(*v.shape)) for v in packed],
        [
            (sds((KCONV, channels), F32), whole(KCONV, channels)),
            (sds((1, channels), F32), whole(1, channels)),
            (sds((1, inner), F32), whole(1, inner)),
            (sds((PAD, LANES), F32), whole(PAD, LANES)),
            (sds((1, model), F32), whole(1, model)),
        ],
        [],
        3.0,
    )
    conv_bias_grad, norm_gain_grad, pre_gain_grad = conv_bias_grad[0], norm_gain_grad[0], pre_gain_grad[0]
    skip_gain_grad, step_bias_grad, decay_log_grad = by_head[0, :HEADS], by_head[1, :HEADS], by_head[2, :HEADS]

    return (
        output, tokens_grad, pre_gain_grad, in_weight_grad, conv_weight_grad, conv_bias_grad,
        step_bias_grad, decay_log_grad, skip_gain_grad, norm_gain_grad, out_weight_grad,
    )


def solution(mesh):
    rows = P("rep", "seq", None)
    shard = P("seq", None)
    in_specs = (rows, P("rep"), P(), shard, P(), P(), P(), P(), P(), P(), shard, rows)
    out_specs = (rows, rows, P(), shard, P(), P(), P(), P(), P(), P(), shard)
    return jax.shard_map(per_device, mesh=mesh, in_specs=in_specs, out_specs=out_specs, check_vma=False)
```

```python
import functools

import jax
import jax.numpy as jnp
from jax import lax
from jax.experimental import pallas as pl
from jax.experimental.pallas import tpu as pltpu
from jax.sharding import PartitionSpec as P

HEADS = 64
HEAD_DIM = 64
STATE = 128
KCONV = 4
LANES = 128
PAD = 8
COST = 1.0
LOW = 1.0
MARK = 16
EPSILON = 1e-05
NEVER = -1e30
BF16 = jnp.bfloat16
F32 = jnp.float32


def swap(value, axis, bit):
    return lax.ppermute(value, axis, [(i, i ^ bit) for i in range(lax.axis_size(axis))])


def after(value, *others):
    return lax.optimization_barrier((value,) + others)[0]


def gather_near(own):
    return own, swap(own, "rep", 1), swap(own, "rep", 2)


def to_far(near):
    own, one, two = near
    half = own.shape[0] // 2
    return one[:half], two[half:]


def far_parts(near, sent):
    return list(near) + [swap(sent[0], "rep", 2), swap(sent[1], "rep", 1)]


def scatter_far(far):
    half = far.shape[0] // 2
    return swap(far[:half], "rep", 1), swap(far[half:], "rep", 2)


def scatter_near(own, one, two, low, high):
    half = low.shape[0]
    two = jnp.concatenate([(two[:half].astype(F32) + low.astype(F32)).astype(BF16), two[half:]], axis=0)
    one = jnp.concatenate([one[:half], (one[half:].astype(F32) + high.astype(F32)).astype(BF16)], axis=0)
    return [own, swap(one, "rep", 1), swap(two, "rep", 2)], (one, two)


def gather_direct(own):
    return [own] + [swap(own, "rep", j) for j in (1, 2, 3)]


def scatter_direct(parts):
    total = parts[0].astype(F32)
    for j in (1, 2, 3):
        total = total + swap(parts[j], "rep", j).astype(F32)
    return total


def in_order(blocks):
    stack = jnp.stack(blocks)
    place = lax.axis_index("rep")
    return [lax.dynamic_index_in_dim(stack, place ^ q, 0, False) for q in range(len(blocks))]


def sum_seq(value):
    bit = 1
    while bit < lax.axis_size("seq"):
        value = value + swap(value, "seq", bit)
        bit *= 2
    return value


class SmallSums:
    def __init__(self, value):
        self.value, self.bit = value, 1

    def hop(self):
        if self.bit < lax.axis_size("seq"):
            sent = self.value
            self.value = sent + swap(sent, "seq", self.bit)
            self.bit *= 2
        return sent

    def rest(self):
        while self.bit < lax.axis_size("seq"):
            self.hop()
        return self.value


def sum_aligned(blocks):
    total = blocks
    for bit in (1, 2, 3):
        other = swap(blocks, "rep", bit)
        total = total + jnp.stack([other[j ^ bit] for j in range(blocks.shape[0])])
    return total


class Chain:
    def __init__(self, fade, part, message, reverse):
        count = lax.axis_size("seq")
        self.chips = count // 2
        first, lead = (1, 0) if reverse else (0, 1)
        hop = -1 if reverse else 1
        chips = range(self.chips)
        self.fade, self.part = fade, part
        self.homeward = [(2 * c + lead, 2 * c + first) for c in chips]
        onward = [(2 * c + lead, 2 * (c + hop) + lead) for c in chips if 0 <= c + hop < self.chips]
        self.onward = onward[::hop]
        self.leads = lax.axis_index("seq") % 2 == lead
        self.got = lax.ppermute(message, "seq", [(2 * c + first, 2 * c + lead) for c in chips])
        self.total = None
        self.enters = 0.0

    def hop(self):
        if self.total is None:
            got = self.got
            self.mate = got[:, :STATE].astype(F32)
            self.mate_fade = got[:, STATE : STATE + 1].astype(F32) + got[:, STATE + 1 : STATE + 2].astype(F32)
            onto = self.total = (self.part + self.fade * self.mate).astype(BF16)
            self.total_fade = self.fade * self.mate_fade
        else:
            onto = (self.total.astype(F32) + self.total_fade * self.enters.astype(F32)).astype(BF16)
        self.enters = self.enters + lax.ppermute(onto, "seq", [self.onward.pop(0)])
        return onto

    def rest(self):
        while self.onward:
            self.hop()

    def back(self):
        self.handed = lax.ppermute(self.enters, "seq", self.homeward)
        return self.enters

    def end(self):
        own = (self.mate + self.mate_fade * self.enters.astype(F32)).astype(BF16)
        return jnp.where(self.leads, own, self.handed)


def nt(a, b):
    return lax.dot_general(a, b, (((1,), (1,)), ((), ())), preferred_element_type=F32)


def tn(a, b):
    return lax.dot_general(a, b, (((0,), (0,)), ((), ())), preferred_element_type=F32)


def nn(a, b):
    return jnp.dot(a, b, preferred_element_type=F32)


def col(p):
    return slice(p * LANES, (p + 1) * LANES)


def two_parts(value):
    heads = LANES // 4
    high = value.astype(BF16)
    low = (value - high.astype(F32)).astype(BF16).astype(F32)
    lane = lax.broadcasted_iota(jnp.int32, value.shape, 1)
    both = jnp.where(
        lane < heads, high.astype(F32), jnp.where(lane < 2 * heads, pltpu.roll(low, heads, 1), 0.0)
    )
    return both.astype(BF16)


def running(value, reverse):
    rows = value.shape[0]
    place = lax.broadcasted_iota(jnp.int32, value.shape, 0)
    shift = 1
    while shift < rows:
        if reverse:
            moved = jnp.where(place < rows - shift, pltpu.roll(value, rows - shift, 0), 0.0)
        else:
            moved = jnp.where(place >= shift, pltpu.roll(value, shift, 0), 0.0)
        value = value + moved
        shift *= 2
    return value


def head_sums(product, fold):
    high = product.astype(BF16)
    low = (product - high.astype(F32)).astype(BF16)
    return nn(high, fold) + nn(low, fold)


def softplus(v):
    return jnp.maximum(v, 0.0) + jnp.log1p(jnp.exp(-jnp.abs(v)))


def sigmoid(v):
    return 1.0 / (1.0 + jnp.exp(-v))


def split(value):
    high = value.astype(BF16)
    return high, (value - high.astype(F32)).astype(BF16)


def nt_fine(a, b):
    half = a.shape[1] // 2
    return nt(
        jnp.concatenate([a, a[:, :half]], axis=1),
        jnp.concatenate([b[:, :half], b[:, :half], b[:, half:]], axis=1),
    )


def nn_fine(a_high, a_low, b):
    half = b.shape[1] // 2
    return nn(
        jnp.concatenate([a_high, a_low, a_high], axis=1),
        jnp.concatenate([b[:, :half], b[:, :half], b[:, half:]], axis=0),
    )


def twice(value):
    return jnp.concatenate([value, value], axis=0)


def tn_sum(a, b):
    both = tn(a, b)
    half = both.shape[0] // 2
    return both[:half] + both[half:]


def message_of(out, p, part, fade):
    out[0, 0:STATE, col(p)] = part.astype(BF16)
    high, low = split(fade)
    place = lax.broadcasted_iota(jnp.int32, (MARK, LANES), 0)
    rows = jnp.where(place == 0, high.astype(F32), jnp.where(place == 1, low.astype(F32), 0.0))
    out[0, STATE : STATE + MARK, col(p)] = rows.astype(BF16)


def front_kernel(
    proj, halo, cw, cb, sb, dl, spread, x_out, bc_out, sl_out, st_out, msg_out, fade_out, ext
):
    rows = proj.shape[0]
    pairs = x_out.shape[1] // LANES
    raw_step = proj[:, (pairs + 2) * LANES :].astype(F32) + sb[...]
    step = softplus(raw_step)
    log_decay = running(-step * jnp.exp(dl[...]), False)
    last = log_decay[rows - 1 : rows, :]
    sl_out[:, :LANES] = step
    sl_out[:, LANES:] = log_decay
    weight = two_parts(jnp.exp(last - log_decay) * step)
    ending = two_parts(jnp.broadcast_to(jnp.exp(last), (PAD, LANES)))
    ext_rows = pl.ds(PAD, rows)

    def activated(p):
        ext[0:PAD, :] = halo[0, :, col(p)].astype(F32)[MARK - PAD :]
        ext[ext_rows, :] = proj[:, col(p)].astype(F32)
        z = cb[:, col(p)] + cw[0:1, col(p)] * ext[pl.ds(PAD - 3, rows), :]
        for k in range(1, KCONV):
            z = z + cw[k : k + 1, col(p)] * ext[pl.ds(PAD - 3 + k, rows), :]
        return z * sigmoid(z)

    b_rows = jnp.concatenate(split(activated(pairs)), axis=1)
    bc_out[:, : 2 * STATE] = b_rows
    bc_out[:, 2 * STATE :] = jnp.concatenate(split(activated(pairs + 1)), axis=1)
    for p in range(pairs):
        x = activated(p)
        x_out[:, col(p)] = x
        scaled = (x * nn(weight, spread[:, col(p)])).astype(BF16)
        part = tn_sum(b_rows, scaled)
        fade = nn(ending, spread[:, col(p)])[0:1, :]
        st_out[0, :, col(p)] = part
        fade_out[0, :, col(p)] = fade
        message_of(msg_out, p, part, fade)


def inside_kernel(x, bc, sl, spread, y_out):
    rows = x.shape[0]
    half = rows // 2
    pairs = x.shape[1] // LANES
    scores = nt_fine(bc[:, 2 * STATE :], bc[:, : 2 * STATE])
    log_decay = sl[:, LANES:]
    across = log_decay.T
    step = two_parts(sl[:, :LANES])
    t = lax.broadcasted_iota(jnp.int32, (half, half), 0)
    s = lax.broadcasted_iota(jnp.int32, (half, half), 1)
    causal = t >= s
    low_lanes = lax.broadcasted_iota(jnp.int32, (rows, LANES), 1) < HEAD_DIM

    def weights(h, later, earlier, masked):
        gap = log_decay[later, h : h + 1] - across[h : h + 1, earlier]
        gap = jnp.where(causal, gap, NEVER) if masked else gap
        return (scores[later, earlier] * jnp.exp(gap)).astype(BF16)

    first, second = slice(0, half), slice(half, rows)
    for p in range(pairs):
        scaled = (x[:, col(p)] * nn(step, spread[:, col(p)])).astype(BF16)
        outs = []
        for h in (2 * p, 2 * p + 1):
            above = nn(weights(h, first, first, True), scaled[:half])
            below = jnp.concatenate([weights(h, second, first, False), weights(h, second, second, True)], axis=1)
            outs.append(jnp.concatenate([above, nn(below, scaled)], axis=0))
        y_out[:, col(p)] = jnp.where(low_lanes, outs[0], outs[1])


def gate_kernel(y, x, bc, sl, start, gate, grad, gain, skip, spread, y_out, sums_out):
    rows = x.shape[0]
    pairs = x.shape[1] // LANES
    c_rows = bc[:, 2 * STATE :]
    decay = two_parts(jnp.exp(sl[:, LANES:]))
    squares = jnp.zeros((rows, LANES), F32)
    cross = jnp.zeros((rows, LANES), F32)
    for p in range(pairs):
        plain = y[:, col(p)] + nn(decay, spread[:, col(p)]) * nn(c_rows, twice(start[0, :, col(p)]))
        y_out[:, col(p)] = plain
        g = gate[:, col(p)].astype(F32)
        v = (plain + skip[:, col(p)] * x[:, col(p)]) * (g * sigmoid(g))
        squares = squares + v * v
        cross = cross + grad[:, col(p)].astype(F32) * gain[:, col(p)] * v
    lane = lax.broadcasted_iota(jnp.int32, (rows, LANES), 1)
    both = jnp.where(
        lane == 0,
        jnp.sum(squares, axis=1, keepdims=True),
        jnp.where(lane == 1, jnp.sum(cross, axis=1, keepdims=True), 0.0),
    )
    sums_out[0] = both.T[0:PAD, :]


def norm_kernel(
    inner, y, x, bc, sl, gate, grad, gain, skip, fade, sums, spread,
    gated_out, dy_out, dgate_out, dstart_out, msg_out, gain_out, skip_out,
):
    rows = x.shape[0]
    pairs = x.shape[1] // LANES

    @pl.when(pl.program_id(0) == 0)
    def _():
        gain_out[...] = jnp.zeros_like(gain_out)
        skip_out[...] = jnp.zeros_like(skip_out)

    c_rows = bc[:, 2 * STATE :]
    decay = two_parts(jnp.exp(sl[:, LANES:]))
    padded = jnp.concatenate([sums[0], jnp.zeros((LANES - PAD, rows), F32)], axis=0).T
    scale = lax.rsqrt(padded[:, 0:1] / inner + EPSILON)
    back = scale * scale * (padded[:, 1:2] / inner)
    for p in range(pairs):
        g = gate[:, col(p)].astype(F32)
        sg = sigmoid(g)
        silu = g * sg
        xp = x[:, col(p)]
        yp = y[:, col(p)] + skip[:, col(p)] * xp
        v = yp * silu
        gp = grad[:, col(p)].astype(F32)
        normal = v * scale
        gated_out[:, col(p)] = (normal * gain[:, col(p)]).astype(BF16)
        gain_out[0:1, col(p)] += jnp.sum(gp * normal, axis=0, keepdims=True)
        dv = scale * (gp * gain[:, col(p)] - v * back)
        dy = (dv * silu).astype(BF16)
        dy_out[:, col(p)] = dy
        dyf = dy.astype(F32)
        dgate_out[:, col(p)] = (dv * yp * (sg * (1.0 + g * (1.0 - sg)))).astype(BF16)
        skip_out[0:1, col(p)] += jnp.sum(dyf * xp, axis=0, keepdims=True)
        faded = (dyf * nn(decay, spread[:, col(p)])).astype(BF16)
        dstart = tn_sum(c_rows, faded)
        dstart_out[0, :, col(p)] = dstart
        message_of(msg_out, p, dstart, fade[0, :, col(p)])


def inside_back_kernel(x, bc, sl, dy, start, spread, dxs_out, dbc_out):
    rows = x.shape[0]
    half = rows // 2
    pairs = x.shape[1] // LANES
    b_rows = bc[:, : 2 * STATE]
    c_rows = bc[:, 2 * STATE :]
    scores = nt_fine(b_rows, c_rows)
    log_decay = sl[:, LANES:]
    across = log_decay.T
    step = two_parts(sl[:, :LANES])
    decay = two_parts(jnp.exp(log_decay))
    s = lax.broadcasted_iota(jnp.int32, (half, half), 0)
    t = lax.broadcasted_iota(jnp.int32, (half, half), 1)
    causal = t >= s
    low_lanes = lax.broadcasted_iota(jnp.int32, (rows, LANES), 1) < HEAD_DIM

    def falls(h, earlier, later, masked):
        gap = across[h : h + 1, later] - log_decay[earlier, h : h + 1]
        return jnp.exp(jnp.where(causal, gap, NEVER) if masked else gap)

    first, second = slice(0, half), slice(half, rows)
    above_grad = jnp.zeros((half, rows), F32)
    below_grad = jnp.zeros((half, half), F32)
    dc = jnp.zeros((rows, LANES), F32)
    for p in range(pairs):
        scaled = x[:, col(p)] * nn(step, spread[:, col(p)])
        dyp = dy[:, col(p)]
        faded = (dyp.astype(F32) * nn(decay, spread[:, col(p)])).astype(BF16)
        dc = dc + nt(faded, start[0, :, col(p)])
        outs = []
        for h in (2 * p, 2 * p + 1):
            above = jnp.concatenate([falls(h, first, first, True), falls(h, first, second, False)], axis=1)
            below = falls(h, second, second, True)
            outs.append(
                jnp.concatenate(
                    [
                        nn((scores[:half] * above).astype(BF16), dyp),
                        nn((scores[half:, half:] * below).astype(BF16), dyp[half:]),
                    ],
                    axis=0,
                )
            )
            mine = low_lanes if h % 2 == 0 else jnp.logical_not(low_lanes)
            own = jnp.where(mine, scaled, 0.0).astype(BF16)
            above_grad = above_grad + above * nt(own[:half], dyp)
            below_grad = below_grad + below * nt(own[half:], dyp[half:])
        dxs_out[:, col(p)] = jnp.where(low_lanes, outs[0], outs[1])
    below_grad = jnp.concatenate([jnp.zeros((half, half), F32), below_grad], axis=1)
    score_grad = jnp.concatenate([above_grad, below_grad], axis=0)
    dbc_out[:, col(0)] = nn_fine(*split(score_grad), c_rows)
    dbc_out[:, col(1)] = dc + nn_fine(*split(score_grad.T), b_rows)


def back_kernel(
    proj, halo, cw, cb, sb, dl, skip, spread, fold, x, bc, sl, y, dy, dxs, dbc, start, part, fade, later,
    pg_out, halo_out, tail_out, cw_out, cb_out, sb_out, dl_out, ext, dext,
):
    rows = x.shape[0]
    pairs = x.shape[1] // LANES

    @pl.when(pl.program_id(0) == 0)
    def _():
        for out in (cw_out, cb_out, sb_out, dl_out):
            out[...] = jnp.zeros_like(out)

    rate = jnp.exp(dl[...])
    step_f = sl[:, :LANES]
    log_decay = sl[:, LANES:]
    last = log_decay[rows - 1 : rows, :]
    step = two_parts(step_f)
    to_end = two_parts(jnp.exp(last - log_decay))
    b_rows = bc[:, : 2 * STATE]
    dext[0:PAD, :] = jnp.zeros((PAD, LANES), F32)
    dext[pl.ds(PAD + rows, PAD), :] = jnp.zeros((PAD, LANES), F32)

    def through_conv(p, grad):
        ext[0:PAD, :] = halo[0, :, col(p)].astype(F32)[MARK - PAD :]
        ext[pl.ds(PAD, rows), :] = proj[:, col(p)].astype(F32)
        taps = [ext[pl.ds(PAD - 3 + k, rows), :] for k in range(KCONV)]
        z = cb[:, col(p)] + cw[0:1, col(p)] * taps[0]
        for k in range(1, KCONV):
            z = z + cw[k : k + 1, col(p)] * taps[k]
        sg = sigmoid(z)
        dz = grad * (sg * (1.0 + z * (1.0 - sg)))
        cb_out[0:1, col(p)] += jnp.sum(dz, axis=0, keepdims=True)
        for k in range(KCONV):
            cw_out[k : k + 1, col(p)] += jnp.sum(dz * taps[k], axis=0, keepdims=True)
        dext[pl.ds(PAD, rows), :] = dz
        whole = rows + PAD
        dm = cw[KCONV - 1 : KCONV, col(p)] * dext[pl.ds(0, whole), :]
        for k in range(KCONV - 1):
            dm = dm + cw[k : k + 1, col(p)] * dext[pl.ds(KCONV - 1 - k, whole), :]
        halo_out[0, :, col(p)] = dm[0:PAD, :]
        pg_out[:, col(p)] = dm[PAD:, :].astype(BF16)
        tail_out[0, :, col(p)] = dm[rows:, :]

    db = dbc[:, col(0)]
    dstep = jnp.zeros((rows, LANES), F32)
    dlog = jnp.zeros((rows, LANES), F32)
    dlast = jnp.zeros((PAD, LANES), F32)
    for p in range(pairs):
        xp = x[:, col(p)]
        step_p = nn(step, spread[:, col(p)])
        end_p = nn(to_end, spread[:, col(p)])
        later_p = later[0, :, col(p)]
        dyf = dy[:, col(p)].astype(F32)
        scaled = xp * step_p
        dxs_p = dxs[:, col(p)] + end_p * nn(b_rows, twice(later_p))
        db = db + nt((end_p * scaled).astype(BF16), later_p)
        dstep = dstep + head_sums(xp * dxs_p, fold[col(p), :])
        dlog = dlog + head_sums(dyf * y[:, col(p)] - scaled * dxs_p, fold[col(p), :])
        end_state = fade[0, :, col(p)] * start[0, :, col(p)].astype(F32) + part[0, :, col(p)]
        ends = jnp.sum(later_p.astype(F32) * end_state, axis=0, keepdims=True)
        dlast = dlast + head_sums(jnp.broadcast_to(ends, (PAD, LANES)), fold[col(p), :])
        through_conv(p, step_p * dxs_p + skip[:, col(p)] * dyf)
    through_conv(pairs, db)
    through_conv(pairs + 1, dbc[:, col(1)])
    place = lax.broadcasted_iota(jnp.int32, (rows, LANES), 0)
    dlog = dlog + jnp.where(place == rows - 1, dlast[0:1, :], 0.0)
    da = running(dlog, True)
    dstep = dstep - rate * da
    raw_step = proj[:, (pairs + 2) * LANES :].astype(F32) + sb[...]
    draw = dstep * sigmoid(raw_step)
    pg_out[:, (pairs + 2) * LANES :] = draw.astype(BF16)
    sb_out[0:1, :] += jnp.sum(draw, axis=0, keepdims=True)
    dl_out[0:1, :] += -rate * jnp.sum(step_f * da, axis=0, keepdims=True)


def rows_kernel(product, left, right, out):
    out[...] = product(left[...], right[...]).astype(BF16)


def gathered_kernel(product, count, *refs):
    blocks, (right, out, left, *last) = refs[:count], refs[count:]
    for j in range(4):

        @pl.when(pl.program_id(0) == j)
        def _():
            first = 0
            for block in blocks[j : j + 1] if j < 3 else blocks[3:]:
                value = block[...].reshape(block.shape[-2:])
                left[first : first + value.shape[0], :] = value
                first += value.shape[0]

    out[...] = product(left[...], right[...]).astype(BF16)
    for tail in last:
        tail[0] = out[out.shape[0] - tail.shape[1] :, : tail.shape[2]]


def weight_kernel(*refs):
    count = len(refs) // 2
    total = tn(refs[0][...], refs[count][...])
    for m in range(1, count):
        total = total + tn(refs[m][...], refs[count + m][...])
    refs[-1][...] = total.astype(BF16)


def both_weights_kernel(count, *refs):
    normed, gates, gated, cots = (refs[i * count : (i + 1) * count] for i in range(4))
    out = refs[-1]
    gate = sum(tn(a[...], b[...]) for a, b in zip(normed, gates))
    back = sum(tn(a[...], b[...]) for a, b in zip(gated, cots))
    rows, width = gate.shape
    half = back.shape[0]
    out[0, :rows] = gate.astype(BF16)
    for part in range(back.shape[1] // width):
        out[0, rows + part * half : rows + (part + 1) * half] = back[:, part * width : (part + 1) * width].astype(BF16)


def branch_kernel(count, *refs):
    lefts, right, outs = refs[:count], refs[count], refs[count + 1 :]
    values = [nn(left[...], right[...]).astype(BF16) for left in lefts]
    for q, out in enumerate(outs):

        @pl.when(pl.program_id(0) == q)
        def _():
            for m, value in enumerate(values):
                out[m] = value


def grad_kernel(mix, gate, w_mix, w_gate, normed, o0, o1, o2, o3, pre):
    @pl.when(pl.program_id(0) == 0)
    def _():
        pre[...] = jnp.zeros_like(pre)

    grad = nt(mix[...], w_mix[...]) + nt(gate[...], w_gate[...])
    pre[0:1, :] += jnp.sum(grad * normed[...].astype(F32), axis=0, keepdims=True)
    grad = grad.astype(BF16)
    for q, out in enumerate((o0, o1, o2, o3)):

        @pl.when(pl.program_id(0) == q)
        def _():
            out[...] = grad


def ordered(place, blocks):
    odd = (place & 1) == 1
    high = (place & 2) == 2
    a, b, c, d = blocks
    a, b = jnp.where(odd, b, a), jnp.where(odd, a, b)
    c, d = jnp.where(odd, d, c), jnp.where(odd, c, d)
    return [jnp.where(high, c, a), jnp.where(high, d, b), jnp.where(high, a, c), jnp.where(high, b, d)]


def turned(place, blocks, out):
    unit = blocks[0].shape[1]
    for q, block in enumerate(ordered(place[0], [b.astype(F32) for b in blocks])):
        out[q * unit : (q + 1) * unit, :] = block.T


def gate_grad_kernel(place, g0, g1, g2, g3, out):
    turned(place, [g[...] for g in (g0, g1, g2, g3)], out)


def mix_grad_kernel(groups, heads, before, place, m0, m1, m2, low, high, where_heads, out):
    step = pl.program_id(0)
    width = heads * HEAD_DIM
    unit = width // groups

    def columns(at, count):
        whole_blocks = [m[:, pl.ds(at, count)] for m in (m0, m1, m2)]
        return whole_blocks + [jnp.concatenate([low[:, pl.ds(at, count)], high[:, pl.ds(at, count)]], axis=0)]

    @pl.when(step < groups)
    def _():
        turned(place, columns(pl.multiple_of(step * unit, LANES), unit), out)

    @pl.when(step == groups)
    def _():
        both = ordered(place[0], [b.astype(F32) for b in columns(width, 2 * STATE)])
        out[: 2 * STATE, :] = ((both[0] + both[1]) + (both[2] + both[3])).T
        steps = ordered(place[0], columns(width + 2 * STATE, LANES))
        placed = nn(steps[0], where_heads[0])
        for q in range(1, 4):
            placed = placed + nn(steps[q], where_heads[q])
        out[2 * STATE : 2 * STATE + 4 * heads, :] = placed.T[: 4 * heads, :]


def small_kernel(groups, heads, blocks, place, gain, where_heads, *refs):
    ins, (cw_out, cb_out, norm_out, head_out, pre_out) = refs[:4], refs[4:]
    parts = ordered(place[0], [b[...] for b in ins])
    total = (parts[0] + parts[1]) + (parts[2] + parts[3])
    width = groups * blocks

    def spread(out, row, first):
        for g in range(groups):
            for q in range(4):
                for k in range(blocks):
                    at = ((g * 4 + q) * blocks + k) * LANES
                    out[row : row + 1, at : at + LANES] = parts[q][first + g * blocks + k :][:1, :]

    first = 0
    for k in range(KCONV + 1):
        out, row = (cw_out, k) if k < KCONV else (cb_out, 0)
        spread(out, row, first)
        for c in (0, 1):
            at = (4 * width + c) * LANES
            out[row : row + 1, at : at + LANES] = total[first + width + c :][:1, :]
        first += width + 2
    spread(norm_out, 0, first)
    first += width
    placed = 0.0
    for q in range(4):
        rows = jnp.concatenate([parts[q][first : first + 3, :], jnp.zeros((PAD - 3, LANES), F32)], axis=0)
        placed = placed + jnp.dot(
            rows, where_heads[q].astype(F32), preferred_element_type=F32, precision=lax.Precision.HIGHEST
        )
    head_out[...] = placed
    first += 3
    for k in range(pre_out.shape[1] // LANES):
        pre_out[:, col(k)] = total[first + k :][:1, :] / gain[:, col(k)]


def out_grad_kernel(rows, place, b0, b1, b2, b3, out):
    from_rep = place[0] ^ pl.program_id(0)
    count = out.shape[0]
    for j, (block, skip) in enumerate(((b0, rows), (b1, rows), (b2, rows), (b3, 0))):

        @pl.when(from_rep == j)
        def _():
            width = block.shape[1]
            for part in range(out.shape[1] // width):
                first = skip + part * count
                out[:, part * width : (part + 1) * width] = block[first : first + count, :].astype(F32)


def each(*shape):
    return pl.BlockSpec((1,) + shape, lambda i: (i, 0, 0))


def whole(*shape):
    return pl.BlockSpec(shape, lambda i: (0,) * len(shape))


def call(kernel, slots, ins, outs, scratch, us, held=None, alias=None):
    arrays = [a for a, _ in ins]
    if held is not None:
        arrays[0] = held(arrays[0])
    out_shape = [o for o, _ in outs]
    return pl.pallas_call(
        kernel,
        grid=(slots,),
        in_specs=[s for _, s in ins],
        out_specs=[s for _, s in outs],
        out_shape=out_shape,
        scratch_shapes=scratch,
        input_output_aliases=alias or {},
        compiler_params=pltpu.CompilerParams(
            dimension_semantics=("arbitrary",), vmem_limit_bytes=48 * 1024 * 1024
        ),
        cost_estimate=pl.CostEstimate(
            flops=int(us * slots * 1.1e9 * COST), bytes_accessed=int(us * slots * 1e6 * COST), transcendentals=0
        ),
    )(*arrays)


def sds(shape, dtype):
    return jax.ShapeDtypeStruct(shape, dtype)


def rows_times(left, right, product, block, held):
    rows, depth = left.shape
    width = right.shape[1] if product is nn else right.shape[0]
    (out,) = call(
        functools.partial(rows_kernel, product),
        rows // block,
        [(left, pl.BlockSpec((block, depth), lambda i: (i, 0))), (right, whole(*right.shape))],
        [(sds((rows, width), BF16), pl.BlockSpec((block, width), lambda i: (i, 0)))],
        [],
        2.0,
        held,
    )
    return out


def gathered_times(parts, right, product, held, batch=None, last=()):
    rows, depth = parts[0].shape[-2:]
    if batch is None:
        ins = [(v, whole(*v.shape)) for v in parts]
    else:
        ins = [(v, pl.BlockSpec((1, rows, depth), lambda i: (batch, 0, 0))) for v in parts]
    width = right.shape[1] if product is nn else right.shape[0]
    block = lambda w: (sds((4 * rows, w), BF16), pl.BlockSpec((rows, w), lambda i: (i, 0)))
    return call(
        functools.partial(gathered_kernel, product, len(parts)),
        4,
        ins + [(right, whole(*right.shape))],
        [block(width), block(depth)] + [(sds((4, MARK, w), BF16), each(MARK, w)) for w in last],
        [],
        2.7,
        held,
    )


def weight_sum(lefts, rights, held, us=2.0):
    rows, width = lefts[0].shape
    depth = rights[0].shape[1]
    block = min(256, width)
    (out,) = call(
        weight_kernel,
        width // block,
        [(v, pl.BlockSpec((rows, block), lambda i: (0, i))) for v in lefts] + [(v, whole(*v.shape)) for v in rights],
        [(sds((width, depth), BF16), pl.BlockSpec((block, depth), lambda i: (i, 0)))],
        [],
        us,
        held,
    )
    return out


def per_device(
    tokens, lengths, pre_gain, in_weight, conv_weight, conv_bias, step_bias, decay_log, skip_gain,
    norm_gain, out_weight, cotangent,
):
    micro, length, model = tokens.shape
    reps = lax.axis_size("rep")
    pieces = lax.axis_size("seq")
    rep = lax.axis_index("rep")
    inner = norm_gain.shape[0]
    heads = HEADS // reps
    width = heads * HEAD_DIM
    rows = reps * length
    xbc = width + 2 * STATE
    cols = xbc + LANES
    groups = pieces if HEADS % (pieces * reps) == 0 else 1
    strided = groups == pieces

    def pick(v, unit):
        each_group = heads // groups * unit
        v = v.reshape(v.shape[:-1] + (groups, reps, each_group))
        v = lax.dynamic_index_in_dim(v, rep, v.ndim - 2, False)
        return v.reshape(v.shape[:-2] + (groups * each_group,))

    def unpick(parts, unit):
        each_group = heads // groups * unit
        lead = parts[0].shape[:-1]
        v = jnp.stack([q.reshape(lead + (groups, each_group)) for q in parts], axis=-2)
        return v.reshape(lead + (HEADS * unit,))

    def lanes_of(v):
        return jnp.pad(v, [(0, 0)] * (v.ndim - 1) + [(0, LANES - v.shape[-1])])

    def conv_share(v):
        return jnp.concatenate([pick(v[..., :inner], HEAD_DIM), v[..., inner:]], axis=-1)

    position = lax.axis_index("seq") * length + jnp.arange(length, dtype=jnp.int32)
    valid = (position[None, :] < lengths[:, None])[..., None]
    token_rows = tokens.astype(F32)
    inverse = lax.rsqrt(jnp.mean(token_rows * token_rows, axis=-1, keepdims=True) + EPSILON)
    normed = (token_rows * inverse * pre_gain).astype(BF16)
    masked = jnp.where(valid, cotangent, jnp.zeros_like(cotangent))

    w_mix = jnp.concatenate(
        [
            pick(in_weight[:, inner : 2 * inner], HEAD_DIM),
            in_weight[:, 2 * inner : 2 * inner + 2 * STATE],
            lanes_of(pick(in_weight[:, 2 * inner + 2 * STATE :], 1)),
        ],
        axis=1,
    )
    w_gate = pick(in_weight[:, :inner], HEAD_DIM)
    w_mix = lax.all_gather(w_mix, "seq", axis=0, tiled=True)
    w_gate = lax.all_gather(w_gate, "seq", axis=0, tiled=True)
    if strided:
        share = out_weight.shape[0] // reps
        w_out = lax.dynamic_slice_in_dim(out_weight, rep * share, share, 0)
        w_out = lax.all_gather(w_out, "seq", axis=0, tiled=True)
    else:
        w_out = lax.all_gather(out_weight, "seq", axis=0, tiled=True)
        w_out = lax.dynamic_slice_in_dim(w_out, rep * width, width, 0)

    spread_row = jnp.arange(LANES, dtype=jnp.int32)[:, None]
    spread = (
        (spread_row < LANES // 2)
        & (spread_row % (LANES // 4) == jnp.arange(width, dtype=jnp.int32)[None, :] // HEAD_DIM)
    ).astype(BF16)
    fold = (
        jnp.arange(width, dtype=jnp.int32)[:, None] // HEAD_DIM
        == jnp.arange(LANES, dtype=jnp.int32)[None, :]
    ).astype(BF16)

    cw = conv_share(conv_weight)
    cb = conv_share(conv_bias)[None, :]
    sb = lanes_of(pick(step_bias, 1))[None, :]
    dl = lanes_of(pick(decay_log, 1))[None, :]
    skip = jnp.repeat(pick(skip_gain, 1), HEAD_DIM)[None, :]
    gain = pick(norm_gain, HEAD_DIM)[None, :]

    line = []

    def held(*others):
        return lambda value: after(value, *line, *others)

    def later(values):
        return list(after(tuple(values), *line))

    def ran(out):
        line[:] = [out]
        return out

    row_spec = lambda w: pl.BlockSpec((length, w), lambda i: (i, 0))
    small = [
        (cw, whole(KCONV, xbc)),
        (cb, whole(1, xbc)),
        (sb, whole(1, LANES)),
        (dl, whole(1, LANES)),
    ]
    spread_in = (spread, whole(LANES, width))
    gain_in = (gain, whole(1, width))
    skip_in = (skip, whole(1, width))
    wide = lambda v: (v, row_spec(width))
    state = lambda v: (v, each(STATE, width))
    out_wide = lambda t: (sds((rows, width), t), row_spec(width))
    out_state = (sds((reps, STATE, width), F32), each(STATE, width))
    out_message = (sds((reps, STATE + MARK, width), BF16), each(STATE + MARK, width))
    out_gain = (sds((PAD, width), F32), whole(PAD, width))
    ext = pltpu.VMEM((length + PAD, LANES), F32)

    proj_in, halo_in, x_in, bc_in, sl_in, part_in, fade_in, start_in = ([None] * micro for _ in range(8))
    gate_in, grad_in, y_in, sums, inside = ([None] * micro for _ in range(5))
    forward_chain = [None] * micro

    def project(m, *others):
        proj, normed_all[m], tail = gathered_times(normed_parts[m], w_mix, nn, held(*others), last=(xbc,))
        ran(proj)
        halo = lax.ppermute(tail, "seq", [(i, i + 1) for i in range(pieces - 1)])
        proj_in[m], halo_in[m] = (proj, row_spec(cols)), (halo, each(MARK, xbc))

    def front(m, *others):
        x, bc, sl, part, message, fade = call(
            front_kernel,
            reps,
            [proj_in[m], halo_in[m]] + small + [spread_in],
            [
                out_wide(F32),
                (sds((rows, 4 * STATE), BF16), row_spec(4 * STATE)),
                (sds((rows, 2 * LANES), F32), row_spec(2 * LANES)),
                out_state,
                out_message,
                (sds((reps, 1, width), F32), each(1, width)),
            ],
            [ext],
            2.3,
            held(*others),
        )
        ran(fade)
        x_in[m], bc_in[m], sl_in[m] = wide(x), (bc, row_spec(4 * STATE)), (sl, row_spec(2 * LANES))
        part_in[m], fade_in[m] = state(part), (fade, each(1, width))
        forward_chain[m] = Chain(fade, part, message, False)

    def within(m, *others):
        (inside[m],) = call(
            inside_kernel, reps, [x_in[m], bc_in[m], sl_in[m], spread_in], [out_wide(F32)], [], 2.2, held(*others)
        )
        ran(inside[m])

    def gate_of(m, *others):
        gate_in[m] = wide(ran(rows_times(normed_all[m], w_gate, nn, length, held(*others))))

    def grad_of(m, *others):
        grad, cot_all[m] = gathered_times(cot_blocks, w_out, nt, held(*others), m)
        grad_in[m] = wide(ran(grad))

    def gating(m, *others):
        start_in[m] = state(forward_chain[m].end())
        y, partial = call(
            gate_kernel,
            reps,
            [wide(inside[m]), x_in[m], bc_in[m], sl_in[m], start_in[m], gate_in[m], grad_in[m], gain_in, skip_in, spread_in],
            [out_wide(F32), (sds((reps, PAD, length), F32), each(PAD, length))],
            [],
            2.8,
            held(*others),
        )
        ran(partial)
        y_in[m] = wide(y)
        partial = sum_aligned(partial[:, :2])
        sums[m] = (jnp.pad(partial, ((0, 0), (0, PAD - 2), (0, 0))), each(PAD, length))

    near = [gather_near(normed[0])]
    far = [to_far(near[0])]
    normed_all, cot_all = [None] * micro, [None] * micro
    normed_parts = [far_parts(near[0], far[0])]
    near.append(gather_near(after(normed[1], *normed_parts[0][3:])))
    project(0, near[1][0])
    near[1] = later(near[1])
    far.append(to_far(near[1]))
    normed_parts.append(far_parts(near[1], far[1]))
    front(0, *far[1])
    cot_blocks = gather_direct(after(masked, *line))
    project(1, cot_blocks[0])
    front(1, forward_chain[0].hop())
    gate_of(0)
    within(0, forward_chain[0].hop(), forward_chain[1].hop())
    gate_of(1)
    within(1, forward_chain[0].hop(), forward_chain[1].hop())
    cot_blocks = later(cot_blocks)
    grad_of(0)
    forward_chain[0].rest()
    grad_of(1, forward_chain[0].back(), forward_chain[1].hop())
    forward_chain[1].rest()
    gating(0, forward_chain[1].back())
    gating(1)

    gated, dy_in, dgate, later_in, gains, skips = ([None] * micro for _ in range(6))
    backward_chain = [None] * micro

    def normalise(m, *others):
        gated[m], dy, dgate[m], dstart, message, gains[m], skips[m] = call(
            functools.partial(norm_kernel, float(inner)),
            reps,
            [y_in[m], x_in[m], bc_in[m], sl_in[m], gate_in[m], grad_in[m], gain_in, skip_in, fade_in[m], sums[m], spread_in],
            [out_wide(BF16), out_wide(BF16), out_wide(BF16), out_state, out_message, out_gain, out_gain],
            [],
            3.1,
            held(*others),
        )
        ran(gains[m])
        dy_in[m] = wide(dy)
        backward_chain[m] = Chain(fade_in[m][0], dstart, message, True)

    inner_back = [None] * micro

    def within_back(m, *others):
        inner_back[m] = call(
            inside_back_kernel,
            reps,
            [x_in[m], bc_in[m], sl_in[m], dy_in[m], start_in[m], spread_in],
            [out_wide(F32), (sds((rows, 2 * STATE), F32), row_spec(2 * STATE))],
            [],
            3.6 * LOW,
            held(*others),
        )
        ran(inner_back[m][1])

    pgs, smalls = [None] * micro, [None] * micro

    def back(m, *others):
        dxs, dbc = inner_back[m]
        later_in[m] = state(backward_chain[m].end())
        pg, halo_grad, tail_grad, *smalls[m] = call(
            back_kernel,
            reps,
            [proj_in[m], halo_in[m]] + small
            + [skip_in, spread_in, (fold, whole(width, LANES)), x_in[m], bc_in[m], sl_in[m], y_in[m], dy_in[m]]
            + [wide(dxs), (dbc, row_spec(2 * STATE)), start_in[m], part_in[m], fade_in[m], later_in[m]],
            [
                (sds((rows, cols), BF16), row_spec(cols)),
                (sds((reps, PAD, xbc), F32), each(PAD, xbc)),
                (sds((reps, PAD, xbc), F32), each(PAD, xbc)),
                (sds((PAD, xbc), F32), whole(PAD, xbc)),
                (sds((PAD, xbc), F32), whole(PAD, xbc)),
                (sds((PAD, LANES), F32), whole(PAD, LANES)),
                (sds((PAD, LANES), F32), whole(PAD, LANES)),
            ],
            [ext, pltpu.VMEM((length + 2 * PAD, LANES), F32)],
            5.1 * LOW,
            held(*others),
        )
        ran(smalls[m][0])
        from_next = lax.ppermute(
            halo_grad[:, PAD - (KCONV - 1) :].astype(BF16), "seq", [(i, i - 1) for i in range(1, pieces)]
        )
        pgs[m] = pg, tail_grad[:, PAD - (KCONV - 1) :], from_next

    def complete(m):
        pg, last_rows, from_next = pgs[m]
        last_rows = last_rows + later([from_next])[0].astype(F32)
        pgs[m] = lax.dynamic_update_slice(
            pg.reshape(reps, length, cols), last_rows.astype(BF16), (0, length - (KCONV - 1), 0)
        ).reshape(rows, cols)

    normed_grad, pre_parts = [None] * micro, [None] * micro

    def grad_through(m, *others):
        *blocks, pre = call(
            grad_kernel,
            reps,
            [(pgs[m], row_spec(cols)), wide(dgate[m]), (w_mix, whole(*w_mix.shape)), (w_gate, whole(*w_gate.shape))]
            + [(normed_all[m], row_spec(model))],
            [(sds((length, model), BF16), whole(length, model))] * reps + [(sds((PAD, model), F32), whole(PAD, model))],
            [],
            80.0 if m == 0 else 0.1,
            held(*others),
        )
        pre_parts[m] = ran(pre)[0]
        if m == 0:
            normed_grad[m] = list(blocks[:1]) + [swap(blocks[q], "rep", q) for q in (1, 2, 3)]
        else:
            normed_grad[m] = list(blocks[:3]) + list(scatter_far(after(blocks[3], *gate_near[1:])))

    def over_seq(parts):
        return lax.psum_scatter(parts, "seq", scatter_dimension=0, tiled=True)

    normalise(0)
    normalise(1)
    branch = call(
        functools.partial(branch_kernel, micro),
        reps,
        [wide(v) for v in gated] + [(w_out, whole(*w_out.shape))],
        [(sds((micro, length, model), BF16), whole(micro, length, model))] * reps,
        [],
        3.8,
        held(backward_chain[0].hop()),
    )
    ran(branch[0])
    branch = [branch[0]] + [swap(branch[q], "rep", q) for q in (1, 2, 3)]
    within_back(0, backward_chain[0].hop(), backward_chain[1].hop())
    onward = backward_chain[0].hop(), backward_chain[1].hop()
    backward_chain[0].rest()
    if strided:
        k_rows, out_share = model // pieces, width // pieces
        both_rows = k_rows + out_share * model // width
        columns = lambda w: pl.BlockSpec((rows, w), lambda i: (0, i))
        (both_part,) = call(
            functools.partial(both_weights_kernel, micro),
            pieces,
            [(v, columns(k_rows)) for v in normed_all]
            + [(v, whole(*v.shape)) for v in dgate]
            + [(v, columns(out_share)) for v in gated]
            + [(v, whole(*v.shape)) for v in cot_all],
            [(sds((pieces, both_rows, width), BF16), each(both_rows, width))],
            [],
            3.2,
            held(*onward),
        )
        ran(both_part)
        gate_sums = out_sums = over_seq(both_part)[0]
    else:
        gate_sums = over_seq(ran(weight_sum(normed_all, dgate, held(*onward))))
        out_part = ran(weight_sum(gated, cot_all, held()))
        out_sums = over_seq(
            lax.dynamic_update_slice(jnp.zeros((inner, model), BF16), out_part, (rep * width, 0))
        )
    back(0, backward_chain[0].back())
    within_back(1, backward_chain[1].hop())
    backward_chain[1].rest()
    complete(0)
    grad_through(0, backward_chain[1].back())
    back(1, *branch[1:])
    complete(1)
    mix_part = ran(weight_sum(normed_all, pgs, held(), 0.1))
    gate_near = gather_near(after(gate_sums, *normed_grad[0]))
    grad_through(1)
    gain_part, skip_part = sum(g[0] for g in gains), sum(v[0] for v in skips)
    cw_part, cb_part, sb_part, dl_part = (sum(v) for v in zip(*smalls))
    skip_heads = skip_part.reshape(heads, HEAD_DIM).sum(axis=1)
    packed = jnp.concatenate(
        [cw_part[:KCONV].reshape(-1), cb_part[0], gain_part, lanes_of(skip_heads), sb_part[0], dl_part[0]]
    )
    mix_sums = over_seq(after(mix_part, gate_sums, out_sums, *normed_grad[0]))
    output = sum(v.astype(F32) for v in later(branch))
    output = jnp.where(valid, token_rows + output, 0.0).astype(BF16)
    normed_grad[0] = later(normed_grad[0])
    far_sums = after(tuple(normed_grad[1][3:]), *line)
    normed_grad[1], sent = scatter_near(*normed_grad[1][:3], *after(far_sums, output))
    gate_rows = far_parts(gate_near, to_far(gate_near)) if strided else gather_direct(gate_sums)
    out_rows = gate_rows if strided else gather_direct(out_sums)
    pre_part = sum(pre_parts)
    small_sums = jnp.concatenate([packed, pre_part]).reshape(-1, LANES)
    small_sums = SmallSums(after(small_sums, *far_sums))
    small_sums.hop()
    small_sums.value = after(small_sums.value, *sent)
    small_sums = small_sums.rest()

    normed_grad = jnp.stack([sum(v.astype(F32) for v in n) for n in normed_grad])
    xhat = token_rows * inverse
    scaled = normed_grad * pre_gain
    rows_grad = inverse * (scaled - xhat * jnp.mean(scaled * xhat, axis=-1, keepdims=True))
    tokens_grad = jnp.where(valid, cotangent.astype(F32), 0.0) + rows_grad


    ready = tuple(gate_rows) + (small_sums, tokens_grad)
    if strided:
        mix_near = gather_near(after(mix_sums, *ready))
        mix_far = to_far(mix_near)
        mix_rows = far_parts(mix_near, mix_far)
    else:
        mix_rows = gather_direct(mix_sums)
        mix_far = mix_rows[1:]
    gate_rows = list(after(tuple(gate_rows), *mix_far))
    out_rows = gate_rows if strided else out_rows
    small_sums = after(small_sums, *mix_far)
    both_packed = jnp.stack([small_sums, swap(small_sums, "rep", 1)])
    far_packed = swap(both_packed, "rep", 2)
    packed = [both_packed[0], both_packed[1], far_packed[0], far_packed[1]]

    rep_scalar = rep.astype(jnp.int32).reshape(1)
    place_in = (rep_scalar, pl.BlockSpec(memory_space=pltpu.SMEM))
    local = jnp.arange(LANES, dtype=jnp.int32)
    a_group = heads // groups
    head_of = (local[None, :] // a_group * reps + jnp.arange(reps, dtype=jnp.int32)[:, None]) * a_group + local % a_group
    head_of = jnp.where(local < heads, head_of, -1)
    where_heads = (head_of[:, :, None] == local[None, None, :]).astype(BF16)
    unit = width // groups
    k_rows = in_weight.shape[0]
    lanes_spec = lambda index: pl.BlockSpec((k_rows, unit), lambda i: (0, index(i)))
    column = lambda first: (
        sds(in_weight.shape[::-1], F32),
        pl.BlockSpec((reps * unit, k_rows), lambda i: (i + first, 0)),
    )
    if strided:
        (out_weight_grad,) = call(
            functools.partial(out_grad_kernel, k_rows),
            reps,
            [place_in] + [(b, whole(*b.shape)) for b in gate_rows[:3] + gate_rows[4:]],
            [(sds(out_weight.shape, F32), pl.BlockSpec((out_share, model), lambda i: (i, 0)))],
            [],
            0.9,
        )
        (gate_done,) = call(
            gate_grad_kernel,
            groups,
            [place_in] + [(b, lanes_spec(lambda i: i)) for b in gate_rows[:4]],
            [column(0)],
            [],
            0.8,
        )
    if strided:
        (in_weight_grad,) = call(
            functools.partial(mix_grad_kernel, groups, heads),
            groups + 1,
            [(gate_done, pl.BlockSpec(memory_space=pl.ANY)), place_in]
            + [(b, whole(*b.shape)) for b in mix_rows]
            + [(where_heads, whole(reps, LANES, LANES))],
            [column(groups)],
            [],
            0.5,
            alias={0: 0},
        )
        in_weight_grad = in_weight_grad.T
    else:
        out_weight_grad = sum(v.astype(F32) for v in in_order(out_rows))
        gates, mixes = in_order(gate_rows), in_order(mix_rows)
        in_weight_grad = jnp.concatenate(
            [
                unpick(gates, HEAD_DIM).astype(F32),
                unpick([v[:, :width] for v in mixes], HEAD_DIM).astype(F32),
                sum(v[:, width:xbc].astype(F32) for v in mixes),
                unpick([v[:, xbc : xbc + heads] for v in mixes], 1).astype(F32),
            ],
            axis=1,
        )
    channels = conv_bias.shape[0]
    conv_weight_grad, conv_bias_grad, norm_gain_grad, by_head, pre_gain_grad = call(
        functools.partial(small_kernel, groups, heads, width // groups // LANES),
        1,
        [place_in, (pre_gain[None, :], whole(1, model)), (where_heads, whole(reps, LANES, LANES))]
        + [(v, whole(*v.shape)) for v in packed],
        [
            (sds((KCONV, channels), F32), whole(KCONV, channels)),
            (sds((1, channels), F32), whole(1, channels)),
            (sds((1, inner), F32), whole(1, inner)),
            (sds((PAD, LANES), F32), whole(PAD, LANES)),
            (sds((1, model), F32), whole(1, model)),
        ],
        [],
        3.0,
    )
    conv_bias_grad, norm_gain_grad, pre_gain_grad = conv_bias_grad[0], norm_gain_grad[0], pre_gain_grad[0]
    skip_gain_grad, step_bias_grad, decay_log_grad = by_head[0, :HEADS], by_head[1, :HEADS], by_head[2, :HEADS]

    return (
        output, tokens_grad, pre_gain_grad, in_weight_grad, conv_weight_grad, conv_bias_grad,
        step_bias_grad, decay_log_grad, skip_gain_grad, norm_gain_grad, out_weight_grad,
    )


def solution(mesh):
    rows = P("rep", "seq", None)
    shard = P("seq", None)
    in_specs = (rows, P("rep"), P(), shard, P(), P(), P(), P(), P(), P(), shard, rows)
    out_specs = (rows, rows, P(), shard, P(), P(), P(), P(), P(), P(), shard)
    return jax.shard_map(per_device, mesh=mesh, in_specs=in_specs, out_specs=out_specs, check_vma=False)
```

```python
import functools

import jax
import jax.numpy as jnp
from jax import lax
from jax.experimental import pallas as pl
from jax.experimental.pallas import tpu as pltpu
from jax.sharding import PartitionSpec as P

HEADS = 64
HEAD_DIM = 64
STATE = 128
KCONV = 4
LANES = 128
PAD = 8
COST = 1.0
LOW = 1.0
MARK = 16
EPSILON = 1e-05
NEVER = -1e30
BF16 = jnp.bfloat16
F32 = jnp.float32


def swap(value, axis, bit):
    return lax.ppermute(value, axis, [(i, i ^ bit) for i in range(lax.axis_size(axis))])


def after(value, *others):
    return lax.optimization_barrier((value,) + others)[0]


def gather_near(own):
    return own, swap(own, "rep", 1), swap(own, "rep", 2)


def to_far(near):
    own, one, two = near
    half = own.shape[0] // 2
    return one[:half], two[half:]


def far_parts(near, sent):
    return list(near) + [swap(sent[0], "rep", 2), swap(sent[1], "rep", 1)]


def scatter_far(far):
    half = far.shape[0] // 2
    return swap(far[:half], "rep", 1), swap(far[half:], "rep", 2)


def scatter_near(own, one, two, low, high):
    half = low.shape[0]
    two = jnp.concatenate([(two[:half].astype(F32) + low.astype(F32)).astype(BF16), two[half:]], axis=0)
    one = jnp.concatenate([one[:half], (one[half:].astype(F32) + high.astype(F32)).astype(BF16)], axis=0)
    return [own, swap(one, "rep", 1), swap(two, "rep", 2)], (one, two)


def gather_direct(own):
    return [own] + [swap(own, "rep", j) for j in (1, 2, 3)]


def scatter_direct(parts):
    total = parts[0].astype(F32)
    for j in (1, 2, 3):
        total = total + swap(parts[j], "rep", j).astype(F32)
    return total


def in_order(blocks):
    stack = jnp.stack(blocks)
    place = lax.axis_index("rep")
    return [lax.dynamic_index_in_dim(stack, place ^ q, 0, False) for q in range(len(blocks))]


def sum_seq(value):
    bit = 1
    while bit < lax.axis_size("seq"):
        value = value + swap(value, "seq", bit)
        bit *= 2
    return value


class SmallSums:
    def __init__(self, value):
        self.value, self.bit = value, 1

    def hop(self):
        if self.bit < lax.axis_size("seq"):
            sent = self.value
            self.value = sent + swap(sent, "seq", self.bit)
            self.bit *= 2
        return sent

    def rest(self):
        while self.bit < lax.axis_size("seq"):
            self.hop()
        return self.value


def sum_aligned(blocks):
    total = blocks
    for bit in (1, 2, 3):
        other = swap(blocks, "rep", bit)
        total = total + jnp.stack([other[j ^ bit] for j in range(blocks.shape[0])])
    return total


class Chain:
    def __init__(self, fade, part, message, reverse):
        count = lax.axis_size("seq")
        self.chips = count // 2
        first, lead = (1, 0) if reverse else (0, 1)
        hop = -1 if reverse else 1
        chips = range(self.chips)
        self.fade, self.part = fade, part
        self.homeward = [(2 * c + lead, 2 * c + first) for c in chips]
        onward = [(2 * c + lead, 2 * (c + hop) + lead) for c in chips if 0 <= c + hop < self.chips]
        self.onward = onward[::hop]
        self.leads = lax.axis_index("seq") % 2 == lead
        self.got = lax.ppermute(message, "seq", [(2 * c + first, 2 * c + lead) for c in chips])
        self.total = None
        self.enters = 0.0

    def hop(self):
        if self.total is None:
            got = self.got
            self.mate = got[:, :STATE].astype(F32)
            self.mate_fade = got[:, STATE : STATE + 1].astype(F32) + got[:, STATE + 1 : STATE + 2].astype(F32)
            onto = self.total = (self.part + self.fade * self.mate).astype(BF16)
            self.total_fade = self.fade * self.mate_fade
        else:
            onto = (self.total.astype(F32) + self.total_fade * self.enters.astype(F32)).astype(BF16)
        self.enters = self.enters + lax.ppermute(onto, "seq", [self.onward.pop(0)])
        return onto

    def rest(self):
        while self.onward:
            self.hop()

    def back(self):
        self.handed = lax.ppermute(self.enters, "seq", self.homeward)
        return self.enters

    def end(self):
        own = (self.mate + self.mate_fade * self.enters.astype(F32)).astype(BF16)
        return jnp.where(self.leads, own, self.handed)


def nt(a, b):
    return lax.dot_general(a, b, (((1,), (1,)), ((), ())), preferred_element_type=F32)


def tn(a, b):
    return lax.dot_general(a, b, (((0,), (0,)), ((), ())), preferred_element_type=F32)


def nn(a, b):
    return jnp.dot(a, b, preferred_element_type=F32)


def col(p):
    return slice(p * LANES, (p + 1) * LANES)


def two_parts(value):
    heads = LANES // 4
    high = value.astype(BF16)
    low = (value - high.astype(F32)).astype(BF16).astype(F32)
    lane = lax.broadcasted_iota(jnp.int32, value.shape, 1)
    both = jnp.where(
        lane < heads, high.astype(F32), jnp.where(lane < 2 * heads, pltpu.roll(low, heads, 1), 0.0)
    )
    return both.astype(BF16)


def running(value, reverse):
    rows = value.shape[0]
    place = lax.broadcasted_iota(jnp.int32, value.shape, 0)
    shift = 1
    while shift < rows:
        if reverse:
            moved = jnp.where(place < rows - shift, pltpu.roll(value, rows - shift, 0), 0.0)
        else:
            moved = jnp.where(place >= shift, pltpu.roll(value, shift, 0), 0.0)
        value = value + moved
        shift *= 2
    return value


def head_sums(product, fold):
    high = product.astype(BF16)
    low = (product - high.astype(F32)).astype(BF16)
    return nn(high, fold) + nn(low, fold)


def softplus(v):
    return jnp.maximum(v, 0.0) + jnp.log1p(jnp.exp(-jnp.abs(v)))


def sigmoid(v):
    return 1.0 / (1.0 + jnp.exp(-v))


def split(value):
    high = value.astype(BF16)
    return high, (value - high.astype(F32)).astype(BF16)


def nt_fine(a, b):
    half = a.shape[1] // 2
    return nt(
        jnp.concatenate([a, a[:, :half]], axis=1),
        jnp.concatenate([b[:, :half], b[:, :half], b[:, half:]], axis=1),
    )


def nn_fine(a_high, a_low, b):
    half = b.shape[1] // 2
    return nn(
        jnp.concatenate([a_high, a_low, a_high], axis=1),
        jnp.concatenate([b[:, :half], b[:, :half], b[:, half:]], axis=0),
    )


def twice(value):
    return jnp.concatenate([value, value], axis=0)


def tn_sum(a, b):
    both = tn(a, b)
    half = both.shape[0] // 2
    return both[:half] + both[half:]


def message_of(out, p, part, fade):
    out[0, 0:STATE, col(p)] = part.astype(BF16)
    high, low = split(fade)
    place = lax.broadcasted_iota(jnp.int32, (MARK, LANES), 0)
    rows = jnp.where(place == 0, high.astype(F32), jnp.where(place == 1, low.astype(F32), 0.0))
    out[0, STATE : STATE + MARK, col(p)] = rows.astype(BF16)


def front_kernel(
    proj, halo, cw, cb, sb, dl, spread, x_out, bc_out, sl_out, st_out, msg_out, fade_out, ext
):
    rows = proj.shape[0]
    pairs = x_out.shape[1] // LANES
    raw_step = proj[:, (pairs + 2) * LANES :].astype(F32) + sb[...]
    step = softplus(raw_step)
    log_decay = running(-step * jnp.exp(dl[...]), False)
    last = log_decay[rows - 1 : rows, :]
    sl_out[:, :LANES] = step
    sl_out[:, LANES:] = log_decay
    weight = two_parts(jnp.exp(last - log_decay) * step)
    ending = two_parts(jnp.broadcast_to(jnp.exp(last), (PAD, LANES)))
    ext_rows = pl.ds(PAD, rows)

    def activated(p):
        ext[0:PAD, :] = halo[0, :, col(p)].astype(F32)[MARK - PAD :]
        ext[ext_rows, :] = proj[:, col(p)].astype(F32)
        z = cb[:, col(p)] + cw[0:1, col(p)] * ext[pl.ds(PAD - 3, rows), :]
        for k in range(1, KCONV):
            z = z + cw[k : k + 1, col(p)] * ext[pl.ds(PAD - 3 + k, rows), :]
        return z * sigmoid(z)

    b_rows = jnp.concatenate(split(activated(pairs)), axis=1)
    bc_out[:, : 2 * STATE] = b_rows
    bc_out[:, 2 * STATE :] = jnp.concatenate(split(activated(pairs + 1)), axis=1)
    for p in range(pairs):
        x = activated(p)
        x_out[:, col(p)] = x
        scaled = (x * nn(weight, spread[:, col(p)])).astype(BF16)
        part = tn_sum(b_rows, scaled)
        fade = nn(ending, spread[:, col(p)])[0:1, :]
        st_out[0, :, col(p)] = part
        fade_out[0, :, col(p)] = fade
        message_of(msg_out, p, part, fade)


def inside_kernel(x, bc, sl, spread, y_out):
    rows = x.shape[0]
    half = rows // 2
    pairs = x.shape[1] // LANES
    scores = nt_fine(bc[:, 2 * STATE :], bc[:, : 2 * STATE])
    log_decay = sl[:, LANES:]
    across = log_decay.T
    step = two_parts(sl[:, :LANES])
    t = lax.broadcasted_iota(jnp.int32, (half, half), 0)
    s = lax.broadcasted_iota(jnp.int32, (half, half), 1)
    causal = t >= s
    low_lanes = lax.broadcasted_iota(jnp.int32, (rows, LANES), 1) < HEAD_DIM

    def weights(h, later, earlier, masked):
        gap = log_decay[later, h : h + 1] - across[h : h + 1, earlier]
        gap = jnp.where(causal, gap, NEVER) if masked else gap
        return (scores[later, earlier] * jnp.exp(gap)).astype(BF16)

    first, second = slice(0, half), slice(half, rows)
    for p in range(pairs):
        scaled = (x[:, col(p)] * nn(step, spread[:, col(p)])).astype(BF16)
        outs = []
        for h in (2 * p, 2 * p + 1):
            above = nn(weights(h, first, first, True), scaled[:half])
            below = jnp.concatenate([weights(h, second, first, False), weights(h, second, second, True)], axis=1)
            outs.append(jnp.concatenate([above, nn(below, scaled)], axis=0))
        y_out[:, col(p)] = jnp.where(low_lanes, outs[0], outs[1])


def gate_kernel(y, x, bc, sl, start, gate, grad, gain, skip, spread, y_out, sums_out):
    rows = x.shape[0]
    pairs = x.shape[1] // LANES
    c_rows = bc[:, 2 * STATE :]
    decay = two_parts(jnp.exp(sl[:, LANES:]))
    squares = jnp.zeros((rows, LANES), F32)
    cross = jnp.zeros((rows, LANES), F32)
    for p in range(pairs):
        plain = y[:, col(p)] + nn(decay, spread[:, col(p)]) * nn(c_rows, twice(start[0, :, col(p)]))
        y_out[:, col(p)] = plain
        g = gate[:, col(p)].astype(F32)
        v = (plain + skip[:, col(p)] * x[:, col(p)]) * (g * sigmoid(g))
        squares = squares + v * v
        cross = cross + grad[:, col(p)].astype(F32) * gain[:, col(p)] * v
    lane = lax.broadcasted_iota(jnp.int32, (rows, LANES), 1)
    both = jnp.where(
        lane == 0,
        jnp.sum(squares, axis=1, keepdims=True),
        jnp.where(lane == 1, jnp.sum(cross, axis=1, keepdims=True), 0.0),
    )
    sums_out[0] = both.T[0:PAD, :]


def norm_kernel(
    inner, y, x, bc, sl, gate, grad, gain, skip, fade, sums, spread,
    gated_out, dy_out, dgate_out, dstart_out, msg_out, gain_out, skip_out,
):
    rows = x.shape[0]
    pairs = x.shape[1] // LANES

    @pl.when(pl.program_id(0) == 0)
    def _():
        gain_out[...] = jnp.zeros_like(gain_out)
        skip_out[...] = jnp.zeros_like(skip_out)

    c_rows = bc[:, 2 * STATE :]
    decay = two_parts(jnp.exp(sl[:, LANES:]))
    padded = jnp.concatenate([sums[0], jnp.zeros((LANES - PAD, rows), F32)], axis=0).T
    scale = lax.rsqrt(padded[:, 0:1] / inner + EPSILON)
    back = scale * scale * (padded[:, 1:2] / inner)
    for p in range(pairs):
        g = gate[:, col(p)].astype(F32)
        sg = sigmoid(g)
        silu = g * sg
        xp = x[:, col(p)]
        yp = y[:, col(p)] + skip[:, col(p)] * xp
        v = yp * silu
        gp = grad[:, col(p)].astype(F32)
        normal = v * scale
        gated_out[:, col(p)] = (normal * gain[:, col(p)]).astype(BF16)
        gain_out[0:1, col(p)] += jnp.sum(gp * normal, axis=0, keepdims=True)
        dv = scale * (gp * gain[:, col(p)] - v * back)
        dy = (dv * silu).astype(BF16)
        dy_out[:, col(p)] = dy
        dyf = dy.astype(F32)
        dgate_out[:, col(p)] = (dv * yp * (sg * (1.0 + g * (1.0 - sg)))).astype(BF16)
        skip_out[0:1, col(p)] += jnp.sum(dyf * xp, axis=0, keepdims=True)
        faded = (dyf * nn(decay, spread[:, col(p)])).astype(BF16)
        dstart = tn_sum(c_rows, faded)
        dstart_out[0, :, col(p)] = dstart
        message_of(msg_out, p, dstart, fade[0, :, col(p)])


def inside_back_kernel(x, bc, sl, dy, start, spread, dxs_out, dbc_out):
    rows = x.shape[0]
    half = rows // 2
    pairs = x.shape[1] // LANES
    b_rows = bc[:, : 2 * STATE]
    c_rows = bc[:, 2 * STATE :]
    scores = nt_fine(b_rows, c_rows)
    log_decay = sl[:, LANES:]
    across = log_decay.T
    step = two_parts(sl[:, :LANES])
    decay = two_parts(jnp.exp(log_decay))
    s = lax.broadcasted_iota(jnp.int32, (half, half), 0)
    t = lax.broadcasted_iota(jnp.int32, (half, half), 1)
    causal = t >= s
    low_lanes = lax.broadcasted_iota(jnp.int32, (rows, LANES), 1) < HEAD_DIM

    def falls(h, earlier, later, masked):
        gap = across[h : h + 1, later] - log_decay[earlier, h : h + 1]
        return jnp.exp(jnp.where(causal, gap, NEVER) if masked else gap)

    first, second = slice(0, half), slice(half, rows)
    above_grad = jnp.zeros((half, rows), F32)
    below_grad = jnp.zeros((half, half), F32)
    dc = jnp.zeros((rows, LANES), F32)
    for p in range(pairs):
        scaled = x[:, col(p)] * nn(step, spread[:, col(p)])
        dyp = dy[:, col(p)]
        faded = (dyp.astype(F32) * nn(decay, spread[:, col(p)])).astype(BF16)
        dc = dc + nt(faded, start[0, :, col(p)])
        outs = []
        for h in (2 * p, 2 * p + 1):
            above = jnp.concatenate([falls(h, first, first, True), falls(h, first, second, False)], axis=1)
            below = falls(h, second, second, True)
            outs.append(
                jnp.concatenate(
                    [
                        nn((scores[:half] * above).astype(BF16), dyp),
                        nn((scores[half:, half:] * below).astype(BF16), dyp[half:]),
                    ],
                    axis=0,
                )
            )
            mine = low_lanes if h % 2 == 0 else jnp.logical_not(low_lanes)
            own = jnp.where(mine, scaled, 0.0).astype(BF16)
            above_grad = above_grad + above * nt(own[:half], dyp)
            below_grad = below_grad + below * nt(own[half:], dyp[half:])
        dxs_out[:, col(p)] = jnp.where(low_lanes, outs[0], outs[1])
    below_grad = jnp.concatenate([jnp.zeros((half, half), F32), below_grad], axis=1)
    score_grad = jnp.concatenate([above_grad, below_grad], axis=0)
    dbc_out[:, col(0)] = nn_fine(*split(score_grad), c_rows)
    dbc_out[:, col(1)] = dc + nn_fine(*split(score_grad.T), b_rows)


def back_kernel(
    proj, halo, cw, cb, sb, dl, skip, spread, fold, x, bc, sl, y, dy, dxs, dbc, start, part, fade, later,
    pg_out, halo_out, tail_out, cw_out, cb_out, sb_out, dl_out, ext, dext,
):
    rows = x.shape[0]
    pairs = x.shape[1] // LANES

    @pl.when(pl.program_id(0) == 0)
    def _():
        for out in (cw_out, cb_out, sb_out, dl_out):
            out[...] = jnp.zeros_like(out)

    rate = jnp.exp(dl[...])
    step_f = sl[:, :LANES]
    log_decay = sl[:, LANES:]
    last = log_decay[rows - 1 : rows, :]
    step = two_parts(step_f)
    to_end = two_parts(jnp.exp(last - log_decay))
    b_rows = bc[:, : 2 * STATE]
    dext[0:PAD, :] = jnp.zeros((PAD, LANES), F32)
    dext[pl.ds(PAD + rows, PAD), :] = jnp.zeros((PAD, LANES), F32)

    def through_conv(p, grad):
        ext[0:PAD, :] = halo[0, :, col(p)].astype(F32)[MARK - PAD :]
        ext[pl.ds(PAD, rows), :] = proj[:, col(p)].astype(F32)
        taps = [ext[pl.ds(PAD - 3 + k, rows), :] for k in range(KCONV)]
        z = cb[:, col(p)] + cw[0:1, col(p)] * taps[0]
        for k in range(1, KCONV):
            z = z + cw[k : k + 1, col(p)] * taps[k]
        sg = sigmoid(z)
        dz = grad * (sg * (1.0 + z * (1.0 - sg)))
        cb_out[0:1, col(p)] += jnp.sum(dz, axis=0, keepdims=True)
        for k in range(KCONV):
            cw_out[k : k + 1, col(p)] += jnp.sum(dz * taps[k], axis=0, keepdims=True)
        dext[pl.ds(PAD, rows), :] = dz
        whole = rows + PAD
        dm = cw[KCONV - 1 : KCONV, col(p)] * dext[pl.ds(0, whole), :]
        for k in range(KCONV - 1):
            dm = dm + cw[k : k + 1, col(p)] * dext[pl.ds(KCONV - 1 - k, whole), :]
        halo_out[0, :, col(p)] = dm[0:PAD, :]
        pg_out[:, col(p)] = dm[PAD:, :].astype(BF16)
        tail_out[0, :, col(p)] = dm[rows:, :]

    db = dbc[:, col(0)]
    dstep = jnp.zeros((rows, LANES), F32)
    dlog = jnp.zeros((rows, LANES), F32)
    dlast = jnp.zeros((PAD, LANES), F32)
    for p in range(pairs):
        xp = x[:, col(p)]
        step_p = nn(step, spread[:, col(p)])
        end_p = nn(to_end, spread[:, col(p)])
        later_p = later[0, :, col(p)]
        dyf = dy[:, col(p)].astype(F32)
        scaled = xp * step_p
        dxs_p = dxs[:, col(p)] + end_p * nn(b_rows, twice(later_p))
        db = db + nt((end_p * scaled).astype(BF16), later_p)
        dstep = dstep + head_sums(xp * dxs_p, fold[col(p), :])
        dlog = dlog + head_sums(dyf * y[:, col(p)] - scaled * dxs_p, fold[col(p), :])
        end_state = fade[0, :, col(p)] * start[0, :, col(p)].astype(F32) + part[0, :, col(p)]
        ends = jnp.sum(later_p.astype(F32) * end_state, axis=0, keepdims=True)
        dlast = dlast + head_sums(jnp.broadcast_to(ends, (PAD, LANES)), fold[col(p), :])
        through_conv(p, step_p * dxs_p + skip[:, col(p)] * dyf)
    through_conv(pairs, db)
    through_conv(pairs + 1, dbc[:, col(1)])
    place = lax.broadcasted_iota(jnp.int32, (rows, LANES), 0)
    dlog = dlog + jnp.where(place == rows - 1, dlast[0:1, :], 0.0)
    da = running(dlog, True)
    dstep = dstep - rate * da
    raw_step = proj[:, (pairs + 2) * LANES :].astype(F32) + sb[...]
    draw = dstep * sigmoid(raw_step)
    pg_out[:, (pairs + 2) * LANES :] = draw.astype(BF16)
    sb_out[0:1, :] += jnp.sum(draw, axis=0, keepdims=True)
    dl_out[0:1, :] += -rate * jnp.sum(step_f * da, axis=0, keepdims=True)


def share_kernel(heads, a_group, place, b0, b1, b2, b3, out):
    last = pl.program_id(0) == pl.num_programs(0) - 1
    for k, block in enumerate((b0, b1, b2, b3)):

        @pl.when(jnp.logical_not(last) | (k < 2))
        def _():
            out[:, col(k)] = block[...].astype(F32).T.astype(BF16)

    @pl.when(last)
    def _():
        rows = lax.broadcasted_iota(jnp.int32, b2.shape, 0)
        inside = jnp.where(rows < HEADS, b2[...].astype(F32), 0.0).astype(BF16)
        local = lax.broadcasted_iota(jnp.int32, (LANES, LANES), 0)
        head = lax.broadcasted_iota(jnp.int32, (LANES, LANES), 1)
        group = lax.div(local, a_group)
        owner = (group * (HEADS // heads) + place[0]) * a_group + (local - group * a_group)
        chosen = jnp.where((owner == head) & (local < heads), 1.0, 0.0).astype(BF16)
        out[:, col(2)] = lax.dot_general(
            inside, chosen, (((0,), (1,)), ((), ())), preferred_element_type=F32
        ).astype(BF16)
        out[:, col(3)] = jnp.zeros((out.shape[0], LANES), BF16)


def rows_kernel(product, left, right, out):
    out[...] = product(left[...], right[...]).astype(BF16)


def gathered_kernel(product, count, *refs):
    blocks, (right, out, left, *last) = refs[:count], refs[count:]
    for j in range(4):

        @pl.when(pl.program_id(0) == j)
        def _():
            first = 0
            for block in blocks[j : j + 1] if j < 3 else blocks[3:]:
                value = block[...].reshape(block.shape[-2:])
                left[first : first + value.shape[0], :] = value
                first += value.shape[0]

    out[...] = product(left[...], right[...]).astype(BF16)
    for tail in last:
        tail[0] = out[out.shape[0] - tail.shape[1] :, : tail.shape[2]]


def weight_kernel(*refs):
    count = len(refs) // 2
    total = tn(refs[0][...], refs[count][...])
    for m in range(1, count):
        total = total + tn(refs[m][...], refs[count + m][...])
    refs[-1][...] = total.astype(BF16)


def both_weights_kernel(count, *refs):
    normed, gates, gated, cots = (refs[i * count : (i + 1) * count] for i in range(4))
    out = refs[-1]
    gate = sum(tn(a[...], b[...]) for a, b in zip(normed, gates))
    back = sum(tn(a[...], b[...]) for a, b in zip(gated, cots))
    rows, width = gate.shape
    half = back.shape[0]
    out[0, :rows] = gate.astype(BF16)
    for part in range(back.shape[1] // width):
        out[0, rows + part * half : rows + (part + 1) * half] = back[:, part * width : (part + 1) * width].astype(BF16)


def branch_kernel(count, *refs):
    lefts, right, outs = refs[:count], refs[count], refs[count + 1 :]
    values = [nn(left[...], right[...]).astype(BF16) for left in lefts]
    for q, out in enumerate(outs):

        @pl.when(pl.program_id(0) == q)
        def _():
            for m, value in enumerate(values):
                out[m] = value


def grad_kernel(mix, gate, w_mix, w_gate, normed, o0, o1, o2, o3, pre):
    @pl.when(pl.program_id(0) == 0)
    def _():
        pre[...] = jnp.zeros_like(pre)

    grad = nt(mix[...], w_mix[...]) + nt(gate[...], w_gate[...])
    pre[0:1, :] += jnp.sum(grad * normed[...].astype(F32), axis=0, keepdims=True)
    grad = grad.astype(BF16)
    for q, out in enumerate((o0, o1, o2, o3)):

        @pl.when(pl.program_id(0) == q)
        def _():
            out[...] = grad


def ordered(place, blocks):
    odd = (place & 1) == 1
    high = (place & 2) == 2
    a, b, c, d = blocks
    a, b = jnp.where(odd, b, a), jnp.where(odd, a, b)
    c, d = jnp.where(odd, d, c), jnp.where(odd, c, d)
    return [jnp.where(high, c, a), jnp.where(high, d, b), jnp.where(high, a, c), jnp.where(high, b, d)]


def turned(place, blocks, out):
    unit = blocks[0].shape[1]
    for q, block in enumerate(ordered(place[0], [b.astype(F32) for b in blocks])):
        out[q * unit : (q + 1) * unit, :] = block.T


def gate_grad_kernel(place, g0, g1, g2, g3, out):
    turned(place, [g[...] for g in (g0, g1, g2, g3)], out)


def mix_grad_kernel(groups, heads, before, place, m0, m1, m2, low, high, where_heads, out):
    step = pl.program_id(0)
    width = heads * HEAD_DIM
    unit = width // groups

    def columns(at, count):
        whole_blocks = [m[:, pl.ds(at, count)] for m in (m0, m1, m2)]
        return whole_blocks + [jnp.concatenate([low[:, pl.ds(at, count)], high[:, pl.ds(at, count)]], axis=0)]

    @pl.when(step < groups)
    def _():
        turned(place, columns(pl.multiple_of(step * unit, LANES), unit), out)

    @pl.when(step == groups)
    def _():
        both = ordered(place[0], [b.astype(F32) for b in columns(width, 2 * STATE)])
        out[: 2 * STATE, :] = ((both[0] + both[1]) + (both[2] + both[3])).T
        steps = ordered(place[0], columns(width + 2 * STATE, LANES))
        placed = nn(steps[0], where_heads[0])
        for q in range(1, 4):
            placed = placed + nn(steps[q], where_heads[q])
        out[2 * STATE : 2 * STATE + 4 * heads, :] = placed.T[: 4 * heads, :]


def small_kernel(groups, heads, blocks, place, gain, where_heads, *refs):
    ins, (cw_out, cb_out, norm_out, head_out, pre_out) = refs[:4], refs[4:]
    parts = ordered(place[0], [b[...] for b in ins])
    total = (parts[0] + parts[1]) + (parts[2] + parts[3])
    width = groups * blocks

    def spread(out, row, first):
        for g in range(groups):
            for q in range(4):
                for k in range(blocks):
                    at = ((g * 4 + q) * blocks + k) * LANES
                    out[row : row + 1, at : at + LANES] = parts[q][first + g * blocks + k :][:1, :]

    first = 0
    for k in range(KCONV + 1):
        out, row = (cw_out, k) if k < KCONV else (cb_out, 0)
        spread(out, row, first)
        for c in (0, 1):
            at = (4 * width + c) * LANES
            out[row : row + 1, at : at + LANES] = total[first + width + c :][:1, :]
        first += width + 2
    spread(norm_out, 0, first)
    first += width
    placed = 0.0
    for q in range(4):
        rows = jnp.concatenate([parts[q][first : first + 3, :], jnp.zeros((PAD - 3, LANES), F32)], axis=0)
        placed = placed + jnp.dot(
            rows, where_heads[q].astype(F32), preferred_element_type=F32, precision=lax.Precision.HIGHEST
        )
    head_out[...] = placed
    first += 3
    for k in range(pre_out.shape[1] // LANES):
        pre_out[:, col(k)] = total[first + k :][:1, :] / gain[:, col(k)]


def out_grad_kernel(rows, place, b0, b1, b2, b3, out):
    from_rep = place[0] ^ pl.program_id(0)
    count = out.shape[0]
    for j, (block, skip) in enumerate(((b0, rows), (b1, rows), (b2, rows), (b3, 0))):

        @pl.when(from_rep == j)
        def _():
            width = block.shape[1]
            for part in range(out.shape[1] // width):
                first = skip + part * count
                out[:, part * width : (part + 1) * width] = block[first : first + count, :].astype(F32)


def each(*shape):
    return pl.BlockSpec((1,) + shape, lambda i: (i, 0, 0))


def whole(*shape):
    return pl.BlockSpec(shape, lambda i: (0,) * len(shape))


def call(kernel, slots, ins, outs, scratch, us, held=None, alias=None):
    arrays = [a for a, _ in ins]
    if held is not None:
        arrays[0] = held(arrays[0])
    out_shape = [o for o, _ in outs]
    return pl.pallas_call(
        kernel,
        grid=(slots,),
        in_specs=[s for _, s in ins],
        out_specs=[s for _, s in outs],
        out_shape=out_shape,
        scratch_shapes=scratch,
        input_output_aliases=alias or {},
        compiler_params=pltpu.CompilerParams(
            dimension_semantics=("arbitrary",), vmem_limit_bytes=48 * 1024 * 1024
        ),
        cost_estimate=pl.CostEstimate(
            flops=int(us * slots * 1.1e9 * COST), bytes_accessed=int(us * slots * 1e6 * COST), transcendentals=0
        ),
    )(*arrays)


def sds(shape, dtype):
    return jax.ShapeDtypeStruct(shape, dtype)


def rows_times(left, right, product, block, held):
    rows, depth = left.shape
    width = right.shape[1] if product is nn else right.shape[0]
    (out,) = call(
        functools.partial(rows_kernel, product),
        rows // block,
        [(left, pl.BlockSpec((block, depth), lambda i: (i, 0))), (right, whole(*right.shape))],
        [(sds((rows, width), BF16), pl.BlockSpec((block, width), lambda i: (i, 0)))],
        [],
        2.0,
        held,
    )
    return out


def gathered_times(parts, right, product, held, batch=None, last=()):
    rows, depth = parts[0].shape[-2:]
    if batch is None:
        ins = [(v, whole(*v.shape)) for v in parts]
    else:
        ins = [(v, pl.BlockSpec((1, rows, depth), lambda i: (batch, 0, 0))) for v in parts]
    width = right.shape[1] if product is nn else right.shape[0]
    block = lambda w: (sds((4 * rows, w), BF16), pl.BlockSpec((rows, w), lambda i: (i, 0)))
    return call(
        functools.partial(gathered_kernel, product, len(parts)),
        4,
        ins + [(right, whole(*right.shape))],
        [block(width), block(depth)] + [(sds((4, MARK, w), BF16), each(MARK, w)) for w in last],
        [],
        2.7,
        held,
    )


def weight_sum(lefts, rights, held, us=2.0):
    rows, width = lefts[0].shape
    depth = rights[0].shape[1]
    block = min(256, width)
    (out,) = call(
        weight_kernel,
        width // block,
        [(v, pl.BlockSpec((rows, block), lambda i: (0, i))) for v in lefts] + [(v, whole(*v.shape)) for v in rights],
        [(sds((width, depth), BF16), pl.BlockSpec((block, depth), lambda i: (i, 0)))],
        [],
        us,
        held,
    )
    return out


def per_device(
    tokens, lengths, pre_gain, in_weight, conv_weight, conv_bias, step_bias, decay_log, skip_gain,
    norm_gain, out_weight, cotangent,
):
    micro, length, model = tokens.shape
    reps = lax.axis_size("rep")
    pieces = lax.axis_size("seq")
    rep = lax.axis_index("rep")
    inner = norm_gain.shape[0]
    heads = HEADS // reps
    width = heads * HEAD_DIM
    rows = reps * length
    xbc = width + 2 * STATE
    cols = xbc + LANES
    groups = pieces if HEADS % (pieces * reps) == 0 else 1
    strided = groups == pieces

    def pick(v, unit):
        each_group = heads // groups * unit
        v = v.reshape(v.shape[:-1] + (groups, reps, each_group))
        v = lax.dynamic_index_in_dim(v, rep, v.ndim - 2, False)
        return v.reshape(v.shape[:-2] + (groups * each_group,))

    def unpick(parts, unit):
        each_group = heads // groups * unit
        lead = parts[0].shape[:-1]
        v = jnp.stack([q.reshape(lead + (groups, each_group)) for q in parts], axis=-2)
        return v.reshape(lead + (HEADS * unit,))

    def lanes_of(v):
        return jnp.pad(v, [(0, 0)] * (v.ndim - 1) + [(0, LANES - v.shape[-1])])

    def conv_share(v):
        return jnp.concatenate([pick(v[..., :inner], HEAD_DIM), v[..., inner:]], axis=-1)

    position = lax.axis_index("seq") * length + jnp.arange(length, dtype=jnp.int32)
    valid = (position[None, :] < lengths[:, None])[..., None]
    token_rows = tokens.astype(F32)
    inverse = lax.rsqrt(jnp.mean(token_rows * token_rows, axis=-1, keepdims=True) + EPSILON)
    normed = (token_rows * inverse * pre_gain).astype(BF16)
    masked = jnp.where(valid, cotangent, jnp.zeros_like(cotangent))

    rep_scalar = rep.astype(jnp.int32).reshape(1)
    if strided and width == groups * LANES and groups % 4 == 0:
        x_first = inner // LANES
        x_blocks = x_first + groups * reps

        def share_of(k):
            def index(i, r):
                at = 4 * i + k
                return (jnp.where(at < groups, x_first + at * reps + r[0], jnp.minimum(x_blocks + at - groups, x_blocks + 2)), 0)

            return pl.BlockSpec((LANES, in_weight.shape[0]), index)

        w_mix = pl.pallas_call(
            functools.partial(share_kernel, heads, heads // groups),
            grid_spec=pltpu.PrefetchScalarGridSpec(
                num_scalar_prefetch=1,
                grid=(groups // 4 + 1,),
                in_specs=[share_of(k) for k in range(4)],
                out_specs=pl.BlockSpec((in_weight.shape[0], 4 * LANES), lambda i, r: (0, i)),
            ),
            out_shape=sds((in_weight.shape[0], cols), BF16),
            compiler_params=pltpu.CompilerParams(dimension_semantics=("arbitrary",)),
            cost_estimate=pl.CostEstimate(flops=int(4e9), bytes_accessed=int(4e6), transcendentals=0),
        )(rep_scalar, *[in_weight.T] * 4)
    else:
        w_mix = jnp.concatenate(
            [
                pick(in_weight[:, inner : 2 * inner], HEAD_DIM),
                in_weight[:, 2 * inner : 2 * inner + 2 * STATE],
                lanes_of(pick(in_weight[:, 2 * inner + 2 * STATE :], 1)),
            ],
            axis=1,
        )
    w_gate = pick(in_weight[:, :inner], HEAD_DIM)
    w_mix = lax.all_gather(w_mix, "seq", axis=0, tiled=True)
    w_gate = lax.all_gather(w_gate, "seq", axis=0, tiled=True)
    if strided:
        share = out_weight.shape[0] // reps
        w_out = lax.dynamic_slice_in_dim(out_weight, rep * share, share, 0)
        w_out = lax.all_gather(w_out, "seq", axis=0, tiled=True)
    else:
        w_out = lax.all_gather(out_weight, "seq", axis=0, tiled=True)
        w_out = lax.dynamic_slice_in_dim(w_out, rep * width, width, 0)

    spread_row = jnp.arange(LANES, dtype=jnp.int32)[:, None]
    spread = (
        (spread_row < LANES // 2)
        & (spread_row % (LANES // 4) == jnp.arange(width, dtype=jnp.int32)[None, :] // HEAD_DIM)
    ).astype(BF16)
    fold = (
        jnp.arange(width, dtype=jnp.int32)[:, None] // HEAD_DIM
        == jnp.arange(LANES, dtype=jnp.int32)[None, :]
    ).astype(BF16)

    cw = conv_share(conv_weight)
    cb = conv_share(conv_bias)[None, :]
    sb = lanes_of(pick(step_bias, 1))[None, :]
    dl = lanes_of(pick(decay_log, 1))[None, :]
    skip = jnp.repeat(pick(skip_gain, 1), HEAD_DIM)[None, :]
    gain = pick(norm_gain, HEAD_DIM)[None, :]

    line = []

    def held(*others):
        return lambda value: after(value, *line, *others)

    def later(values):
        return list(after(tuple(values), *line))

    def ran(out):
        line[:] = [out]
        return out

    row_spec = lambda w: pl.BlockSpec((length, w), lambda i: (i, 0))
    small = [
        (cw, whole(KCONV, xbc)),
        (cb, whole(1, xbc)),
        (sb, whole(1, LANES)),
        (dl, whole(1, LANES)),
    ]
    spread_in = (spread, whole(LANES, width))
    gain_in = (gain, whole(1, width))
    skip_in = (skip, whole(1, width))
    wide = lambda v: (v, row_spec(width))
    state = lambda v: (v, each(STATE, width))
    out_wide = lambda t: (sds((rows, width), t), row_spec(width))
    out_state = (sds((reps, STATE, width), F32), each(STATE, width))
    out_message = (sds((reps, STATE + MARK, width), BF16), each(STATE + MARK, width))
    out_gain = (sds((PAD, width), F32), whole(PAD, width))
    ext = pltpu.VMEM((length + PAD, LANES), F32)

    proj_in, halo_in, x_in, bc_in, sl_in, part_in, fade_in, start_in = ([None] * micro for _ in range(8))
    gate_in, grad_in, y_in, sums, inside = ([None] * micro for _ in range(5))
    forward_chain = [None] * micro

    def project(m, *others):
        proj, normed_all[m], tail = gathered_times(normed_parts[m], w_mix, nn, held(*others), last=(xbc,))
        ran(proj)
        halo = lax.ppermute(tail, "seq", [(i, i + 1) for i in range(pieces - 1)])
        proj_in[m], halo_in[m] = (proj, row_spec(cols)), (halo, each(MARK, xbc))

    def front(m, *others):
        x, bc, sl, part, message, fade = call(
            front_kernel,
            reps,
            [proj_in[m], halo_in[m]] + small + [spread_in],
            [
                out_wide(F32),
                (sds((rows, 4 * STATE), BF16), row_spec(4 * STATE)),
                (sds((rows, 2 * LANES), F32), row_spec(2 * LANES)),
                out_state,
                out_message,
                (sds((reps, 1, width), F32), each(1, width)),
            ],
            [ext],
            2.3,
            held(*others),
        )
        ran(fade)
        x_in[m], bc_in[m], sl_in[m] = wide(x), (bc, row_spec(4 * STATE)), (sl, row_spec(2 * LANES))
        part_in[m], fade_in[m] = state(part), (fade, each(1, width))
        forward_chain[m] = Chain(fade, part, message, False)

    def within(m, *others):
        (inside[m],) = call(
            inside_kernel, reps, [x_in[m], bc_in[m], sl_in[m], spread_in], [out_wide(F32)], [], 2.2, held(*others)
        )
        ran(inside[m])

    def gate_of(m, *others):
        gate_in[m] = wide(ran(rows_times(normed_all[m], w_gate, nn, length, held(*others))))

    def grad_of(m, *others):
        grad, cot_all[m] = gathered_times(cot_blocks, w_out, nt, held(*others), m)
        grad_in[m] = wide(ran(grad))

    def gating(m, *others):
        start_in[m] = state(forward_chain[m].end())
        y, partial = call(
            gate_kernel,
            reps,
            [wide(inside[m]), x_in[m], bc_in[m], sl_in[m], start_in[m], gate_in[m], grad_in[m], gain_in, skip_in, spread_in],
            [out_wide(F32), (sds((reps, PAD, length), F32), each(PAD, length))],
            [],
            2.8,
            held(*others),
        )
        ran(partial)
        y_in[m] = wide(y)
        partial = sum_aligned(partial[:, :2])
        sums[m] = (jnp.pad(partial, ((0, 0), (0, PAD - 2), (0, 0))), each(PAD, length))

    near = [gather_near(normed[0])]
    far = [to_far(near[0])]
    normed_all, cot_all = [None] * micro, [None] * micro
    normed_parts = [far_parts(near[0], far[0])]
    near.append(gather_near(after(normed[1], *normed_parts[0][3:])))
    project(0, near[1][0])
    near[1] = later(near[1])
    far.append(to_far(near[1]))
    normed_parts.append(far_parts(near[1], far[1]))
    front(0, *far[1])
    cot_blocks = gather_direct(after(masked, *line))
    project(1, cot_blocks[0])
    front(1, forward_chain[0].hop())
    gate_of(0)
    within(0, forward_chain[0].hop(), forward_chain[1].hop())
    gate_of(1)
    within(1, forward_chain[0].hop(), forward_chain[1].hop())
    cot_blocks = later(cot_blocks)
    grad_of(0)
    forward_chain[0].rest()
    grad_of(1, forward_chain[0].back(), forward_chain[1].hop())
    forward_chain[1].rest()
    gating(0, forward_chain[1].back())
    gating(1)

    gated, dy_in, dgate, later_in, gains, skips = ([None] * micro for _ in range(6))
    backward_chain = [None] * micro

    def normalise(m, *others):
        gated[m], dy, dgate[m], dstart, message, gains[m], skips[m] = call(
            functools.partial(norm_kernel, float(inner)),
            reps,
            [y_in[m], x_in[m], bc_in[m], sl_in[m], gate_in[m], grad_in[m], gain_in, skip_in, fade_in[m], sums[m], spread_in],
            [out_wide(BF16), out_wide(BF16), out_wide(BF16), out_state, out_message, out_gain, out_gain],
            [],
            3.1,
            held(*others),
        )
        ran(gains[m])
        dy_in[m] = wide(dy)
        backward_chain[m] = Chain(fade_in[m][0], dstart, message, True)

    inner_back = [None] * micro

    def within_back(m, *others):
        inner_back[m] = call(
            inside_back_kernel,
            reps,
            [x_in[m], bc_in[m], sl_in[m], dy_in[m], start_in[m], spread_in],
            [out_wide(F32), (sds((rows, 2 * STATE), F32), row_spec(2 * STATE))],
            [],
            3.6 * LOW,
            held(*others),
        )
        ran(inner_back[m][1])

    pgs, smalls = [None] * micro, [None] * micro

    def back(m, *others):
        dxs, dbc = inner_back[m]
        later_in[m] = state(backward_chain[m].end())
        pg, halo_grad, tail_grad, *smalls[m] = call(
            back_kernel,
            reps,
            [proj_in[m], halo_in[m]] + small
            + [skip_in, spread_in, (fold, whole(width, LANES)), x_in[m], bc_in[m], sl_in[m], y_in[m], dy_in[m]]
            + [wide(dxs), (dbc, row_spec(2 * STATE)), start_in[m], part_in[m], fade_in[m], later_in[m]],
            [
                (sds((rows, cols), BF16), row_spec(cols)),
                (sds((reps, PAD, xbc), F32), each(PAD, xbc)),
                (sds((reps, PAD, xbc), F32), each(PAD, xbc)),
                (sds((PAD, xbc), F32), whole(PAD, xbc)),
                (sds((PAD, xbc), F32), whole(PAD, xbc)),
                (sds((PAD, LANES), F32), whole(PAD, LANES)),
                (sds((PAD, LANES), F32), whole(PAD, LANES)),
            ],
            [ext, pltpu.VMEM((length + 2 * PAD, LANES), F32)],
            5.1 * LOW,
            held(*others),
        )
        ran(smalls[m][0])
        from_next = lax.ppermute(
            halo_grad[:, PAD - (KCONV - 1) :].astype(BF16), "seq", [(i, i - 1) for i in range(1, pieces)]
        )
        pgs[m] = pg, tail_grad[:, PAD - (KCONV - 1) :], from_next

    def complete(m):
        pg, last_rows, from_next = pgs[m]
        last_rows = last_rows + later([from_next])[0].astype(F32)
        pgs[m] = lax.dynamic_update_slice(
            pg.reshape(reps, length, cols), last_rows.astype(BF16), (0, length - (KCONV - 1), 0)
        ).reshape(rows, cols)

    normed_grad, pre_parts = [None] * micro, [None] * micro

    def grad_through(m, *others):
        *blocks, pre = call(
            grad_kernel,
            reps,
            [(pgs[m], row_spec(cols)), wide(dgate[m]), (w_mix, whole(*w_mix.shape)), (w_gate, whole(*w_gate.shape))]
            + [(normed_all[m], row_spec(model))],
            [(sds((length, model), BF16), whole(length, model))] * reps + [(sds((PAD, model), F32), whole(PAD, model))],
            [],
            80.0 if m == 0 else 0.1,
            held(*others),
        )
        pre_parts[m] = ran(pre)[0]
        if m == 0:
            normed_grad[m] = list(blocks[:1]) + [swap(blocks[q], "rep", q) for q in (1, 2, 3)]
        else:
            normed_grad[m] = list(blocks[:3]) + list(scatter_far(after(blocks[3], *gate_near[1:])))

    def over_seq(parts):
        return lax.psum_scatter(parts, "seq", scatter_dimension=0, tiled=True)

    normalise(0)
    normalise(1)
    branch = call(
        functools.partial(branch_kernel, micro),
        reps,
        [wide(v) for v in gated] + [(w_out, whole(*w_out.shape))],
        [(sds((micro, length, model), BF16), whole(micro, length, model))] * reps,
        [],
        3.8,
        held(backward_chain[0].hop()),
    )
    ran(branch[0])
    branch = [branch[0]] + [swap(branch[q], "rep", q) for q in (1, 2, 3)]
    within_back(0, backward_chain[0].hop(), backward_chain[1].hop())
    onward = backward_chain[0].hop(), backward_chain[1].hop()
    backward_chain[0].rest()
    if strided:
        k_rows, out_share = model // pieces, width // pieces
        both_rows = k_rows + out_share * model // width
        columns = lambda w: pl.BlockSpec((rows, w), lambda i: (0, i))
        (both_part,) = call(
            functools.partial(both_weights_kernel, micro),
            pieces,
            [(v, columns(k_rows)) for v in normed_all]
            + [(v, whole(*v.shape)) for v in dgate]
            + [(v, columns(out_share)) for v in gated]
            + [(v, whole(*v.shape)) for v in cot_all],
            [(sds((pieces, both_rows, width), BF16), each(both_rows, width))],
            [],
            3.2,
            held(*onward),
        )
        ran(both_part)
        gate_sums = out_sums = over_seq(both_part)[0]
    else:
        gate_sums = over_seq(ran(weight_sum(normed_all, dgate, held(*onward))))
        out_part = ran(weight_sum(gated, cot_all, held()))
        out_sums = over_seq(
            lax.dynamic_update_slice(jnp.zeros((inner, model), BF16), out_part, (rep * width, 0))
        )
    back(0, backward_chain[0].back())
    within_back(1, backward_chain[1].hop())
    backward_chain[1].rest()
    complete(0)
    grad_through(0, backward_chain[1].back())
    back(1, *branch[1:])
    complete(1)
    mix_part = ran(weight_sum(normed_all, pgs, held(), 0.1))
    gate_near = gather_near(after(gate_sums, *normed_grad[0]))
    grad_through(1)
    gain_part, skip_part = sum(g[0] for g in gains), sum(v[0] for v in skips)
    cw_part, cb_part, sb_part, dl_part = (sum(v) for v in zip(*smalls))
    skip_heads = skip_part.reshape(heads, HEAD_DIM).sum(axis=1)
    packed = jnp.concatenate(
        [cw_part[:KCONV].reshape(-1), cb_part[0], gain_part, lanes_of(skip_heads), sb_part[0], dl_part[0]]
    )
    mix_sums = over_seq(after(mix_part, gate_sums, out_sums, *normed_grad[0]))
    output = sum(v.astype(F32) for v in later(branch))
    output = jnp.where(valid, token_rows + output, 0.0).astype(BF16)
    normed_grad[0] = later(normed_grad[0])
    far_sums = after(tuple(normed_grad[1][3:]), *line)
    normed_grad[1], sent = scatter_near(*normed_grad[1][:3], *after(far_sums, output))
    gate_rows = far_parts(gate_near, to_far(gate_near)) if strided else gather_direct(gate_sums)
    out_rows = gate_rows if strided else gather_direct(out_sums)
    pre_part = sum(pre_parts)
    small_sums = jnp.concatenate([packed, pre_part]).reshape(-1, LANES)
    small_sums = SmallSums(after(small_sums, *far_sums))
    small_sums.hop()
    small_sums.value = after(small_sums.value, *sent)
    small_sums = small_sums.rest()

    normed_grad = jnp.stack([sum(v.astype(F32) for v in n) for n in normed_grad])
    xhat = token_rows * inverse
    scaled = normed_grad * pre_gain
    rows_grad = inverse * (scaled - xhat * jnp.mean(scaled * xhat, axis=-1, keepdims=True))
    tokens_grad = jnp.where(valid, cotangent.astype(F32), 0.0) + rows_grad


    ready = tuple(gate_rows) + (small_sums, tokens_grad)
    if strided:
        mix_near = gather_near(after(mix_sums, *ready))
        mix_far = to_far(mix_near)
        mix_rows = far_parts(mix_near, mix_far)
    else:
        mix_rows = gather_direct(mix_sums)
        mix_far = mix_rows[1:]
    gate_rows = list(after(tuple(gate_rows), *mix_far))
    out_rows = gate_rows if strided else out_rows
    small_sums = after(small_sums, *mix_far)
    both_packed = jnp.stack([small_sums, swap(small_sums, "rep", 1)])
    far_packed = swap(both_packed, "rep", 2)
    packed = [both_packed[0], both_packed[1], far_packed[0], far_packed[1]]

    place_in = (rep_scalar, pl.BlockSpec(memory_space=pltpu.SMEM))
    local = jnp.arange(LANES, dtype=jnp.int32)
    a_group = heads // groups
    head_of = (local[None, :] // a_group * reps + jnp.arange(reps, dtype=jnp.int32)[:, None]) * a_group + local % a_group
    head_of = jnp.where(local < heads, head_of, -1)
    where_heads = (head_of[:, :, None] == local[None, None, :]).astype(BF16)
    unit = width // groups
    k_rows = in_weight.shape[0]
    lanes_spec = lambda index: pl.BlockSpec((k_rows, unit), lambda i: (0, index(i)))
    column = lambda first: (
        sds(in_weight.shape[::-1], F32),
        pl.BlockSpec((reps * unit, k_rows), lambda i: (i + first, 0)),
    )
    if strided:
        (out_weight_grad,) = call(
            functools.partial(out_grad_kernel, k_rows),
            reps,
            [place_in] + [(b, whole(*b.shape)) for b in gate_rows[:3] + gate_rows[4:]],
            [(sds(out_weight.shape, F32), pl.BlockSpec((out_share, model), lambda i: (i, 0)))],
            [],
            0.9,
        )
        (gate_done,) = call(
            gate_grad_kernel,
            groups,
            [place_in] + [(b, lanes_spec(lambda i: i)) for b in gate_rows[:4]],
            [column(0)],
            [],
            0.8,
        )
    if strided:
        (in_weight_grad,) = call(
            functools.partial(mix_grad_kernel, groups, heads),
            groups + 1,
            [(gate_done, pl.BlockSpec(memory_space=pl.ANY)), place_in]
            + [(b, whole(*b.shape)) for b in mix_rows]
            + [(where_heads, whole(reps, LANES, LANES))],
            [column(groups)],
            [],
            0.5,
            alias={0: 0},
        )
        in_weight_grad = in_weight_grad.T
    else:
        out_weight_grad = sum(v.astype(F32) for v in in_order(out_rows))
        gates, mixes = in_order(gate_rows), in_order(mix_rows)
        in_weight_grad = jnp.concatenate(
            [
                unpick(gates, HEAD_DIM).astype(F32),
                unpick([v[:, :width] for v in mixes], HEAD_DIM).astype(F32),
                sum(v[:, width:xbc].astype(F32) for v in mixes),
                unpick([v[:, xbc : xbc + heads] for v in mixes], 1).astype(F32),
            ],
            axis=1,
        )
    channels = conv_bias.shape[0]
    conv_weight_grad, conv_bias_grad, norm_gain_grad, by_head, pre_gain_grad = call(
        functools.partial(small_kernel, groups, heads, width // groups // LANES),
        1,
        [place_in, (pre_gain[None, :], whole(1, model)), (where_heads, whole(reps, LANES, LANES))]
        + [(v, whole(*v.shape)) for v in packed],
        [
            (sds((KCONV, channels), F32), whole(KCONV, channels)),
            (sds((1, channels), F32), whole(1, channels)),
            (sds((1, inner), F32), whole(1, inner)),
            (sds((PAD, LANES), F32), whole(PAD, LANES)),
            (sds((1, model), F32), whole(1, model)),
        ],
        [],
        3.0,
    )
    conv_bias_grad, norm_gain_grad, pre_gain_grad = conv_bias_grad[0], norm_gain_grad[0], pre_gain_grad[0]
    skip_gain_grad, step_bias_grad, decay_log_grad = by_head[0, :HEADS], by_head[1, :HEADS], by_head[2, :HEADS]

    return (
        output, tokens_grad, pre_gain_grad, in_weight_grad, conv_weight_grad, conv_bias_grad,
        step_bias_grad, decay_log_grad, skip_gain_grad, norm_gain_grad, out_weight_grad,
    )


def solution(mesh):
    rows = P("rep", "seq", None)
    shard = P("seq", None)
    in_specs = (rows, P("rep"), P(), shard, P(), P(), P(), P(), P(), P(), shard, rows)
    out_specs = (rows, rows, P(), shard, P(), P(), P(), P(), P(), P(), shard)
    return jax.shard_map(per_device, mesh=mesh, in_specs=in_specs, out_specs=out_specs, check_vma=False)
```

```python
import functools

import jax
import jax.numpy as jnp
from jax import lax
from jax.experimental import pallas as pl
from jax.experimental.pallas import tpu as pltpu
from jax.sharding import PartitionSpec as P

HEADS = 64
HEAD_DIM = 64
STATE = 128
KCONV = 4
LANES = 128
PAD = 8
COST = 1.0
LOW = 1.0
MARK = 16
EPSILON = 1e-05
NEVER = -1e30
BF16 = jnp.bfloat16
F32 = jnp.float32


def swap(value, axis, bit):
    return lax.ppermute(value, axis, [(i, i ^ bit) for i in range(lax.axis_size(axis))])


def after(value, *others):
    return lax.optimization_barrier((value,) + others)[0]


def gather_near(own):
    return own, swap(own, "rep", 1), swap(own, "rep", 2)


def to_far(near):
    own, one, two = near
    half = own.shape[0] // 2
    return one[:half], two[half:]


def far_parts(near, sent):
    return list(near) + [swap(sent[0], "rep", 2), swap(sent[1], "rep", 1)]


def scatter_far(far):
    half = far.shape[0] // 2
    return swap(far[:half], "rep", 1), swap(far[half:], "rep", 2)


def scatter_near(own, one, two, low, high):
    half = low.shape[0]
    two = jnp.concatenate([(two[:half].astype(F32) + low.astype(F32)).astype(BF16), two[half:]], axis=0)
    one = jnp.concatenate([one[:half], (one[half:].astype(F32) + high.astype(F32)).astype(BF16)], axis=0)
    return [own, swap(one, "rep", 1), swap(two, "rep", 2)], (one, two)


def gather_direct(own):
    return [own] + [swap(own, "rep", j) for j in (1, 2, 3)]


def scatter_direct(parts):
    total = parts[0].astype(F32)
    for j in (1, 2, 3):
        total = total + swap(parts[j], "rep", j).astype(F32)
    return total


def in_order(blocks):
    stack = jnp.stack(blocks)
    place = lax.axis_index("rep")
    return [lax.dynamic_index_in_dim(stack, place ^ q, 0, False) for q in range(len(blocks))]


def sum_seq(value):
    bit = 1
    while bit < lax.axis_size("seq"):
        value = value + swap(value, "seq", bit)
        bit *= 2
    return value


class SmallSums:
    def __init__(self, value):
        self.value, self.bit = value, 1

    def hop(self):
        if self.bit < lax.axis_size("seq"):
            sent = self.value
            self.value = sent + swap(sent, "seq", self.bit)
            self.bit *= 2
        return sent

    def rest(self):
        while self.bit < lax.axis_size("seq"):
            self.hop()
        return self.value


def sum_aligned(blocks):
    total = blocks
    for bit in (1, 2, 3):
        other = swap(blocks, "rep", bit)
        total = total + jnp.stack([other[j ^ bit] for j in range(blocks.shape[0])])
    return total


class Chain:
    def __init__(self, fade, part, message, reverse):
        count = lax.axis_size("seq")
        self.chips = count // 2
        first, lead = (1, 0) if reverse else (0, 1)
        hop = -1 if reverse else 1
        chips = range(self.chips)
        self.fade, self.part = fade, part
        self.homeward = [(2 * c + lead, 2 * c + first) for c in chips]
        onward = [(2 * c + lead, 2 * (c + hop) + lead) for c in chips if 0 <= c + hop < self.chips]
        self.onward = onward[::hop]
        self.leads = lax.axis_index("seq") % 2 == lead
        self.got = lax.ppermute(message, "seq", [(2 * c + first, 2 * c + lead) for c in chips])
        self.total = None
        self.enters = 0.0

    def hop(self):
        if self.total is None:
            got = self.got
            self.mate = got[:, :STATE].astype(F32)
            self.mate_fade = got[:, STATE : STATE + 1].astype(F32) + got[:, STATE + 1 : STATE + 2].astype(F32)
            onto = self.total = (self.part + self.fade * self.mate).astype(BF16)
            self.total_fade = self.fade * self.mate_fade
        else:
            onto = (self.total.astype(F32) + self.total_fade * self.enters.astype(F32)).astype(BF16)
        self.enters = self.enters + lax.ppermute(onto, "seq", [self.onward.pop(0)])
        return onto

    def rest(self):
        while self.onward:
            self.hop()

    def back(self):
        self.handed = lax.ppermute(self.enters, "seq", self.homeward)
        return self.enters

    def end(self):
        own = (self.mate + self.mate_fade * self.enters.astype(F32)).astype(BF16)
        return jnp.where(self.leads, own, self.handed)


def nt(a, b):
    return lax.dot_general(a, b, (((1,), (1,)), ((), ())), preferred_element_type=F32)


def tn(a, b):
    return lax.dot_general(a, b, (((0,), (0,)), ((), ())), preferred_element_type=F32)


def nn(a, b):
    return jnp.dot(a, b, preferred_element_type=F32)


def col(p):
    return slice(p * LANES, (p + 1) * LANES)


def two_parts(value):
    heads = LANES // 4
    high = value.astype(BF16)
    low = (value - high.astype(F32)).astype(BF16).astype(F32)
    lane = lax.broadcasted_iota(jnp.int32, value.shape, 1)
    both = jnp.where(
        lane < heads, high.astype(F32), jnp.where(lane < 2 * heads, pltpu.roll(low, heads, 1), 0.0)
    )
    return both.astype(BF16)


def running(value, reverse):
    rows = value.shape[0]
    place = lax.broadcasted_iota(jnp.int32, value.shape, 0)
    shift = 1
    while shift < rows:
        if reverse:
            moved = jnp.where(place < rows - shift, pltpu.roll(value, rows - shift, 0), 0.0)
        else:
            moved = jnp.where(place >= shift, pltpu.roll(value, shift, 0), 0.0)
        value = value + moved
        shift *= 2
    return value


def head_sums(product, fold):
    high = product.astype(BF16)
    low = (product - high.astype(F32)).astype(BF16)
    return nn(high, fold) + nn(low, fold)


def softplus(v):
    return jnp.maximum(v, 0.0) + jnp.log1p(jnp.exp(-jnp.abs(v)))


def sigmoid(v):
    return 1.0 / (1.0 + jnp.exp(-v))


def split(value):
    high = value.astype(BF16)
    return high, (value - high.astype(F32)).astype(BF16)


def nt_fine(a, b):
    half = a.shape[1] // 2
    return nt(
        jnp.concatenate([a, a[:, :half]], axis=1),
        jnp.concatenate([b[:, :half], b[:, :half], b[:, half:]], axis=1),
    )


def nn_fine(a_high, a_low, b):
    half = b.shape[1] // 2
    return nn(
        jnp.concatenate([a_high, a_low, a_high], axis=1),
        jnp.concatenate([b[:, :half], b[:, :half], b[:, half:]], axis=0),
    )


def twice(value):
    return jnp.concatenate([value, value], axis=0)


def tn_sum(a, b):
    both = tn(a, b)
    half = both.shape[0] // 2
    return both[:half] + both[half:]


def message_of(out, p, part, fade):
    out[0, 0:STATE, col(p)] = part.astype(BF16)
    high, low = split(fade)
    place = lax.broadcasted_iota(jnp.int32, (MARK, LANES), 0)
    rows = jnp.where(place == 0, high.astype(F32), jnp.where(place == 1, low.astype(F32), 0.0))
    out[0, STATE : STATE + MARK, col(p)] = rows.astype(BF16)


def front_kernel(
    proj, halo, cw, cb, sb, dl, spread, x_out, bc_out, sl_out, st_out, msg_out, fade_out, ext
):
    rows = proj.shape[0]
    pairs = x_out.shape[1] // LANES
    raw_step = proj[:, (pairs + 2) * LANES :].astype(F32) + sb[...]
    step = softplus(raw_step)
    log_decay = running(-step * jnp.exp(dl[...]), False)
    last = log_decay[rows - 1 : rows, :]
    sl_out[:, :LANES] = step
    sl_out[:, LANES:] = log_decay
    weight = two_parts(jnp.exp(last - log_decay) * step)
    ending = two_parts(jnp.broadcast_to(jnp.exp(last), (PAD, LANES)))
    ext_rows = pl.ds(PAD, rows)

    def activated(p):
        ext[0:PAD, :] = halo[0, :, col(p)].astype(F32)[MARK - PAD :]
        ext[ext_rows, :] = proj[:, col(p)].astype(F32)
        z = cb[:, col(p)] + cw[0:1, col(p)] * ext[pl.ds(PAD - 3, rows), :]
        for k in range(1, KCONV):
            z = z + cw[k : k + 1, col(p)] * ext[pl.ds(PAD - 3 + k, rows), :]
        return z * sigmoid(z)

    b_rows = jnp.concatenate(split(activated(pairs)), axis=1)
    bc_out[:, : 2 * STATE] = b_rows
    bc_out[:, 2 * STATE :] = jnp.concatenate(split(activated(pairs + 1)), axis=1)
    for p in range(pairs):
        x = activated(p)
        x_out[:, col(p)] = x
        scaled = (x * nn(weight, spread[:, col(p)])).astype(BF16)
        part = tn_sum(b_rows, scaled)
        fade = nn(ending, spread[:, col(p)])[0:1, :]
        st_out[0, :, col(p)] = part
        fade_out[0, :, col(p)] = fade
        message_of(msg_out, p, part, fade)


def inside_kernel(x, bc, sl, spread, y_out):
    rows = x.shape[0]
    half = rows // 2
    pairs = x.shape[1] // LANES
    scores = nt_fine(bc[:, 2 * STATE :], bc[:, : 2 * STATE])
    log_decay = sl[:, LANES:]
    across = log_decay.T
    step = two_parts(sl[:, :LANES])
    t = lax.broadcasted_iota(jnp.int32, (half, half), 0)
    s = lax.broadcasted_iota(jnp.int32, (half, half), 1)
    causal = t >= s
    low_lanes = lax.broadcasted_iota(jnp.int32, (rows, LANES), 1) < HEAD_DIM

    def weights(h, later, earlier, masked):
        gap = log_decay[later, h : h + 1] - across[h : h + 1, earlier]
        gap = jnp.where(causal, gap, NEVER) if masked else gap
        return (scores[later, earlier] * jnp.exp(gap)).astype(BF16)

    first, second = slice(0, half), slice(half, rows)
    for p in range(pairs):
        scaled = (x[:, col(p)] * nn(step, spread[:, col(p)])).astype(BF16)
        outs = []
        for h in (2 * p, 2 * p + 1):
            above = nn(weights(h, first, first, True), scaled[:half])
            below = jnp.concatenate([weights(h, second, first, False), weights(h, second, second, True)], axis=1)
            outs.append(jnp.concatenate([above, nn(below, scaled)], axis=0))
        y_out[:, col(p)] = jnp.where(low_lanes, outs[0], outs[1])


def gate_kernel(y, x, bc, sl, start, gate, grad, gain, skip, spread, y_out, sums_out):
    rows = x.shape[0]
    pairs = x.shape[1] // LANES
    c_rows = bc[:, 2 * STATE :]
    decay = two_parts(jnp.exp(sl[:, LANES:]))
    squares = jnp.zeros((rows, LANES), F32)
    cross = jnp.zeros((rows, LANES), F32)
    for p in range(pairs):
        plain = y[:, col(p)] + nn(decay, spread[:, col(p)]) * nn(c_rows, twice(start[0, :, col(p)]))
        y_out[:, col(p)] = plain
        g = gate[:, col(p)].astype(F32)
        v = (plain + skip[:, col(p)] * x[:, col(p)]) * (g * sigmoid(g))
        squares = squares + v * v
        cross = cross + grad[:, col(p)].astype(F32) * gain[:, col(p)] * v
    lane = lax.broadcasted_iota(jnp.int32, (rows, LANES), 1)
    both = jnp.where(
        lane == 0,
        jnp.sum(squares, axis=1, keepdims=True),
        jnp.where(lane == 1, jnp.sum(cross, axis=1, keepdims=True), 0.0),
    )
    sums_out[0] = both.T[0:PAD, :]


def norm_kernel(
    inner, y, x, bc, sl, gate, grad, gain, skip, fade, sums, spread,
    gated_out, dy_out, dgate_out, dstart_out, msg_out, gain_out, skip_out,
):
    rows = x.shape[0]
    pairs = x.shape[1] // LANES

    @pl.when(pl.program_id(0) == 0)
    def _():
        gain_out[...] = jnp.zeros_like(gain_out)
        skip_out[...] = jnp.zeros_like(skip_out)

    c_rows = bc[:, 2 * STATE :]
    decay = two_parts(jnp.exp(sl[:, LANES:]))
    padded = jnp.concatenate([sums[0], jnp.zeros((LANES - PAD, rows), F32)], axis=0).T
    scale = lax.rsqrt(padded[:, 0:1] / inner + EPSILON)
    back = scale * scale * (padded[:, 1:2] / inner)
    for p in range(pairs):
        g = gate[:, col(p)].astype(F32)
        sg = sigmoid(g)
        silu = g * sg
        xp = x[:, col(p)]
        yp = y[:, col(p)] + skip[:, col(p)] * xp
        v = yp * silu
        gp = grad[:, col(p)].astype(F32)
        normal = v * scale
        gated_out[:, col(p)] = (normal * gain[:, col(p)]).astype(BF16)
        gain_out[0:1, col(p)] += jnp.sum(gp * normal, axis=0, keepdims=True)
        dv = scale * (gp * gain[:, col(p)] - v * back)
        dy = (dv * silu).astype(BF16)
        dy_out[:, col(p)] = dy
        dyf = dy.astype(F32)
        dgate_out[:, col(p)] = (dv * yp * (sg * (1.0 + g * (1.0 - sg)))).astype(BF16)
        skip_out[0:1, col(p)] += jnp.sum(dyf * xp, axis=0, keepdims=True)
        faded = (dyf * nn(decay, spread[:, col(p)])).astype(BF16)
        dstart = tn_sum(c_rows, faded)
        dstart_out[0, :, col(p)] = dstart
        message_of(msg_out, p, dstart, fade[0, :, col(p)])


def inside_back_kernel(x, bc, sl, dy, start, spread, dxs_out, dbc_out):
    rows = x.shape[0]
    half = rows // 2
    pairs = x.shape[1] // LANES
    b_rows = bc[:, : 2 * STATE]
    c_rows = bc[:, 2 * STATE :]
    scores = nt_fine(b_rows, c_rows)
    log_decay = sl[:, LANES:]
    across = log_decay.T
    step = two_parts(sl[:, :LANES])
    decay = two_parts(jnp.exp(log_decay))
    s = lax.broadcasted_iota(jnp.int32, (half, half), 0)
    t = lax.broadcasted_iota(jnp.int32, (half, half), 1)
    causal = t >= s
    low_lanes = lax.broadcasted_iota(jnp.int32, (rows, LANES), 1) < HEAD_DIM

    def falls(h, earlier, later, masked):
        gap = across[h : h + 1, later] - log_decay[earlier, h : h + 1]
        return jnp.exp(jnp.where(causal, gap, NEVER) if masked else gap)

    first, second = slice(0, half), slice(half, rows)
    above_grad = jnp.zeros((half, rows), F32)
    below_grad = jnp.zeros((half, half), F32)
    dc = jnp.zeros((rows, LANES), F32)
    for p in range(pairs):
        scaled = x[:, col(p)] * nn(step, spread[:, col(p)])
        dyp = dy[:, col(p)]
        faded = (dyp.astype(F32) * nn(decay, spread[:, col(p)])).astype(BF16)
        dc = dc + nt(faded, start[0, :, col(p)])
        outs = []
        for h in (2 * p, 2 * p + 1):
            above = jnp.concatenate([falls(h, first, first, True), falls(h, first, second, False)], axis=1)
            below = falls(h, second, second, True)
            outs.append(
                jnp.concatenate(
                    [
                        nn((scores[:half] * above).astype(BF16), dyp),
                        nn((scores[half:, half:] * below).astype(BF16), dyp[half:]),
                    ],
                    axis=0,
                )
            )
            mine = low_lanes if h % 2 == 0 else jnp.logical_not(low_lanes)
            own = jnp.where(mine, scaled, 0.0).astype(BF16)
            above_grad = above_grad + above * nt(own[:half], dyp)
            below_grad = below_grad + below * nt(own[half:], dyp[half:])
        dxs_out[:, col(p)] = jnp.where(low_lanes, outs[0], outs[1])
    below_grad = jnp.concatenate([jnp.zeros((half, half), F32), below_grad], axis=1)
    score_grad = jnp.concatenate([above_grad, below_grad], axis=0)
    dbc_out[:, col(0)] = nn_fine(*split(score_grad), c_rows)
    dbc_out[:, col(1)] = dc + nn_fine(*split(score_grad.T), b_rows)


def back_kernel(
    proj, halo, cw, cb, sb, dl, skip, spread, fold, x, bc, sl, y, dy, dxs, dbc, start, part, fade, later,
    pg_out, halo_out, tail_out, cw_out, cb_out, sb_out, dl_out, ext, dext,
):
    rows = x.shape[0]
    pairs = x.shape[1] // LANES

    @pl.when(pl.program_id(0) == 0)
    def _():
        for out in (cw_out, cb_out, sb_out, dl_out):
            out[...] = jnp.zeros_like(out)

    rate = jnp.exp(dl[...])
    step_f = sl[:, :LANES]
    log_decay = sl[:, LANES:]
    last = log_decay[rows - 1 : rows, :]
    step = two_parts(step_f)
    to_end = two_parts(jnp.exp(last - log_decay))
    b_rows = bc[:, : 2 * STATE]
    dext[0:PAD, :] = jnp.zeros((PAD, LANES), F32)
    dext[pl.ds(PAD + rows, PAD), :] = jnp.zeros((PAD, LANES), F32)

    def through_conv(p, grad):
        ext[0:PAD, :] = halo[0, :, col(p)].astype(F32)[MARK - PAD :]
        ext[pl.ds(PAD, rows), :] = proj[:, col(p)].astype(F32)
        taps = [ext[pl.ds(PAD - 3 + k, rows), :] for k in range(KCONV)]
        z = cb[:, col(p)] + cw[0:1, col(p)] * taps[0]
        for k in range(1, KCONV):
            z = z + cw[k : k + 1, col(p)] * taps[k]
        sg = sigmoid(z)
        dz = grad * (sg * (1.0 + z * (1.0 - sg)))
        cb_out[0:1, col(p)] += jnp.sum(dz, axis=0, keepdims=True)
        for k in range(KCONV):
            cw_out[k : k + 1, col(p)] += jnp.sum(dz * taps[k], axis=0, keepdims=True)
        dext[pl.ds(PAD, rows), :] = dz
        whole = rows + PAD
        dm = cw[KCONV - 1 : KCONV, col(p)] * dext[pl.ds(0, whole), :]
        for k in range(KCONV - 1):
            dm = dm + cw[k : k + 1, col(p)] * dext[pl.ds(KCONV - 1 - k, whole), :]
        halo_out[0, :, col(p)] = dm[0:PAD, :]
        pg_out[:, col(p)] = dm[PAD:, :].astype(BF16)
        tail_out[0, :, col(p)] = dm[rows:, :]

    db = dbc[:, col(0)]
    dstep = jnp.zeros((rows, LANES), F32)
    dlog = jnp.zeros((rows, LANES), F32)
    dlast = jnp.zeros((PAD, LANES), F32)
    for p in range(pairs):
        xp = x[:, col(p)]
        step_p = nn(step, spread[:, col(p)])
        end_p = nn(to_end, spread[:, col(p)])
        later_p = later[0, :, col(p)]
        dyf = dy[:, col(p)].astype(F32)
        scaled = xp * step_p
        dxs_p = dxs[:, col(p)] + end_p * nn(b_rows, twice(later_p))
        db = db + nt((end_p * scaled).astype(BF16), later_p)
        dstep = dstep + head_sums(xp * dxs_p, fold[col(p), :])
        dlog = dlog + head_sums(dyf * y[:, col(p)] - scaled * dxs_p, fold[col(p), :])
        end_state = fade[0, :, col(p)] * start[0, :, col(p)].astype(F32) + part[0, :, col(p)]
        ends = jnp.sum(later_p.astype(F32) * end_state, axis=0, keepdims=True)
        dlast = dlast + head_sums(jnp.broadcast_to(ends, (PAD, LANES)), fold[col(p), :])
        through_conv(p, step_p * dxs_p + skip[:, col(p)] * dyf)
    through_conv(pairs, db)
    through_conv(pairs + 1, dbc[:, col(1)])
    place = lax.broadcasted_iota(jnp.int32, (rows, LANES), 0)
    dlog = dlog + jnp.where(place == rows - 1, dlast[0:1, :], 0.0)
    da = running(dlog, True)
    dstep = dstep - rate * da
    raw_step = proj[:, (pairs + 2) * LANES :].astype(F32) + sb[...]
    draw = dstep * sigmoid(raw_step)
    pg_out[:, (pairs + 2) * LANES :] = draw.astype(BF16)
    sb_out[0:1, :] += jnp.sum(draw, axis=0, keepdims=True)
    dl_out[0:1, :] += -rate * jnp.sum(step_f * da, axis=0, keepdims=True)


def share_kernel(heads, a_group, place, b0, b1, b2, b3, out):
    last = pl.program_id(0) == pl.num_programs(0) - 1
    for k, block in enumerate((b0, b1, b2, b3)):

        @pl.when(jnp.logical_not(last) | (k < 2))
        def _():
            out[:, col(k)] = block[...].astype(F32).T.astype(BF16)

    @pl.when(last)
    def _():
        rows = lax.broadcasted_iota(jnp.int32, b2.shape, 0)
        inside = jnp.where(rows < HEADS, b2[...].astype(F32), 0.0).astype(BF16)
        local = lax.broadcasted_iota(jnp.int32, (LANES, LANES), 0)
        head = lax.broadcasted_iota(jnp.int32, (LANES, LANES), 1)
        group = lax.div(local, a_group)
        owner = (group * (HEADS // heads) + place[0]) * a_group + (local - group * a_group)
        chosen = jnp.where((owner == head) & (local < heads), 1.0, 0.0).astype(BF16)
        out[:, col(2)] = lax.dot_general(
            inside, chosen, (((0,), (1,)), ((), ())), preferred_element_type=F32
        ).astype(BF16)
        out[:, col(3)] = jnp.zeros((out.shape[0], LANES), BF16)


def rows_kernel(product, left, right, out):
    out[...] = product(left[...], right[...]).astype(BF16)


def gathered_kernel(product, count, *refs):
    blocks, (right, out, left, *last) = refs[:count], refs[count:]
    for j in range(4):

        @pl.when(pl.program_id(0) == j)
        def _():
            first = 0
            for block in blocks[j : j + 1] if j < 3 else blocks[3:]:
                value = block[...].reshape(block.shape[-2:])
                left[first : first + value.shape[0], :] = value
                first += value.shape[0]

    out[...] = product(left[...], right[...]).astype(BF16)
    for tail in last:
        tail[0] = out[out.shape[0] - tail.shape[1] :, : tail.shape[2]]


def weight_kernel(*refs):
    count = len(refs) // 2
    total = tn(refs[0][...], refs[count][...])
    for m in range(1, count):
        total = total + tn(refs[m][...], refs[count + m][...])
    refs[-1][...] = total.astype(BF16)


def both_weights_kernel(count, *refs):
    normed, gates, gated, cots = (refs[i * count : (i + 1) * count] for i in range(4))
    out = refs[-1]
    gate = sum(tn(a[...], b[...]) for a, b in zip(normed, gates))
    back = sum(tn(a[...], b[...]) for a, b in zip(gated, cots))
    rows, width = gate.shape
    half = back.shape[0]
    out[0, :rows] = gate.astype(BF16)
    for part in range(back.shape[1] // width):
        out[0, rows + part * half : rows + (part + 1) * half] = back[:, part * width : (part + 1) * width].astype(BF16)


def branch_kernel(count, *refs):
    lefts, right, outs = refs[:count], refs[count], refs[count + 1 :]
    values = [nn(left[...], right[...]).astype(BF16) for left in lefts]
    for q, out in enumerate(outs):

        @pl.when(pl.program_id(0) == q)
        def _():
            for m, value in enumerate(values):
                out[m] = value


def grad_kernel(mix, gate, w_mix, w_gate, normed, o0, o1, o2, o3, pre):
    @pl.when(pl.program_id(0) == 0)
    def _():
        pre[...] = jnp.zeros_like(pre)

    grad = nt(mix[...], w_mix[...]) + nt(gate[...], w_gate[...])
    pre[0:1, :] += jnp.sum(grad * normed[...].astype(F32), axis=0, keepdims=True)
    grad = grad.astype(BF16)
    for q, out in enumerate((o0, o1, o2, o3)):

        @pl.when(pl.program_id(0) == q)
        def _():
            out[...] = grad


def ordered(place, blocks):
    odd = (place & 1) == 1
    high = (place & 2) == 2
    a, b, c, d = blocks
    a, b = jnp.where(odd, b, a), jnp.where(odd, a, b)
    c, d = jnp.where(odd, d, c), jnp.where(odd, c, d)
    return [jnp.where(high, c, a), jnp.where(high, d, b), jnp.where(high, a, c), jnp.where(high, b, d)]


def turned(place, blocks, out):
    unit = blocks[0].shape[1]
    for q, block in enumerate(ordered(place[0], [b.astype(F32) for b in blocks])):
        out[q * unit : (q + 1) * unit, :] = block.T


def gate_grad_kernel(place, g0, g1, g2, g3, out):
    turned(place, [g[...] for g in (g0, g1, g2, g3)], out)


def mix_grad_kernel(groups, heads, before, place, m0, m1, m2, low, high, where_heads, out):
    step = pl.program_id(0)
    width = heads * HEAD_DIM
    unit = width // groups

    def columns(at, count):
        whole_blocks = [m[:, pl.ds(at, count)] for m in (m0, m1, m2)]
        return whole_blocks + [jnp.concatenate([low[:, pl.ds(at, count)], high[:, pl.ds(at, count)]], axis=0)]

    @pl.when(step < groups)
    def _():
        turned(place, columns(pl.multiple_of(step * unit, LANES), unit), out)

    @pl.when(step == groups)
    def _():
        both = ordered(place[0], [b.astype(F32) for b in columns(width, 2 * STATE)])
        out[: 2 * STATE, :] = ((both[0] + both[1]) + (both[2] + both[3])).T
        steps = ordered(place[0], columns(width + 2 * STATE, LANES))
        placed = nn(steps[0], where_heads[0])
        for q in range(1, 4):
            placed = placed + nn(steps[q], where_heads[q])
        out[2 * STATE : 2 * STATE + 4 * heads, :] = placed.T[: 4 * heads, :]


def small_kernel(groups, heads, blocks, place, gain, where_heads, *refs):
    ins, (cw_out, cb_out, norm_out, head_out, pre_out) = refs[:4], refs[4:]
    parts = ordered(place[0], [b[...] for b in ins])
    total = (parts[0] + parts[1]) + (parts[2] + parts[3])
    width = groups * blocks

    def spread(out, row, first):
        for g in range(groups):
            for q in range(4):
                for k in range(blocks):
                    at = ((g * 4 + q) * blocks + k) * LANES
                    out[row : row + 1, at : at + LANES] = parts[q][first + g * blocks + k :][:1, :]

    first = 0
    for k in range(KCONV + 1):
        out, row = (cw_out, k) if k < KCONV else (cb_out, 0)
        spread(out, row, first)
        for c in (0, 1):
            at = (4 * width + c) * LANES
            out[row : row + 1, at : at + LANES] = total[first + width + c :][:1, :]
        first += width + 2
    spread(norm_out, 0, first)
    first += width
    placed = 0.0
    for q in range(4):
        rows = jnp.concatenate([parts[q][first : first + 3, :], jnp.zeros((PAD - 3, LANES), F32)], axis=0)
        placed = placed + jnp.dot(
            rows, where_heads[q].astype(F32), preferred_element_type=F32, precision=lax.Precision.HIGHEST
        )
    head_out[...] = placed
    first += 3
    for k in range(pre_out.shape[1] // LANES):
        pre_out[:, col(k)] = total[first + k :][:1, :] / gain[:, col(k)]


def out_grad_kernel(rows, place, b0, b1, b2, b3, out):
    from_rep = place[0] ^ pl.program_id(0)
    count = out.shape[0]
    for j, (block, skip) in enumerate(((b0, rows), (b1, rows), (b2, rows), (b3, 0))):

        @pl.when(from_rep == j)
        def _():
            width = block.shape[1]
            for part in range(out.shape[1] // width):
                first = skip + part * count
                out[:, part * width : (part + 1) * width] = block[first : first + count, :].astype(F32)


def each(*shape):
    return pl.BlockSpec((1,) + shape, lambda i: (i, 0, 0))


def whole(*shape):
    return pl.BlockSpec(shape, lambda i: (0,) * len(shape))


def call(kernel, slots, ins, outs, scratch, us, held=None, alias=None):
    arrays = [a for a, _ in ins]
    if held is not None:
        arrays[0] = held(arrays[0])
    out_shape = [o for o, _ in outs]
    return pl.pallas_call(
        kernel,
        grid=(slots,),
        in_specs=[s for _, s in ins],
        out_specs=[s for _, s in outs],
        out_shape=out_shape,
        scratch_shapes=scratch,
        input_output_aliases=alias or {},
        compiler_params=pltpu.CompilerParams(
            dimension_semantics=("arbitrary",), vmem_limit_bytes=52 * 1024 * 1024
        ),
        cost_estimate=pl.CostEstimate(
            flops=int(us * slots * 1.1e9 * COST), bytes_accessed=int(us * slots * 1e6 * COST), transcendentals=0
        ),
    )(*arrays)


def sds(shape, dtype):
    return jax.ShapeDtypeStruct(shape, dtype)


def rows_times(left, right, product, block, held):
    rows, depth = left.shape
    width = right.shape[1] if product is nn else right.shape[0]
    (out,) = call(
        functools.partial(rows_kernel, product),
        rows // block,
        [(left, pl.BlockSpec((block, depth), lambda i: (i, 0))), (right, whole(*right.shape))],
        [(sds((rows, width), BF16), pl.BlockSpec((block, width), lambda i: (i, 0)))],
        [],
        2.0,
        held,
    )
    return out


def gathered_times(parts, right, product, held, batch=None, last=()):
    rows, depth = parts[0].shape[-2:]
    if batch is None:
        ins = [(v, whole(*v.shape)) for v in parts]
    else:
        ins = [(v, pl.BlockSpec((1, rows, depth), lambda i: (batch, 0, 0))) for v in parts]
    width = right.shape[1] if product is nn else right.shape[0]
    block = lambda w: (sds((4 * rows, w), BF16), pl.BlockSpec((rows, w), lambda i: (i, 0)))
    return call(
        functools.partial(gathered_kernel, product, len(parts)),
        4,
        ins + [(right, whole(*right.shape))],
        [block(width), block(depth)] + [(sds((4, MARK, w), BF16), each(MARK, w)) for w in last],
        [],
        2.7,
        held,
    )


def weight_sum(lefts, rights, held, us=2.0):
    rows, width = lefts[0].shape
    depth = rights[0].shape[1]
    block = min(256, width)
    (out,) = call(
        weight_kernel,
        width // block,
        [(v, pl.BlockSpec((rows, block), lambda i: (0, i))) for v in lefts] + [(v, whole(*v.shape)) for v in rights],
        [(sds((width, depth), BF16), pl.BlockSpec((block, depth), lambda i: (i, 0)))],
        [],
        us,
        held,
    )
    return out


def per_device(
    tokens, lengths, pre_gain, in_weight, conv_weight, conv_bias, step_bias, decay_log, skip_gain,
    norm_gain, out_weight, cotangent,
):
    micro, length, model = tokens.shape
    reps = lax.axis_size("rep")
    pieces = lax.axis_size("seq")
    rep = lax.axis_index("rep")
    inner = norm_gain.shape[0]
    heads = HEADS // reps
    width = heads * HEAD_DIM
    rows = reps * length
    xbc = width + 2 * STATE
    cols = xbc + LANES
    groups = pieces if HEADS % (pieces * reps) == 0 else 1
    strided = groups == pieces

    def pick(v, unit):
        each_group = heads // groups * unit
        v = v.reshape(v.shape[:-1] + (groups, reps, each_group))
        v = lax.dynamic_index_in_dim(v, rep, v.ndim - 2, False)
        return v.reshape(v.shape[:-2] + (groups * each_group,))

    def unpick(parts, unit):
        each_group = heads // groups * unit
        lead = parts[0].shape[:-1]
        v = jnp.stack([q.reshape(lead + (groups, each_group)) for q in parts], axis=-2)
        return v.reshape(lead + (HEADS * unit,))

    def lanes_of(v):
        return jnp.pad(v, [(0, 0)] * (v.ndim - 1) + [(0, LANES - v.shape[-1])])

    def conv_share(v):
        return jnp.concatenate([pick(v[..., :inner], HEAD_DIM), v[..., inner:]], axis=-1)

    position = lax.axis_index("seq") * length + jnp.arange(length, dtype=jnp.int32)
    valid = (position[None, :] < lengths[:, None])[..., None]
    token_rows = tokens.astype(F32)
    inverse = lax.rsqrt(jnp.mean(token_rows * token_rows, axis=-1, keepdims=True) + EPSILON)
    normed = (token_rows * inverse * pre_gain).astype(BF16)
    masked = jnp.where(valid, cotangent, jnp.zeros_like(cotangent))

    rep_scalar = rep.astype(jnp.int32).reshape(1)
    if strided and width == groups * LANES and groups % 4 == 0:
        x_first = inner // LANES
        x_blocks = x_first + groups * reps

        def share_of(k):
            def index(i, r):
                at = 4 * i + k
                return (jnp.where(at < groups, x_first + at * reps + r[0], jnp.minimum(x_blocks + at - groups, x_blocks + 2)), 0)

            return pl.BlockSpec((LANES, in_weight.shape[0]), index)

        w_mix = pl.pallas_call(
            functools.partial(share_kernel, heads, heads // groups),
            grid_spec=pltpu.PrefetchScalarGridSpec(
                num_scalar_prefetch=1,
                grid=(groups // 4 + 1,),
                in_specs=[share_of(k) for k in range(4)],
                out_specs=pl.BlockSpec((in_weight.shape[0], 4 * LANES), lambda i, r: (0, i)),
            ),
            out_shape=sds((in_weight.shape[0], cols), BF16),
            compiler_params=pltpu.CompilerParams(dimension_semantics=("arbitrary",)),
            cost_estimate=pl.CostEstimate(flops=int(4e9), bytes_accessed=int(4e6), transcendentals=0),
        )(rep_scalar, *[in_weight.T] * 4)
    else:
        w_mix = jnp.concatenate(
            [
                pick(in_weight[:, inner : 2 * inner], HEAD_DIM),
                in_weight[:, 2 * inner : 2 * inner + 2 * STATE],
                lanes_of(pick(in_weight[:, 2 * inner + 2 * STATE :], 1)),
            ],
            axis=1,
        )
    w_gate = pick(in_weight[:, :inner], HEAD_DIM)
    w_mix = lax.all_gather(w_mix, "seq", axis=0, tiled=True)
    w_gate = lax.all_gather(w_gate, "seq", axis=0, tiled=True)
    if strided:
        share = out_weight.shape[0] // reps
        w_out = lax.dynamic_slice_in_dim(out_weight, rep * share, share, 0)
        w_out = lax.all_gather(w_out, "seq", axis=0, tiled=True)
    else:
        w_out = lax.all_gather(out_weight, "seq", axis=0, tiled=True)
        w_out = lax.dynamic_slice_in_dim(w_out, rep * width, width, 0)

    spread_row = jnp.arange(LANES, dtype=jnp.int32)[:, None]
    spread = (
        (spread_row < LANES // 2)
        & (spread_row % (LANES // 4) == jnp.arange(width, dtype=jnp.int32)[None, :] // HEAD_DIM)
    ).astype(BF16)
    fold = (
        jnp.arange(width, dtype=jnp.int32)[:, None] // HEAD_DIM
        == jnp.arange(LANES, dtype=jnp.int32)[None, :]
    ).astype(BF16)

    cw = conv_share(conv_weight)
    cb = conv_share(conv_bias)[None, :]
    sb = lanes_of(pick(step_bias, 1))[None, :]
    dl = lanes_of(pick(decay_log, 1))[None, :]
    skip = jnp.repeat(pick(skip_gain, 1), HEAD_DIM)[None, :]
    gain = pick(norm_gain, HEAD_DIM)[None, :]

    line = []

    def held(*others):
        return lambda value: after(value, *line, *others)

    def later(values):
        return list(after(tuple(values), *line))

    def ran(out):
        line[:] = [out]
        return out

    row_spec = lambda w: pl.BlockSpec((length, w), lambda i: (i, 0))
    small = [
        (cw, whole(KCONV, xbc)),
        (cb, whole(1, xbc)),
        (sb, whole(1, LANES)),
        (dl, whole(1, LANES)),
    ]
    spread_in = (spread, whole(LANES, width))
    gain_in = (gain, whole(1, width))
    skip_in = (skip, whole(1, width))
    wide = lambda v: (v, row_spec(width))
    state = lambda v: (v, each(STATE, width))
    out_wide = lambda t: (sds((rows, width), t), row_spec(width))
    out_state = (sds((reps, STATE, width), F32), each(STATE, width))
    out_message = (sds((reps, STATE + MARK, width), BF16), each(STATE + MARK, width))
    out_gain = (sds((PAD, width), F32), whole(PAD, width))
    ext = pltpu.VMEM((length + PAD, LANES), F32)

    proj_in, halo_in, x_in, bc_in, sl_in, part_in, fade_in, start_in = ([None] * micro for _ in range(8))
    gate_in, grad_in, y_in, sums, inside = ([None] * micro for _ in range(5))
    forward_chain = [None] * micro

    def project(m, *others):
        proj, normed_all[m], tail = gathered_times(normed_parts[m], w_mix, nn, held(*others), last=(xbc,))
        ran(proj)
        halo = lax.ppermute(tail, "seq", [(i, i + 1) for i in range(pieces - 1)])
        proj_in[m], halo_in[m] = (proj, row_spec(cols)), (halo, each(MARK, xbc))

    def front(m, *others):
        x, bc, sl, part, message, fade = call(
            front_kernel,
            reps,
            [proj_in[m], halo_in[m]] + small + [spread_in],
            [
                out_wide(F32),
                (sds((rows, 4 * STATE), BF16), row_spec(4 * STATE)),
                (sds((rows, 2 * LANES), F32), row_spec(2 * LANES)),
                out_state,
                out_message,
                (sds((reps, 1, width), F32), each(1, width)),
            ],
            [ext],
            2.3,
            held(*others),
        )
        ran(fade)
        x_in[m], bc_in[m], sl_in[m] = wide(x), (bc, row_spec(4 * STATE)), (sl, row_spec(2 * LANES))
        part_in[m], fade_in[m] = state(part), (fade, each(1, width))
        forward_chain[m] = Chain(fade, part, message, False)

    def within(m, *others):
        (inside[m],) = call(
            inside_kernel, reps, [x_in[m], bc_in[m], sl_in[m], spread_in], [out_wide(F32)], [], 2.2, held(*others)
        )
        ran(inside[m])

    def gate_of(m, *others):
        gate_in[m] = wide(ran(rows_times(normed_all[m], w_gate, nn, length, held(*others))))

    def grad_of(m, *others):
        grad, cot_all[m] = gathered_times(cot_blocks, w_out, nt, held(*others), m)
        grad_in[m] = wide(ran(grad))

    def gating(m, *others):
        start_in[m] = state(forward_chain[m].end())
        y, partial = call(
            gate_kernel,
            reps,
            [wide(inside[m]), x_in[m], bc_in[m], sl_in[m], start_in[m], gate_in[m], grad_in[m], gain_in, skip_in, spread_in],
            [out_wide(F32), (sds((reps, PAD, length), F32), each(PAD, length))],
            [],
            2.8,
            held(*others),
        )
        ran(partial)
        y_in[m] = wide(y)
        partial = sum_aligned(partial[:, :2])
        sums[m] = (jnp.pad(partial, ((0, 0), (0, PAD - 2), (0, 0))), each(PAD, length))

    near = [gather_near(normed[0])]
    far = [to_far(near[0])]
    normed_all, cot_all = [None] * micro, [None] * micro
    normed_parts = [far_parts(near[0], far[0])]
    near.append(gather_near(after(normed[1], *normed_parts[0][3:])))
    project(0, near[1][0])
    near[1] = later(near[1])
    far.append(to_far(near[1]))
    normed_parts.append(far_parts(near[1], far[1]))
    front(0, *far[1])
    cot_blocks = gather_direct(after(masked, *line))
    project(1, cot_blocks[0])
    front(1, forward_chain[0].hop())
    gate_of(0)
    within(0, forward_chain[0].hop(), forward_chain[1].hop())
    gate_of(1)
    within(1, forward_chain[0].hop(), forward_chain[1].hop())
    cot_blocks = later(cot_blocks)
    grad_of(0)
    forward_chain[0].rest()
    grad_of(1, forward_chain[0].back(), forward_chain[1].hop())
    forward_chain[1].rest()
    gating(0, forward_chain[1].back())
    gating(1)

    gated, dy_in, dgate, later_in, gains, skips = ([None] * micro for _ in range(6))
    backward_chain = [None] * micro

    def normalise(m, *others):
        gated[m], dy, dgate[m], dstart, message, gains[m], skips[m] = call(
            functools.partial(norm_kernel, float(inner)),
            reps,
            [y_in[m], x_in[m], bc_in[m], sl_in[m], gate_in[m], grad_in[m], gain_in, skip_in, fade_in[m], sums[m], spread_in],
            [out_wide(BF16), out_wide(BF16), out_wide(BF16), out_state, out_message, out_gain, out_gain],
            [],
            3.1,
            held(*others),
        )
        ran(gains[m])
        dy_in[m] = wide(dy)
        backward_chain[m] = Chain(fade_in[m][0], dstart, message, True)

    inner_back = [None] * micro

    def within_back(m, *others):
        inner_back[m] = call(
            inside_back_kernel,
            reps,
            [x_in[m], bc_in[m], sl_in[m], dy_in[m], start_in[m], spread_in],
            [out_wide(F32), (sds((rows, 2 * STATE), F32), row_spec(2 * STATE))],
            [],
            3.6 * LOW,
            held(*others),
        )
        ran(inner_back[m][1])

    pgs, smalls = [None] * micro, [None] * micro

    def back(m, *others):
        dxs, dbc = inner_back[m]
        later_in[m] = state(backward_chain[m].end())
        pg, halo_grad, tail_grad, *smalls[m] = call(
            back_kernel,
            reps,
            [proj_in[m], halo_in[m]] + small
            + [skip_in, spread_in, (fold, whole(width, LANES)), x_in[m], bc_in[m], sl_in[m], y_in[m], dy_in[m]]
            + [wide(dxs), (dbc, row_spec(2 * STATE)), start_in[m], part_in[m], fade_in[m], later_in[m]],
            [
                (sds((rows, cols), BF16), row_spec(cols)),
                (sds((reps, PAD, xbc), F32), each(PAD, xbc)),
                (sds((reps, PAD, xbc), F32), each(PAD, xbc)),
                (sds((PAD, xbc), F32), whole(PAD, xbc)),
                (sds((PAD, xbc), F32), whole(PAD, xbc)),
                (sds((PAD, LANES), F32), whole(PAD, LANES)),
                (sds((PAD, LANES), F32), whole(PAD, LANES)),
            ],
            [ext, pltpu.VMEM((length + 2 * PAD, LANES), F32)],
            5.1 * LOW,
            held(*others),
        )
        ran(smalls[m][0])
        from_next = lax.ppermute(
            halo_grad[:, PAD - (KCONV - 1) :].astype(BF16), "seq", [(i, i - 1) for i in range(1, pieces)]
        )
        pgs[m] = pg, tail_grad[:, PAD - (KCONV - 1) :], from_next

    def complete(m):
        pg, last_rows, from_next = pgs[m]
        last_rows = last_rows + later([from_next])[0].astype(F32)
        pgs[m] = lax.dynamic_update_slice(
            pg.reshape(reps, length, cols), last_rows.astype(BF16), (0, length - (KCONV - 1), 0)
        ).reshape(rows, cols)

    normed_grad, pre_parts = [None] * micro, [None] * micro

    def grad_through(m, *others):
        *blocks, pre = call(
            grad_kernel,
            reps,
            [(pgs[m], row_spec(cols)), wide(dgate[m]), (w_mix, whole(*w_mix.shape)), (w_gate, whole(*w_gate.shape))]
            + [(normed_all[m], row_spec(model))],
            [(sds((length, model), BF16), whole(length, model))] * reps + [(sds((PAD, model), F32), whole(PAD, model))],
            [],
            80.0 if m == 0 else 0.1,
            held(*others),
        )
        pre_parts[m] = ran(pre)[0]
        if m == 0:
            normed_grad[m] = list(blocks[:1]) + [swap(blocks[q], "rep", q) for q in (1, 2, 3)]
        else:
            normed_grad[m] = list(blocks[:3]) + list(scatter_far(after(blocks[3], *gate_near[1:])))

    def over_seq(parts):
        return lax.psum_scatter(parts, "seq", scatter_dimension=0, tiled=True)

    normalise(0)
    normalise(1)
    branch = call(
        functools.partial(branch_kernel, micro),
        reps,
        [wide(v) for v in gated] + [(w_out, whole(*w_out.shape))],
        [(sds((micro, length, model), BF16), whole(micro, length, model))] * reps,
        [],
        3.8,
        held(backward_chain[0].hop()),
    )
    ran(branch[0])
    branch = [branch[0]] + [swap(branch[q], "rep", q) for q in (1, 2, 3)]
    within_back(0, backward_chain[0].hop(), backward_chain[1].hop())
    onward = backward_chain[0].hop(), backward_chain[1].hop()
    backward_chain[0].rest()
    if strided:
        k_rows, out_share = model // pieces, width // pieces
        both_rows = k_rows + out_share * model // width
        columns = lambda w: pl.BlockSpec((rows, w), lambda i: (0, i))
        (both_part,) = call(
            functools.partial(both_weights_kernel, micro),
            pieces,
            [(v, columns(k_rows)) for v in normed_all]
            + [(v, whole(*v.shape)) for v in dgate]
            + [(v, columns(out_share)) for v in gated]
            + [(v, whole(*v.shape)) for v in cot_all],
            [(sds((pieces, both_rows, width), BF16), each(both_rows, width))],
            [],
            3.2,
            held(*onward),
        )
        ran(both_part)
        gate_sums = out_sums = over_seq(both_part)[0]
    else:
        gate_sums = over_seq(ran(weight_sum(normed_all, dgate, held(*onward))))
        out_part = ran(weight_sum(gated, cot_all, held()))
        out_sums = over_seq(
            lax.dynamic_update_slice(jnp.zeros((inner, model), BF16), out_part, (rep * width, 0))
        )
    back(0, backward_chain[0].back())
    within_back(1, backward_chain[1].hop())
    backward_chain[1].rest()
    complete(0)
    grad_through(0, backward_chain[1].back())
    back(1, *branch[1:])
    complete(1)
    mix_part = ran(weight_sum(normed_all, pgs, held(), 0.1))
    gate_near = gather_near(after(gate_sums, *normed_grad[0]))
    grad_through(1)
    gain_part, skip_part = sum(g[0] for g in gains), sum(v[0] for v in skips)
    cw_part, cb_part, sb_part, dl_part = (sum(v) for v in zip(*smalls))
    skip_heads = skip_part.reshape(heads, HEAD_DIM).sum(axis=1)
    packed = jnp.concatenate(
        [cw_part[:KCONV].reshape(-1), cb_part[0], gain_part, lanes_of(skip_heads), sb_part[0], dl_part[0]]
    )
    mix_sums = over_seq(after(mix_part, gate_sums, out_sums, *normed_grad[0]))
    output = sum(v.astype(F32) for v in later(branch))
    output = jnp.where(valid, token_rows + output, 0.0).astype(BF16)
    normed_grad[0] = later(normed_grad[0])
    far_sums = after(tuple(normed_grad[1][3:]), *line)
    normed_grad[1], sent = scatter_near(*normed_grad[1][:3], *after(far_sums, output))
    gate_rows = far_parts(gate_near, to_far(gate_near)) if strided else gather_direct(gate_sums)
    out_rows = gate_rows if strided else gather_direct(out_sums)
    pre_part = sum(pre_parts)
    small_sums = jnp.concatenate([packed, pre_part]).reshape(-1, LANES)
    small_sums = SmallSums(after(small_sums, *far_sums))
    small_sums.hop()
    small_sums.value = after(small_sums.value, *sent)
    small_sums = small_sums.rest()

    normed_grad = jnp.stack([sum(v.astype(F32) for v in n) for n in normed_grad])
    xhat = token_rows * inverse
    scaled = normed_grad * pre_gain
    rows_grad = inverse * (scaled - xhat * jnp.mean(scaled * xhat, axis=-1, keepdims=True))
    tokens_grad = jnp.where(valid, cotangent.astype(F32), 0.0) + rows_grad


    ready = tuple(gate_rows) + (small_sums, tokens_grad)
    if strided:
        mix_near = gather_near(after(mix_sums, *ready))
        mix_far = to_far(mix_near)
        mix_rows = far_parts(mix_near, mix_far)
    else:
        mix_rows = gather_direct(mix_sums)
        mix_far = mix_rows[1:]
    gate_rows = list(after(tuple(gate_rows), *mix_far))
    out_rows = gate_rows if strided else out_rows
    small_sums = after(small_sums, *mix_far)
    both_packed = jnp.stack([small_sums, swap(small_sums, "rep", 1)])
    far_packed = swap(both_packed, "rep", 2)
    packed = [both_packed[0], both_packed[1], far_packed[0], far_packed[1]]

    place_in = (rep_scalar, pl.BlockSpec(memory_space=pltpu.SMEM))
    local = jnp.arange(LANES, dtype=jnp.int32)
    a_group = heads // groups
    head_of = (local[None, :] // a_group * reps + jnp.arange(reps, dtype=jnp.int32)[:, None]) * a_group + local % a_group
    head_of = jnp.where(local < heads, head_of, -1)
    where_heads = (head_of[:, :, None] == local[None, None, :]).astype(BF16)
    unit = width // groups
    k_rows = in_weight.shape[0]
    lanes_spec = lambda index: pl.BlockSpec((k_rows, unit), lambda i: (0, index(i)))
    column = lambda first: (
        sds(in_weight.shape[::-1], F32),
        pl.BlockSpec((reps * unit, k_rows), lambda i: (i + first, 0)),
    )
    if strided:
        (out_weight_grad,) = call(
            functools.partial(out_grad_kernel, k_rows),
            reps,
            [place_in] + [(b, whole(*b.shape)) for b in gate_rows[:3] + gate_rows[4:]],
            [(sds(out_weight.shape, F32), pl.BlockSpec((out_share, model), lambda i: (i, 0)))],
            [],
            0.9,
        )
        (gate_done,) = call(
            gate_grad_kernel,
            groups,
            [place_in] + [(b, lanes_spec(lambda i: i)) for b in gate_rows[:4]],
            [column(0)],
            [],
            0.8,
        )
    if strided:
        (in_weight_grad,) = call(
            functools.partial(mix_grad_kernel, groups, heads),
            groups + 1,
            [(gate_done, pl.BlockSpec(memory_space=pl.ANY)), place_in]
            + [(b, whole(*b.shape)) for b in mix_rows]
            + [(where_heads, whole(reps, LANES, LANES))],
            [column(groups)],
            [],
            0.5,
            alias={0: 0},
        )
        in_weight_grad = in_weight_grad.T
    else:
        out_weight_grad = sum(v.astype(F32) for v in in_order(out_rows))
        gates, mixes = in_order(gate_rows), in_order(mix_rows)
        in_weight_grad = jnp.concatenate(
            [
                unpick(gates, HEAD_DIM).astype(F32),
                unpick([v[:, :width] for v in mixes], HEAD_DIM).astype(F32),
                sum(v[:, width:xbc].astype(F32) for v in mixes),
                unpick([v[:, xbc : xbc + heads] for v in mixes], 1).astype(F32),
            ],
            axis=1,
        )
    channels = conv_bias.shape[0]
    conv_weight_grad, conv_bias_grad, norm_gain_grad, by_head, pre_gain_grad = call(
        functools.partial(small_kernel, groups, heads, width // groups // LANES),
        1,
        [place_in, (pre_gain[None, :], whole(1, model)), (where_heads, whole(reps, LANES, LANES))]
        + [(v, whole(*v.shape)) for v in packed],
        [
            (sds((KCONV, channels), F32), whole(KCONV, channels)),
            (sds((1, channels), F32), whole(1, channels)),
            (sds((1, inner), F32), whole(1, inner)),
            (sds((PAD, LANES), F32), whole(PAD, LANES)),
            (sds((1, model), F32), whole(1, model)),
        ],
        [],
        3.0,
    )
    conv_bias_grad, norm_gain_grad, pre_gain_grad = conv_bias_grad[0], norm_gain_grad[0], pre_gain_grad[0]
    skip_gain_grad, step_bias_grad, decay_log_grad = by_head[0, :HEADS], by_head[1, :HEADS], by_head[2, :HEADS]

    return (
        output, tokens_grad, pre_gain_grad, in_weight_grad, conv_weight_grad, conv_bias_grad,
        step_bias_grad, decay_log_grad, skip_gain_grad, norm_gain_grad, out_weight_grad,
    )


def solution(mesh):
    rows = P("rep", "seq", None)
    shard = P("seq", None)
    in_specs = (rows, P("rep"), P(), shard, P(), P(), P(), P(), P(), P(), shard, rows)
    out_specs = (rows, rows, P(), shard, P(), P(), P(), P(), P(), P(), shard)
    return jax.shard_map(per_device, mesh=mesh, in_specs=in_specs, out_specs=out_specs, check_vma=False)
```
